32 devices in a mesh: seq: 8 (over y, x, core), rows: 4 (over z).
Axes of the slice: x: 2, y: 2, z: 4, core: 2. Of those that a mesh axis runs over, the one named last changes fastest.
Arguments:
- queries: bfloat16 [24, 2048, 768], P('rows', 'seq'), may hold values from -6 to 6
- latents: bfloat16 [24, 256, 1280], P('rows', 'seq'), may hold values from -6 to 6
- query_ids: int32 [24, 2048], P('rows', 'seq'), may hold values from 0 to 3, as said below
- latent_ids: int32 [24, 256], P('rows'), may hold values from 0 to 3, as said below
- query_weight: bfloat16 [768, 256], replicated, may hold values from -0.21875 to 0.21875
- key_weight: bfloat16 [1280, 256], replicated, may hold values from -0.15625 to 0.15625
- value_weight: bfloat16 [1280, 768], replicated, may hold values from -0.15625 to 0.15625
- out_weight: bfloat16 [768, 768], replicated, may hold values from -1.75 to 1.75
- up_weight: bfloat16 [768, 768], replicated, may hold values from -0.21875 to 0.21875
- down_weight: bfloat16 [768, 768], replicated, may hold values from -0.21875 to 0.21875
- gain_query: float32 [768], replicated, may hold values from 0.1 to 1.9
- shift_query: float32 [768], replicated, may hold values from -3 to 3
- gain_latent: float32 [1280], replicated, may hold values from 0.1 to 1.9
- shift_latent: float32 [1280], replicated, may hold values from -3 to 3
- gain_hidden: float32 [768], replicated, may hold values from 0.1 to 1.9
- shift_hidden: float32 [768], replicated, may hold values from -3 to 3
- bias_up: float32 [768], replicated, may hold values from -3 to 3
- bias_down: float32 [768], replicated, may hold values from -3 to 3
- cotangent: bfloat16 [24, 2048, 768], P('rows', 'seq'), may hold values from -6 to 6
Outputs:
- block_out: bfloat16 [24, 2048, 768], P('rows', 'seq')
- grad_queries: float32 [24, 2048, 768], P('rows', 'seq')
- grad_latents: float32 [24, 256, 1280], P('rows', 'seq')
- grad_query_weight: float32 [768, 256], P('seq')
- grad_key_weight: float32 [1280, 256], P('seq')
- grad_value_weight: float32 [1280, 768], P('seq')
- grad_out_weight: float32 [768, 768], P('seq')
- grad_up_weight: float32 [768, 768], P('seq')
- grad_down_weight: float32 [768, 768], P('seq')
- grad_gain_query: float32 [768], P('seq')
- grad_shift_query: float32 [768], P('seq')
- grad_gain_latent: float32 [1280], P('seq')
- grad_shift_latent: float32 [1280], P('seq')
- grad_gain_hidden: float32 [768], P('seq')
- grad_shift_hidden: float32 [768], P('seq')
- grad_bias_up: float32 [768], P('seq')
- grad_bias_down: float32 [768], P('seq')
The draws below stay inside these ranges and needn't reach their ends.
Inputs may be any that keep to these rules, and one draw needn't show every extreme that they name: `query_ids`: within each row the ids never fall, start at 0 and take every value up to 3. `latent_ids`: in each row, every aligned block of 32 latents holds every id of 0 to 3 at least once.
All inputs are finite; a program needn't handle non-finite values.
Results may differ from the reference program's by a relative error of at most 0.015.
Values may be sent and summed in bfloat16 or wider, within the bound.
A program may use at most 128 MiB of HBM per device.

```python
import jax
import jax.numpy as jnp
from jax import lax

D = 768
DL = 1280
HEADS = 8
HDIM = 96
QKDIM = 32
FF = 768
NL = 256
NDOC = 4
SEQ_LEN = 2048
ROWS = 24
LAT_DEV = 32


def draw_query_ids(key, part):
    key = jax.random.fold_in(key, 11)
    row_keys = jax.random.split(key, ROWS)
    shuffled = jax.vmap(lambda k: jax.random.permutation(k, SEQ_LEN - 1))(row_keys)
    cuts = jnp.sort(shuffled[:, :NDOC - 1], axis=1) + 1
    position = jnp.arange(SEQ_LEN)
    return jnp.sum(position[None, :, None] >= cuts[:, None, :], axis=2).astype(jnp.int32)


def draw_latent_ids(key, part):
    key = jax.random.fold_in(key, 23)
    fill_key, order_key = jax.random.split(key)
    blocks = NL // LAT_DEV
    position = jnp.arange(LAT_DEV)
    filler = jax.random.randint(fill_key, (ROWS, blocks, LAT_DEV), 0, NDOC)
    base = jnp.where(position[None, None, :] < NDOC, position[None, None, :], filler)
    ranking = jax.random.randint(order_key, (ROWS, blocks, LAT_DEV), 0, 1 << 20) * LAT_DEV + position
    order = jnp.argsort(ranking, axis=2, stable=True)
    return jnp.take_along_axis(base, order, axis=2).reshape(ROWS, NL).astype(jnp.int32)


def block_scale(own_key, shape, pieces, smallest, high):
    loudness, own = 1.0, jax.random.fold_in(own_key, 6)
    for dim, blocks in pieces:
        steps = jnp.exp(jax.random.uniform(jax.random.fold_in(own, dim), (blocks,), jnp.float32, smallest / len(pieces), high / len(pieces)))
        loudness = loudness * jnp.repeat(steps, shape[dim] // blocks).reshape([-1 if axis == dim else 1 for axis in range(len(shape))])
    return loudness


def gaussian(rng, dims, scale, most, pieces=(), kind=jnp.bfloat16):
    level = block_scale(rng, dims, pieces, -0.22, 0.18) if pieces else 1.0
    values = jax.random.normal(rng, dims, jnp.float32) * scale * level
    return jnp.minimum(jnp.maximum(values, -most), most).astype(kind)


def setup_inputs(seed: int = 0) -> dict:
    splits = jax.random.split(jax.random.key(seed), 20)
    queries = gaussian(splits[0], (ROWS, SEQ_LEN, D), 1.0, 6.0, ((0, 4), (1, 8)))
    latents = gaussian(splits[1], (ROWS, NL, DL), 1.0, 6.0, ((0, 4), (1, 8)))
    query_ids = draw_query_ids(jax.random.fold_in(splits[19], 71), 0)
    latent_ids = draw_latent_ids(jax.random.fold_in(splits[19], 71), 0)
    query_weight = gaussian(splits[4], (D, HEADS * QKDIM), D ** -0.5, 0.21875)
    key_weight = gaussian(splits[5], (DL, HEADS * QKDIM), DL ** -0.5, 0.15625)
    value_weight = gaussian(splits[6], (DL, D), DL ** -0.5, 0.15625)
    out_weight = gaussian(splits[7], (D, D), (D * NDOC // NL) ** -0.5, 1.75)
    up_weight = gaussian(splits[8], (D, FF), D ** -0.5, 0.21875)
    down_weight = gaussian(splits[9], (FF, D), FF ** -0.5, 0.21875)
    gain_query = jnp.clip(1.0 + 0.18 * jax.random.normal(splits[10], (D,), jnp.float32), 0.1, 1.9)
    shift_query = gaussian(splits[11], (D,), 0.3, 3.0, (), jnp.float32)
    gain_latent = jnp.clip(1.0 + 0.18 * jax.random.normal(splits[12], (DL,), jnp.float32), 0.1, 1.9)
    shift_latent = gaussian(splits[13], (DL,), 0.3, 3.0, (), jnp.float32)
    gain_hidden = jnp.clip(1.0 + 0.18 * jax.random.normal(splits[14], (D,), jnp.float32), 0.1, 1.9)
    shift_hidden = gaussian(splits[15], (D,), 0.3, 3.0, (), jnp.float32)
    bias_up = gaussian(splits[16], (FF,), 0.3, 3.0, (), jnp.float32)
    bias_down = gaussian(splits[17], (D,), 0.3, 3.0, (), jnp.float32)
    cotangent = gaussian(splits[18], (ROWS, SEQ_LEN, D), 1.0, 6.0, ((0, 4), (1, 8)))
    return dict(queries=queries, latents=latents, query_ids=query_ids, latent_ids=latent_ids, query_weight=query_weight, key_weight=key_weight, value_weight=value_weight, out_weight=out_weight, up_weight=up_weight, down_weight=down_weight, gain_query=gain_query, shift_query=shift_query, gain_latent=gain_latent, shift_latent=shift_latent, gain_hidden=gain_hidden, shift_hidden=shift_hidden, bias_up=bias_up, bias_down=bias_down, cotangent=cotangent)


EPS = 1e-05
HIGH = lax.Precision.HIGHEST

@jax.custom_vjp
def low(v):
    return lax.optimization_barrier(v.astype(jnp.bfloat16)).astype(jnp.float32)

@jax.custom_vjp
def low_back(v):
    return v

def low_keep(v):
    return (low(v), None)

def low_pass(kept, grad):
    return (grad,)

def back_keep(v):
    return (v, None)

def back_low(kept, grad):
    return (low(grad),)
low.defvjp(low_keep, low_pass)
low_back.defvjp(back_keep, back_low)

def layer_norm(field, gain, shift):
    center = field - lax.optimization_barrier(jnp.mean(field, axis=-1, keepdims=True))
    spread = lax.optimization_barrier(jnp.mean(center * center, axis=-1, keepdims=True))
    return center * lax.rsqrt(spread + EPS) * gain + shift

def matmul(left, right):
    return jnp.dot(left, right, precision=HIGH, preferred_element_type=jnp.float32)

def block_row(params, queries, latents, query_ids, latent_ids):
    query_weight, key_weight, value_weight, out_weight, up_weight, down_weight, gain_query, shift_query, gain_latent, shift_latent, gain_hidden, shift_hidden, bias_up, bias_down = params
    scale = QKDIM ** (-0.5)
    query_normed = low(layer_norm(queries, gain_query, shift_query))
    query_proj = low(low_back(matmul(query_normed, query_weight) * scale))
    latent_normed = low(layer_norm(latents, gain_latent, shift_latent))
    keys = low(low_back(matmul(latent_normed, key_weight)))
    values = low(low_back(matmul(latent_normed, value_weight)))
    heads_query = query_proj.reshape(SEQ_LEN, HEADS, QKDIM)
    heads_key = keys.reshape(NL, HEADS, QKDIM)
    heads_value = values.reshape(NL, HEADS, HDIM)
    scores = low_back(jnp.einsum('qhd,khd->hqk', heads_query, heads_key, precision=HIGH))
    allowed = query_ids[:, None] == latent_ids[None, :]
    scores = jnp.where(allowed[None], scores, -1e+30)
    probs = low(jax.nn.softmax(scores, axis=-1))
    mixed = jnp.einsum('hqk,khd->qhd', probs, heads_value, precision=HIGH).reshape(SEQ_LEN, HEADS * HDIM)
    mixed = low(low_back(mixed))
    resid = queries + low_back(matmul(mixed, out_weight))
    hidden_normed = low(layer_norm(resid, gain_hidden, shift_hidden))
    pre = low_back(matmul(hidden_normed, up_weight) + bias_up)
    act = low(jax.nn.gelu(pre, approximate=False))
    return resid + matmul(act, down_weight) + bias_down

def reference(queries, latents, query_ids, latent_ids, query_weight, key_weight, value_weight, out_weight, up_weight, down_weight, gain_query, shift_query, gain_latent, shift_latent, gain_hidden, shift_hidden, bias_up, bias_down, cotangent):
    params = tuple((p.astype(jnp.float32) for p in (query_weight, key_weight, value_weight, out_weight, up_weight, down_weight, gain_query, shift_query, gain_latent, shift_latent, gain_hidden, shift_hidden, bias_up, bias_down)))

    def one_row(totals, row):
        query_row, latent_row, query_row_ids, latent_row_ids, cot_row = row

        def forward(weights, first, second):
            return block_row(weights, first, second, query_row_ids, latent_row_ids)
        result, pull = jax.vjp(forward, params, query_row.astype(jnp.float32), latent_row.astype(jnp.float32))
        grad_params, grad_query_row, grad_latent_row = pull(cot_row.astype(jnp.float32))
        totals = jax.tree.map(lambda acc, term: acc + term, totals, grad_params)
        return (totals, (result.astype(jnp.bfloat16), grad_query_row, grad_latent_row))
    zeros = jax.tree.map(jnp.zeros_like, params)
    totals, (block_out, grad_queries, grad_latents) = lax.scan(one_row, zeros, (queries, latents, query_ids, latent_ids, cotangent))
    return (block_out, grad_queries, grad_latents, totals[0], totals[1], totals[2], totals[3], totals[4], totals[5], totals[6], totals[7], totals[8], totals[9], totals[10], totals[11], totals[12], totals[13])
```

```python
import functools
import types
from typing import Any, NamedTuple

import jax
import jax.numpy as jnp
from jax import lax
from jax.experimental import pallas as pl
from jax.experimental.pallas import tpu as pltpu
from jax.sharding import PartitionSpec as P

HEADS = 8
HDIM = 96
QKDIM = 32
EPS = 1e-05
SCALE = QKDIM ** (-0.5)
MESH = pl.DeviceIdType.MESH
f32, bf16 = jnp.float32, jnp.bfloat16


def dg(a, b, ca, cb):
    return lax.dot_general(a, b, (((ca,), (cb,)), ((), ())), preferred_element_type=f32)


def norm(x):
    mean = jnp.mean(x, -1, keepdims=True)
    cen = x - mean
    inv = lax.rsqrt(jnp.mean(cen * cen, -1, keepdims=True) + EPS)
    return cen * inv, inv


def norm_back(grad, gain, hat, inv):
    g = grad * gain
    return inv * (
        g - jnp.mean(g, -1, keepdims=True) - hat * jnp.mean(g * hat, -1, keepdims=True)
    )


def row_sum(x):
    n, w = x.shape
    return jnp.sum(x.reshape(n // 8, 8, w), axis=0)


def flat(x):
    return x.reshape(-1, x.shape[-1])


def add(a, b):
    return (a.astype(f32) + b.astype(f32)).astype(bf16)


class Place:
    def __init__(self, n_rows):
        self.n = n_rows
        self.s = lax.axis_index("seq")
        self.r = lax.axis_index("rows")
        self.core = lax.rem(self.s, 2)
        self.chip = self.s // 2
        self.xc = self.chip + 1 - 2 * lax.rem(self.chip, 2)
        self.yc = lax.rem(self.chip + 2, 4)
        self.dc = lax.rem(self.xc + 2, 4)
        self.sib = (self.s + 1 - 2 * self.core, self.r)
        self.xn = (2 * self.xc + self.core, self.r)
        self.yn = (2 * self.yc + self.core, self.r)
        half = n_rows // 2
        self.left = self.r < half
        self.mid = (self.r == half - 1) | (self.r == half)
        self.not_end = (self.r != 0) & (self.r != n_rows - 1)
        step = jnp.where(self.left, 1, -1)
        self.inner = (self.s, lax.rem(self.r + step + n_rows, n_rows))
        self.outer = (self.s, lax.rem(self.r - step + n_rows, n_rows))

    def barrier(self):
        bar = pltpu.get_barrier_semaphore()
        up = (self.s, lax.rem(self.r + 1, self.n))
        down = (self.s, lax.rem(self.r + self.n - 1, self.n))
        peers = [self.sib, self.xn, self.yn, up, down]
        for peer in peers:
            pl.semaphore_signal(bar, inc=1, device_id=peer, device_id_type=MESH)
        pl.semaphore_wait(bar, len(peers))


def rcopy(src, dst, ssem, rsem, peer):
    return pltpu.make_async_remote_copy(
        src_ref=src, dst_ref=dst, send_sem=ssem, recv_sem=rsem, device_id=peer, device_id_type=MESH
    )


class Line:
    def __init__(self, pc, src, zo, zi, ssem, rsem, kind):
        zt = zo
        self.pc, self.src, self.zo, self.zi, self.zt, self.kind = pc, src, zo, zi, zt, kind
        self.up_c = rcopy(src, zo, ssem.at[0], rsem.at[0], pc.inner)
        self.cross_c = rcopy(src, zi, ssem.at[1], rsem.at[1], pc.inner)
        self.down_mid = rcopy(zt, zi, ssem.at[2], rsem.at[1], pc.outer)
        self.down_far = rcopy(zi, zi, ssem.at[2], rsem.at[1], pc.outer)

    def plus(self, a, b):
        return (a.astype(f32) + b.astype(f32)).astype(self.kind)

    def up(self):
        pc = self.pc

        @pl.when(pc.not_end)
        def _():
            self.up_c.wait_recv()
            self.src[...] = self.plus(self.src[...], self.zo[...])

        pl.when(pc.mid)(self.cross_c.start)
        pl.when(jnp.logical_not(pc.mid))(self.up_c.start)

    def middle(self):
        pc = self.pc

        @pl.when(pc.mid)
        def _():
            self.cross_c.wait_recv()
            self.zt[...] = self.plus(self.src[...], self.zi[...])

        pl.when(pc.mid & pc.not_end)(self.down_mid.start)

    def down(self):
        pc = self.pc
        pl.when(jnp.logical_not(pc.mid))(self.cross_c.wait_recv)
        pl.when(jnp.logical_not(pc.mid) & pc.not_end)(self.down_far.start)

    def result(self, write):
        pc = self.pc
        pl.when(pc.mid)(lambda: write(self.zt))
        pl.when(jnp.logical_not(pc.mid))(lambda: write(self.zi))

    def drain(self):
        pc = self.pc
        pl.when(pc.mid)(self.cross_c.wait_send)
        pl.when(jnp.logical_not(pc.mid))(self.up_c.wait_send)
        pl.when(pc.mid & pc.not_end)(self.down_mid.wait_send)
        pl.when(jnp.logical_not(pc.mid) & pc.not_end)(self.down_far.wait_send)


class Scatter:
    def __init__(self, pc, part, width, l0, la, lb, la2, lb2, ssem, rsem):
        self.pc, self.part, self.l0 = pc, part, l0
        self.la, self.lb, self.la2, self.lb2 = la, lb, la2, lb2
        h = width // 2
        self.A, self.B = pl.ds(0, h), pl.ds(h, h)
        lead = (slice(None),) * (len(l0.shape) - 2)
        self.lead = lead

        def blk(chip, cols):
            return l0.at[(chip, *lead, cols)]

        self.blk = blk
        other = 1 - pc.core
        self.pair = [
            rcopy(part(2 * q + other), l0.at[q], ssem.at[q], rsem.at[q], pc.sib) for q in range(4)
        ]
        A, B = self.A, self.B
        self.first = [
            rcopy(blk(pc.xc, A), la.at[0], ssem.at[4], rsem.at[4], pc.xn),
            rcopy(blk(pc.dc, A), la.at[1], ssem.at[5], rsem.at[5], pc.xn),
            rcopy(blk(pc.yc, B), lb.at[0], ssem.at[6], rsem.at[6], pc.yn),
            rcopy(blk(pc.dc, B), lb.at[1], ssem.at[7], rsem.at[7], pc.yn),
        ]
        self.second = [
            rcopy(blk(pc.yc, A), la2, ssem.at[8], rsem.at[8], pc.yn),
            rcopy(blk(pc.xc, B), lb2, ssem.at[9], rsem.at[9], pc.xn),
        ]

    def p0(self):
        for c in self.pair:
            c.start()

    def p1(self):
        pc = self.pc
        for q in range(4):
            self.pair[q].wait_recv()
            self.l0[q] = add(self.l0[q], self.part(2 * q + pc.core)[...])
        for c in self.first:
            c.start()

    def p2(self):
        pc = self.pc
        for c in self.first:
            c.wait_recv()

        def into(chip, cols, got):
            v = self.blk(chip, cols)
            v[...] = add(v[...], got[...])

        into(pc.yc, self.A, self.la.at[1])
        into(pc.xc, self.B, self.lb.at[1])
        for c in self.second:
            c.start()
        into(pc.chip, self.A, self.la.at[0])
        into(pc.chip, self.B, self.lb.at[0])

    def p3(self):
        pc = self.pc
        for c, cols, got in zip(self.second, (self.A, self.B), (self.la2, self.lb2)):
            c.wait_recv()
            v = self.blk(pc.chip, cols)
            v[...] = add(v[...], got[...])

    def drain(self):
        for c in self.pair + self.first + self.second:
            c.wait_send()


def scatter_scratch(lead, width):
    half = width // 2
    return dict(
        l0=pltpu.VMEM((4, *lead, width), bf16),
        la=pltpu.VMEM((2, *lead, half), bf16),
        lb=pltpu.VMEM((2, *lead, half), bf16),
        la2=pltpu.VMEM((*lead, half), bf16),
        lb2=pltpu.VMEM((*lead, half), bf16),
        ssem=pltpu.SemaphoreType.DMA((10,)),
        rsem=pltpu.SemaphoreType.DMA((10,)),
    )


def line_scratch(shape, kind):
    return dict(
        zo=pltpu.VMEM(shape, kind),
        zi=pltpu.VMEM(shape, kind),
        ssem=pltpu.SemaphoreType.DMA((3,)),
        rsem=pltpu.SemaphoreType.DMA((2,)),
    )


class Gather:
    def __init__(self, pc, kv, rows, ssem, rsem):
        def blk(t, cols=slice(None)):
            return kv.at[rows, pl.ds(pl.multiple_of(t * 32, 32), 32), cols]

        h = kv.shape[-1] // 2
        A, B = pl.ds(0, h), pl.ds(h, h)
        ds_ = 2 * pc.dc + pc.core

        def copy(k, ref, peer):
            return rcopy(ref, ref, ssem.at[k], rsem.at[k], peer)

        self.own = [copy(0, blk(pc.s), pc.sib), copy(1, blk(pc.s), pc.xn), copy(2, blk(pc.s), pc.yn)]
        self.from_x = [copy(3, blk(pc.xn[0], A), pc.yn), copy(4, blk(pc.xn[0]), pc.sib)]
        self.from_y = [copy(5, blk(pc.yn[0], B), pc.xn), copy(6, blk(pc.yn[0]), pc.sib)]
        self.from_d = [copy(7, blk(ds_, A), pc.sib), copy(8, blk(ds_, B), pc.sib)]

    def p0(self):
        for c in self.own[::-1]:
            c.start()

    def p1(self):
        self.own[1].wait_recv()
        for c in self.from_x:
            c.start()
        self.own[2].wait_recv()
        for c in self.from_y:
            c.start()

    def p2(self):
        self.from_x[0].wait_recv()
        self.from_d[0].start()
        self.from_y[0].wait_recv()
        self.from_d[1].start()

    def p3(self):
        for c in (self.own[0], self.from_x[1], self.from_y[1], *self.from_d):
            c.wait_recv()

    def drain(self):
        for c in self.own + self.from_x + self.from_y + self.from_d:
            c.wait_send()


def kernel(n_rows, names, *refs):
    R = types.SimpleNamespace(**dict(zip(names, refs, strict=True)))
    q_hbm, c_hbm, lat_hbm = R.queries, R.cotangent, R.latents
    line_of = lambda ref: ref[...].reshape(1, -1)
    q_ref, c_ref, lat_ref = R.q_v, R.c_v, R.lat_v
    wq, wk, wv, wo, wu, wd = R.wq_v, R.wk_v, R.wv_v, R.wo_v, R.wu_v, R.wd_v
    kv, qn_s, qp_s, p_s, mix_s, hn_s = R.kv, R.qn, R.qp, R.p, R.mix, R.hn
    act_s, dpre_s, dres_s, dm_s, dq_s = R.act, R.dpre, R.dres, R.dm, R.dq
    bo_v, gq_v, s_scr = R.bo_v, R.gq_v, R.s_scr
    lidT, ln_s, dkv_own, vec = R.lidT, R.ln, R.dkv_own, R.vec
    rows, positions, width = q_ref.shape
    lats, lwidth = lat_ref.shape[1:]
    pair = 2
    n_pairs = rows // pair
    tokens = rows * positions
    span = positions * pair

    loads = {}
    for k, (name, src, dst) in enumerate(
        [
            ("lat", lat_hbm, lat_ref),
            ("wk", R.key_weight, wk),
            ("wv", R.value_weight, wv),
            ("q", q_hbm, q_ref),
            ("wq", R.query_weight, wq),
            ("wo", R.out_weight, wo),
            ("wu", R.up_weight, wu),
            ("wd", R.down_weight, wd),
            ("c", c_hbm, c_ref),
        ]
    ):
        loads[name] = pltpu.make_async_copy(src, dst, R.load_sem.at[k])
        loads[name].start()

    pc = Place(n_rows)
    pc.barrier()

    def loop(first, last, body):
        def step(i, carry):
            body(i)
            return carry

        lax.fori_loop(first, last, step, 0)

    lane1 = lax.broadcasted_iota(jnp.int32, (1, 128), 1)

    def head_mask(hh, kind):
        return ((lane1 >= QKDIM * hh) & (lane1 < QKDIM * (hh + 1))).astype(kind)

    own = pl.ds(pl.multiple_of(pc.s * lats, lats), lats)

    def l0(g):
        rs = pl.ds(g * pair, pair)
        hat, _ = norm(flat(lat_ref[rs]).astype(f32))
        ln = (hat * line_of(R.gain_latent) + line_of(R.shift_latent)).astype(bf16)
        ln_s[pl.ds(g * pair * lats, pair * lats), :] = ln
        k = dg(ln, wk[...], 1, 0).astype(bf16)
        v = dg(ln, wv[...], 1, 0).astype(bf16)
        kv[rs, own, 0:256] = k.reshape(pair, lats, -1)
        kv[rs, own, 256:1024] = v.reshape(pair, lats, -1)

    def at(i):
        return pl.ds(pl.multiple_of(i * span, span), span)

    def row(r):
        return pl.ds(pl.multiple_of(r * positions, positions), positions)

    def f1(i):
        hat, _ = norm(flat(q_ref[pl.ds(i * pair, pair)]).astype(f32))
        qn = (hat * line_of(R.gain_query) + line_of(R.shift_query)).astype(bf16)
        qn_s[at(i), :] = qn
        qp_s[at(i), :] = (dg(qn, wq[...], 1, 0) * SCALE).astype(bf16)

    def f1b(i):
        c = flat(c_ref[pl.ds(i * pair, pair)])
        vec[5, :, :width] += row_sum(c.astype(f32))
        dpre_s[at(i), :] = dg(c, wd[...], 1, 1).astype(bf16)

    def spot(r, h):
        return pl.ds(pl.multiple_of((r * HEADS + h) * 256, 256), 256)

    def spots(r, g):
        return pl.ds(pl.multiple_of((r * HEADS + 4 * g) * 256, 1024), 1024)

    def f2(r):
        k = kv[r, :, :256]
        vT = kv[r, :, 256:].T
        lane = lax.broadcasted_iota(jnp.int32, (256, 128), 1)
        col = jnp.sum(jnp.where(lane == r, lidT[...], 0.0), axis=1, keepdims=True)
        allowed = col == R.query_ids[pl.ds(r, 1), :].astype(f32)
        for g in range(2):
            kb = k[:, 128 * g : 128 * g + 128]
            km = jnp.concatenate([kb * head_mask(hh, bf16) for hh in range(4)], axis=0)
            sg = dg(km, qp_s[row(r), 128 * g : 128 * g + 128], 1, 1)
            for hh in range(4):
                s_scr[4 * g + hh] = sg[256 * hh : 256 * (hh + 1)]
        for h in range(HEADS):
            s = jnp.where(allowed, s_scr[h], -1e30)
            e = jnp.exp(s - jnp.max(s, axis=0, keepdims=True))
            p_s[spot(r, h), :] = (e * (1.0 / jnp.sum(e, axis=0, keepdims=True))).astype(bf16)
        for h in range(HEADS):
            hs = slice(HDIM * h, HDIM * (h + 1))
            mix_s[hs, row(r)] = dg(vT[hs], p_s[spot(r, h), :], 1, 0).astype(bf16)


    def put_out(i):
        return pltpu.make_async_copy(bo_v, R.block_out.at[pl.ds(i * pair, pair)], R.bo_sem)

    def put_gq(r):
        return pltpu.make_async_copy(gq_v, R.grad_queries.at[r], R.gq_sem)

    def f3(i):
        rs = pl.ds(i * pair, pair)
        resid = flat(q_ref[rs]).astype(f32) + dg(mix_s[:, at(i)], wo[...], 0, 0)
        hat, inv = norm(resid)
        hn = (hat * line_of(R.gain_hidden) + line_of(R.shift_hidden)).astype(bf16)
        hn_s[at(i), :] = hn
        pre = dg(hn, wu[...], 1, 0) + line_of(R.bias_up)
        phi = 0.5 * (1.0 + lax.erf(pre * (0.5**0.5)))
        act = (pre * phi).astype(bf16)
        act_s[at(i), :] = act
        slope = phi + pre * (jnp.exp(-0.5 * pre * pre) * 0.3989422804014327)
        dpre = (dpre_s[at(i), :].astype(f32) * slope).astype(bf16)
        dpre_s[at(i), :] = dpre

        @pl.when(i >= 1)
        def _():
            put_out(i - 1).wait()

        out = (resid + dg(act, wd[...], 1, 0) + line_of(R.bias_down)).astype(bf16)
        bo_v[...] = out.reshape(bo_v.shape)
        put_out(i).start()
        vec[4, :, :width] += row_sum(dpre.astype(f32))
        dh = dg(dpre, wu[...], 1, 1)
        vec[2, :, :width] += row_sum(dh * hat)
        vec[3, :, :width] += row_sum(dh)
        cf = flat(c_ref[rs]).astype(f32)
        dlow = (norm_back(dh, line_of(R.gain_hidden), hat, inv) + cf).astype(bf16)
        dres_s[at(i), :] = dlow
        dm_s[:, at(i)] = dg(wo[...], dlow, 1, 1).astype(bf16)

    def b2(r):
        k = kv[r, :, :256]
        kT = k.T
        v = kv[r, :, 256:]
        dvs, dqs, dks = [], [], []
        for h in range(HEADS):
            hs = slice(HDIM * h, HDIM * (h + 1))
            s_scr[h] = dg(v[:, hs], dm_s[hs, row(r)], 1, 0)
        for h in range(HEADS):
            hs = slice(HDIM * h, HDIM * (h + 1))
            dvs.append(dg(dm_s[hs, row(r)], p_s[spot(r, h), :], 1, 1).astype(bf16))
        for h in range(HEADS):
            p = p_s[spot(r, h), :].astype(f32)
            pd = p * s_scr[h]
            ds = pd - p * jnp.sum(pd, axis=0, keepdims=True)
            p_s[spot(r, h), :] = ds.astype(bf16)
        for g in range(2):
            t = dg(p_s[spots(r, g), :], qp_s[row(r), 128 * g : 128 * g + 128], 1, 0)
            dks.append(sum(t[256 * hh : 256 * (hh + 1)] * head_mask(hh, f32) for hh in range(4)))
        for h in range(HEADS):
            kh = kT[QKDIM * h : QKDIM * (h + 1)]
            dqs.append(dg(kh, p_s[spot(r, h), :], 1, 0).astype(bf16))
        dq_s[row(r), :] = jnp.concatenate(dqs, axis=0).T
        kv[r, :, :128] = dks[0].astype(bf16)
        kv[r, :, 128:256] = dks[1].astype(bf16)
        kv[r, :, 256:] = jnp.concatenate(dvs, axis=0).T

    def b3(r):
        dqn = dg(dq_s[row(r), :], wq[...], 1, 1) * SCALE
        hat, inv = norm(q_ref[r].astype(f32))
        vec[0, :, :width] += row_sum(dqn * hat)
        vec[1, :, :width] += row_sum(dqn)

        got = norm_back(dqn, line_of(R.gain_query), hat, inv) + dres_s[row(r), :].astype(f32)

        @pl.when(r >= 1)
        def _():
            put_gq(r - 1).wait()

        gq_v[...] = got
        put_gq(r).start()

    def cols(j):
        return pl.ds(pl.multiple_of(j * 256, 256), 256)

    g_up, g_out = act_s.at[pl.ds(0, width)], hn_s.at[pl.ds(0, width)]

    def w_down():
        R.g_down[...] = dg(act_s[...], flat(c_ref[...]), 0, 0).astype(bf16)

    def w_up():
        g_up[...] = dg(hn_s[...], dpre_s[...], 0, 0).astype(bf16)

    def w_out():
        g_out[...] = dg(mix_s[...], dres_s[...], 1, 0).astype(bf16)

    def w_q():
        R.g_q[...] = (dg(qn_s[...], dq_s[...], 0, 0) * SCALE).astype(bf16)

    def w_kv(j):
        got = dg(ln_s[:, cols(j)], dkv_own[...], 0, 0).astype(bf16)
        for k in range(4):
            to = pl.ds(pl.multiple_of(k * lwidth + j * 256, 256), 256)
            p_s[to, :] = got[:, 256 * k : 256 * (k + 1)]

    put_gl = [
        pltpu.make_async_copy(
            s_scr.at[k, pl.ds(0, rows * lats)], R.grad_latents.at[:, pl.ds(256 * k, 256)], R.gl_sem.at[k]
        )
        for k in range(lwidth // 256)
    ]

    def l1():
        d = dg(dkv_own[:, :256], wk[...], 1, 1) + dg(dkv_own[:, 256:], wv[...], 1, 1)
        hat, inv = norm(flat(lat_ref[...]).astype(f32))
        vec[6] += row_sum(d * hat)
        vec[7] += row_sum(d)
        got = norm_back(d, line_of(R.gain_latent), hat, inv)
        for k, c in enumerate(put_gl):
            s_scr[k, : rows * lats, :] = got[:, 256 * k : 256 * (k + 1)]
            c.start()

    gathers = [
        Gather(pc, kv, pl.ds(g * pair, pair), R.ag_s.at[g], R.ag_r.at[g]) for g in range(n_pairs)
    ]
    scat, line = {}, {}
    for name, ref, lo, n in (
        ("down", R.g_down, 0, width),
        ("up", act_s, 0, width),
        ("out", hn_s, 0, width),
        ("q", R.g_q, 0, 256),
        *((f"kv{k}", p_s, k * lwidth, 256) for k in range(4)),
    ):
        block = (lwidth if ref is p_s else width) // 8

        def part(t, ref=ref, lo=lo, block=block):
            return ref.at[pl.ds(pl.multiple_of(lo + t * block, 32), block), :]

        sc = R.sc[name]
        scat[name] = Scatter(pc, part, n, **sc)
        line[name] = Line(pc, sc["l0"].at[pc.chip], kind=bf16, **R.li[name])
    for g in range(n_pairs):

        def part(t, g=g):
            return kv.at[pl.ds(g * pair, pair), pl.ds(pl.multiple_of(t * lats, lats), lats), :]

        scat[f"d{g}"] = Scatter(pc, part, 1024, **R.sc[f"d{g}"])

    def keep(g):
        dkv_own[pl.ds(g * pair * lats, pair * lats), :] = flat(R.sc[f"d{g}"]["l0"][pc.chip])

    vec[...] = jnp.zeros_like(vec)
    lid = R.latent_ids[...].astype(f32)
    lidT[...] = jnp.concatenate([lid, jnp.zeros((128 - rows, lid.shape[1]), f32)], axis=0).T
    G0, G1, G2 = gathers
    d0, d1, d2 = (scat[f"d{g}"] for g in range(3))
    D, U, O, Q = (scat[k] for k in ("down", "up", "out", "q"))
    LD, LU, LO, LQ = (line[k] for k in ("down", "up", "out", "q"))
    for k in ("lat", "wk", "wv"):
        loads[k].wait()
    l0(0)
    G0.p0()
    l0(1)
    l0(2)
    for k in ("q", "wq"):
        loads[k].wait()
    loop(0, n_pairs, f1)
    G0.p1()
    G1.p0()
    for k in ("c", "wd"):
        loads[k].wait()
    loop(0, n_pairs, f1b)
    G0.p2()
    G0.p3()
    for k in ("wo", "wu"):
        loads[k].wait()
    hooks = {
        0: ([G1.p1, G2.p0], [G1.p2, G1.p3, G2.p1, G0.drain], [d0.p0]),
        1: ([d0.p1, G2.p2], [d0.p2, G2.p3, G1.drain], [d0.p3, lambda: keep(0), d1.p0]),
        2: ([d1.p1], [d1.p2, G2.drain], []),
    }

    def hook(i, k):
        for p, fns in hooks.items():
            if fns[k]:

                @pl.when(i == p)
                def _():
                    for fn in fns[k]:
                        fn()

    def main(i):
        loop(i * pair, i * pair + pair, f2)
        hook(i, 0)
        f3(i)
        hook(i, 1)

        @pl.when(i < n_pairs - 1)
        def _():
            loop(i * pair, i * pair + pair, b2)

        hook(i, 2)

    loop(0, n_pairs, main)
    w_down()
    D.p0()
    d1.p3()
    keep(1)
    w_up()
    U.p0()
    D.p1()
    w_out()
    O.p0()
    U.p1()
    D.p2()
    b2(rows - 2)
    O.p1()
    b2(rows - 1)
    d2.p0()
    D.p3()
    LD.up()
    U.p2()
    loop(0, 3, b3)
    d2.p1()
    O.p2()
    U.p3()
    LU.up()
    LD.middle()
    loop(3, rows, b3)
    d2.p2()
    w_q()
    Q.p0()
    O.p3()
    LO.up()
    LU.middle()
    LD.down()
    d2.p3()
    keep(2)
    Q.p1()
    loop(0, 5, w_kv)
    KV = [scat[f"kv{k}"] for k in range(4)]
    LKV = [line[f"kv{k}"] for k in range(4)]
    for K in KV:
        K.p0()
    l1()
    vtot = R.vtot
    vtot[0] = jnp.sum(vec[...], axis=1)
    vsteps = [
        rcopy(vtot.at[k], R.vland.at[k], R.vs.at[k], R.vr.at[k], peer)
        for k, peer in enumerate((pc.sib, pc.xn, pc.yn))
    ]
    lv = Line(pc, vtot.at[3], kind=f32, **R.ln_vec)

    def vstep(k):
        vsteps[k].wait_recv()
        vtot[k + 1] = vtot[k] + R.vland[k]

    LO.middle()
    LU.down()
    vsteps[0].start()
    KV[0].p1()
    KV[1].p1()
    vstep(0)
    vsteps[1].start()
    Q.p2()
    KV[2].p1()
    LO.down()
    KV[3].p1()
    KV[0].p2()
    vstep(1)
    vsteps[2].start()
    KV[1].p2()
    Q.p3()
    LQ.up()
    KV[0].p3()
    LKV[0].up()
    KV[2].p2()
    KV[1].p3()
    LKV[1].up()
    vstep(2)
    lv.up()
    KV[3].p2()
    LQ.middle()
    LKV[0].middle()
    KV[2].p3()
    LKV[2].up()
    LKV[1].middle()
    lv.middle()
    KV[3].p3()
    LKV[3].up()
    LQ.down()
    LKV[0].down()
    LKV[2].middle()
    LKV[1].down()
    lv.down()
    LKV[3].middle()
    LKV[2].down()
    LKV[3].down()

    totals = []
    for k, (name, out) in enumerate(
        (
            ("down", R.t_down),
            ("up", R.t_up),
            ("out", R.t_out),
            ("q", R.t_q),
            *((f"kv{j}", R.t_kv.at[j]) for j in range(4)),
            ("v", R.t_vec),
        )
    ):
        sem = R.t_sem.at[k]
        x = line.get(name, lv)
        x.result(lambda src, out=out, sem=sem: pltpu.make_async_copy(src, out, sem).start())
        totals.append(pltpu.make_async_copy(x.zt, out, sem))
    for c in totals:
        c.wait()
    for x in (*scat.values(), *line.values(), lv):
        x.drain()
    for c in vsteps:
        c.wait_send()
    put_out(n_pairs - 1).wait()
    put_gq(rows - 1).wait()
    for c in put_gl:
        c.wait()


def unpack(*refs):
    block_out, grad_queries, grad_latents, t_down, t_up, t_out, t_q, t_kv, t_vec = refs[:9]
    out = Outs(*refs[9 : 9 + len(Outs._fields)])
    through = refs[9 + len(Outs._fields) :]
    rows = block_out.shape[0]
    step = rows // 3
    pipes = []
    for k, (src, dst) in enumerate(
        ((grad_queries, out.grad_queries), (block_out, out.block_out), (grad_latents, out.grad_latents))
    ):
        via, sem_in, sem_out = through[3 * k : 3 * k + 3]
        for j in range(3):
            rs = pl.ds(j * step, step)
            inward = pltpu.make_async_copy(src.at[rs], via.at[rs], sem_in.at[j])
            pipes.append((inward, pltpu.make_async_copy(via.at[rs], dst.at[rs], sem_out.at[j])))
    for inward, _ in pipes:
        inward.start()

    def spread():
        out.grad_down_weight[...] = t_down[...].astype(f32)
        out.grad_up_weight[...] = t_up[...].astype(f32)
        out.grad_out_weight[...] = t_out[...].astype(f32)
        out.grad_query_weight[...] = t_q[...].astype(f32)
        out.grad_key_weight[...] = t_kv[0].astype(f32)
        for k in range(3):
            out.grad_value_weight[:, 256 * k : 256 * (k + 1)] = t_kv[k + 1].astype(f32)
        vectors = (
            out.grad_gain_query,
            out.grad_shift_query,
            out.grad_gain_hidden,
            out.grad_shift_hidden,
            out.grad_bias_up,
            out.grad_bias_down,
            out.grad_gain_latent,
            out.grad_shift_latent,
        )
        for t in range(8):

            @pl.when(lax.axis_index("seq") == t)
            def _():
                for k, ref in enumerate(vectors):
                    n = ref.shape[0]
                    ref[...] = t_vec[k, n * t : n * (t + 1)]

    for inward, outward in pipes:
        inward.wait()
        outward.start()
    spread()
    for _, outward in pipes:
        outward.wait()


class Args(NamedTuple):
    queries: Any
    latents: Any
    query_ids: Any
    latent_ids: Any
    query_weight: Any
    key_weight: Any
    value_weight: Any
    out_weight: Any
    up_weight: Any
    down_weight: Any
    gain_query: Any
    shift_query: Any
    gain_latent: Any
    shift_latent: Any
    gain_hidden: Any
    shift_hidden: Any
    bias_up: Any
    bias_down: Any
    cotangent: Any


class Outs(NamedTuple):
    block_out: Any
    grad_queries: Any
    grad_latents: Any
    grad_query_weight: Any
    grad_key_weight: Any
    grad_value_weight: Any
    grad_out_weight: Any
    grad_up_weight: Any
    grad_down_weight: Any
    grad_gain_query: Any
    grad_shift_query: Any
    grad_gain_latent: Any
    grad_shift_latent: Any
    grad_gain_hidden: Any
    grad_shift_hidden: Any
    grad_bias_up: Any
    grad_bias_down: Any


def body(n_rows, n_seq, *args):
    A = Args(*args)
    rows, pos, width = A.queries.shape
    lats, lwidth = A.latents.shape[1:]
    nl = lats * n_seq
    F_ = lambda *s: jax.ShapeDtypeStruct(s, f32)
    wide, vec, lvec = F_(width // n_seq, width), F_(width // n_seq), F_(lwidth // n_seq)
    out = Outs(
        block_out=jax.ShapeDtypeStruct((rows, pos, width), bf16),
        grad_queries=F_(rows, pos, width),
        grad_latents=F_(rows, lats, lwidth),
        grad_query_weight=F_(width // n_seq, 256),
        grad_key_weight=F_(lwidth // n_seq, 256),
        grad_value_weight=F_(lwidth // n_seq, width),
        grad_out_weight=wide,
        grad_up_weight=wide,
        grad_down_weight=wide,
        grad_gain_query=vec,
        grad_shift_query=vec,
        grad_gain_latent=lvec,
        grad_shift_latent=lvec,
        grad_gain_hidden=vec,
        grad_shift_hidden=vec,
        grad_bias_up=vec,
        grad_bias_down=vec,
    )
    V = lambda *s: pltpu.VMEM(s, bf16)
    F = lambda *s: pltpu.VMEM(s, f32)
    dma = lambda *s: pltpu.SemaphoreType.DMA(s)
    tok = V(rows, pos, width)
    tok2 = V(rows * pos, width)
    tokT = V(width, rows * pos)
    scratch = dict(
        q_v=tok,
        c_v=tok,
        lat_v=V(rows, lats, lwidth),
        wq_v=V(width, 256),
        wk_v=V(lwidth, 256),
        wv_v=V(lwidth, width),
        wo_v=V(width, width),
        wu_v=V(width, width),
        wd_v=V(width, width),
        kv=V(rows, nl, 1024),
        qn=tok2,
        qp=V(rows * pos, 256),
        s_scr=F(HEADS, nl, pos),
        p=V(rows * HEADS * nl, pos),
        mix=tokT,
        hn=tok2,
        act=tok2,
        dpre=tok2,
        dres=tok2,
        dm=tokT,
        dq=V(rows * pos, 256),
        lidT=F(nl, 128),
        ln=V(rows * lats, lwidth),
        dkv_own=V(rows * lats, 1024),
        vec=F(8, 8, lwidth),
        vtot=F(4, 8, lwidth),
        vland=F(3, 8, lwidth),
        vs=dma(3),
        vr=dma(3),
        bo_v=V(2, pos, width),
        gq_v=F(pos, width),
        bo_sem=pltpu.SemaphoreType.DMA(()),
        gq_sem=pltpu.SemaphoreType.DMA(()),
        gl_sem=dma(lwidth // 256),
        t_sem=dma(9),
        load_sem=dma(9),
        ag_s=dma(rows // 2, 9),
        ag_r=dma(rows // 2, 9),
        g_down=V(width, width),
        g_q=V(width, 256),
        ln_vec=line_scratch((8, lwidth), f32),
    )
    lead, llead = (width // n_seq,), (lwidth // n_seq,)
    scratch["sc"] = dict(
        down=scatter_scratch(lead, width),
        up=scatter_scratch(lead, width),
        out=scatter_scratch(lead, width),
        q=scatter_scratch(lead, 256),
        **{f"d{g}": scatter_scratch((2, lats), 1024) for g in range(rows // 2)},
        **{f"kv{k}": scatter_scratch(llead, 256) for k in range(4)},
    )
    scratch["li"] = dict(
        down=line_scratch((*lead, width), bf16),
        up=line_scratch((*lead, width), bf16),
        out=line_scratch((*lead, width), bf16),
        q=line_scratch((*lead, 256), bf16),
        **{f"kv{k}": line_scratch((*llead, 256), bf16) for k in range(4)},
    )
    any_ = pl.BlockSpec(memory_space=pl.ANY)
    vm = pl.BlockSpec(memory_space=pltpu.VMEM)
    far = (A.queries, A.cotangent, A.latents, *A[4:10])
    in_specs = [any_ if any(a is f for f in far) else vm for a in A]
    sds = jax.ShapeDtypeStruct
    mid = dict(
        block_out=out.block_out,
        grad_queries=out.grad_queries,
        grad_latents=F_(rows * lats, lwidth),
        t_down=sds(wide.shape, bf16),
        t_up=sds(wide.shape, bf16),
        t_out=sds(wide.shape, bf16),
        t_q=sds((width // n_seq, 256), bf16),
        t_kv=sds((4, lwidth // n_seq, 256), bf16),
        t_vec=sds((8, lwidth), f32),
    )
    names = (*Args._fields, *mid, *scratch)
    flops = 2 * rows * pos * width * width * 14
    got = pl.pallas_call(
        functools.partial(kernel, n_rows, names),
        out_shape=tuple(mid.values()),
        in_specs=in_specs,
        out_specs=(any_,) * len(mid),
        scratch_shapes=list(scratch.values()),
        compiler_params=pltpu.CompilerParams(
            collective_id=0, has_side_effects=True, vmem_limit_bytes=64 << 20
        ),
        cost_estimate=pl.CostEstimate(flops=flops, bytes_accessed=24 << 20, transcendentals=0),
    )(*A)
    got = (*got[:2], got[2].reshape(rows, lats, lwidth), *got[3:])
    return pl.pallas_call(
        unpack,
        out_shape=tuple(out),
        in_specs=[any_] * 3 + [vm] * 6,
        out_specs=(any_,) * 3 + (vm,) * 14,
        scratch_shapes=[
            x
            for o in (out.grad_queries, out.block_out, out.grad_latents)
            for x in (pltpu.VMEM(o.shape, o.dtype), dma(3), dma(3))
        ],
        compiler_params=pltpu.CompilerParams(vmem_limit_bytes=64 << 20),
        cost_estimate=pl.CostEstimate(flops=0, bytes_accessed=18 << 20, transcendentals=0),
    )(*got)


def solution(mesh):
    seq = P("rows", "seq", None)
    rep = P()
    in_specs = (seq, seq, P("rows", "seq"), P("rows", None)) + (rep,) * 14 + (seq,)
    out_specs = (seq,) * 3 + (P("seq", None),) * 6 + (P("seq"),) * 8
    return jax.shard_map(
        functools.partial(body, mesh.shape["rows"], mesh.shape["seq"]),
        mesh=mesh,
        in_specs=in_specs,
        out_specs=out_specs,
        check_vma=False,
    )
```

```python
import functools
import types
from typing import Any, NamedTuple

import jax
import jax.numpy as jnp
from jax import lax
from jax.experimental import pallas as pl
from jax.experimental.pallas import tpu as pltpu
from jax.sharding import PartitionSpec as P

HEADS = 8
HDIM = 96
QKDIM = 32
EPS = 1e-05
SCALE = QKDIM ** (-0.5)
MESH = pl.DeviceIdType.MESH
f32, bf16 = jnp.float32, jnp.bfloat16


def dg(a, b, ca, cb):
    return lax.dot_general(a, b, (((ca,), (cb,)), ((), ())), preferred_element_type=f32)


def norm(x):
    mean = jnp.mean(x, -1, keepdims=True)
    cen = x - mean
    inv = lax.rsqrt(jnp.mean(cen * cen, -1, keepdims=True) + EPS)
    return cen * inv, inv


def norm_back(grad, gain, hat, inv):
    g = grad * gain
    return inv * (
        g - jnp.mean(g, -1, keepdims=True) - hat * jnp.mean(g * hat, -1, keepdims=True)
    )


def row_sum(x):
    n, w = x.shape
    return jnp.sum(x.reshape(n // 8, 8, w), axis=0)


def flat(x):
    return x.reshape(-1, x.shape[-1])


def add(a, b):
    return (a.astype(f32) + b.astype(f32)).astype(bf16)


class Place:
    def __init__(self, n_rows):
        self.n = n_rows
        self.s = lax.axis_index("seq")
        self.r = lax.axis_index("rows")
        self.core = lax.rem(self.s, 2)
        self.chip = self.s // 2
        self.xc = self.chip + 1 - 2 * lax.rem(self.chip, 2)
        self.yc = lax.rem(self.chip + 2, 4)
        self.dc = lax.rem(self.xc + 2, 4)
        self.xb, self.yb = lax.rem(self.chip, 2), self.chip // 2
        self.sib = (self.s + 1 - 2 * self.core, self.r)
        self.xn = (2 * self.xc + self.core, self.r)
        self.yn = (2 * self.yc + self.core, self.r)
        half = n_rows // 2
        self.left = self.r < half
        self.mid = (self.r == half - 1) | (self.r == half)
        self.not_end = (self.r != 0) & (self.r != n_rows - 1)
        step = jnp.where(self.left, 1, -1)
        self.inner = (self.s, lax.rem(self.r + step + n_rows, n_rows))
        self.outer = (self.s, lax.rem(self.r - step + n_rows, n_rows))

    def greet(self):
        up = (self.s, lax.rem(self.r + 1, self.n))
        down = (self.s, lax.rem(self.r + self.n - 1, self.n))
        self.bar = pltpu.get_barrier_semaphore()
        for peer in (self.sib, self.xn, self.yn, up, down):
            pl.semaphore_signal(self.bar, inc=1, device_id=peer, device_id_type=MESH)

    def met(self):
        pl.semaphore_wait(self.bar, 5)


def rcopy(src, dst, ssem, rsem, peer):
    return pltpu.make_async_remote_copy(
        src_ref=src, dst_ref=dst, send_sem=ssem, recv_sem=rsem, device_id=peer, device_id_type=MESH
    )


class Line:
    def __init__(self, pc, src, zo, zi, ssem, rsem, kind):
        zt = zo
        self.pc, self.src, self.zo, self.zi, self.zt, self.kind = pc, src, zo, zi, zt, kind
        self.up_c = rcopy(src, zo, ssem.at[0], rsem.at[0], pc.inner)
        self.cross_c = rcopy(src, zi, ssem.at[1], rsem.at[1], pc.inner)
        self.down_mid = rcopy(zt, zi, ssem.at[2], rsem.at[1], pc.outer)
        self.down_far = rcopy(zi, zi, ssem.at[2], rsem.at[1], pc.outer)

    def plus(self, a, b):
        return (a.astype(f32) + b.astype(f32)).astype(self.kind)

    def send(self):
        pc = self.pc
        pl.when(jnp.logical_not(pc.not_end) & jnp.logical_not(pc.mid))(self.up_c.start)

    def up(self):
        pc = self.pc

        @pl.when(pc.not_end)
        def _():
            self.up_c.wait_recv()
            self.src[...] = self.plus(self.src[...], self.zo[...])

        pl.when(pc.mid)(self.cross_c.start)
        pl.when(jnp.logical_not(pc.mid) & pc.not_end)(self.up_c.start)

    def middle(self):
        pc = self.pc

        @pl.when(pc.mid)
        def _():
            self.cross_c.wait_recv()
            self.zt[...] = self.plus(self.src[...], self.zi[...])

        pl.when(pc.mid & pc.not_end)(self.down_mid.start)

    def down(self):
        pc = self.pc
        pl.when(jnp.logical_not(pc.mid))(self.cross_c.wait_recv)
        pl.when(jnp.logical_not(pc.mid) & pc.not_end)(self.down_far.start)

    def result(self, write):
        pc = self.pc
        pl.when(pc.mid)(lambda: write(self.zt))
        pl.when(jnp.logical_not(pc.mid))(lambda: write(self.zi))

    def drain(self):
        pc = self.pc
        pl.when(pc.mid)(self.cross_c.wait_send)
        pl.when(jnp.logical_not(pc.mid))(self.up_c.wait_send)
        pl.when(pc.mid & pc.not_end)(self.down_mid.wait_send)
        pl.when(jnp.logical_not(pc.mid) & pc.not_end)(self.down_far.wait_send)


class Scatter:
    def __init__(self, pc, part, width, l0, la, lb, la2, lb2, ssem, rsem, then=None):
        self.pc, self.part, self.l0, self.then = pc, part, l0, then
        self.la, self.lb, self.la2, self.lb2 = la, lb, la2, lb2
        h = width // 2
        A, B = self.A, self.B = pl.ds(0, h), pl.ds(h, h)
        lead = (slice(None),) * (len(l0.shape) - 3)
        xb, yb = pc.xb, pc.yb

        def blk(y, x, cols):
            return l0.at[(y, x, *lead, cols)]

        self.blk = blk
        other = 1 - pc.core
        self.pair = [
            rcopy(part(2 * q + other), l0.at[q // 2, q % 2], ssem.at[q], rsem.at[q], pc.sib)
            for q in range(4)
        ]
        every = slice(None)
        self.first = [
            rcopy(blk(every, 1 - xb, A), la, ssem.at[4], rsem.at[4], pc.xn),
            rcopy(blk(1 - yb, every, B), lb, ssem.at[5], rsem.at[5], pc.yn),
        ]
        self.second = [
            rcopy(blk(1 - yb, xb, A), la2, ssem.at[6], rsem.at[6], pc.yn),
            rcopy(blk(yb, 1 - xb, B), lb2, ssem.at[7], rsem.at[7], pc.xn),
        ]

    def p0(self):
        for c in self.pair:
            c.start()

    def p1(self):
        for q in range(4):
            self.pair[q].wait_recv()
            own = self.part(2 * q + self.pc.core)[...]
            self.l0[q // 2, q % 2] = add(self.l0[q // 2, q % 2], own)
        for c in self.first:
            c.start()

    def into(self, y, x, cols, got):
        v = self.blk(y, x, cols)
        v[...] = add(v[...], got[...])

    def p2(self):
        xb, yb = self.pc.xb, self.pc.yb
        self.first[0].wait_recv()
        self.into(1 - yb, xb, self.A, self.la.at[1 - yb])
        self.second[0].start()
        self.first[1].wait_recv()
        self.into(yb, 1 - xb, self.B, self.lb.at[1 - xb])
        self.second[1].start()
        self.into(yb, xb, self.A, self.la.at[yb])
        self.into(yb, xb, self.B, self.lb.at[xb])

    def p3(self):
        for c, cols, got in zip(self.second, (self.A, self.B), (self.la2, self.lb2)):
            c.wait_recv()
            self.into(self.pc.yb, self.pc.xb, cols, got)
        self.then()

    def drain(self):
        for c in self.pair + self.first + self.second:
            c.wait_send()


class Job:
    def __init__(self, scatter, line, out, sem):
        self.scatter, self.line = scatter, line
        scatter.then = line.send
        self.p0, self.p1, self.p2, self.p3 = scatter.p0, scatter.p1, scatter.p2, scatter.p3
        self.up, self.mid, self.dn = line.up, line.middle, line.down
        self.out, self.sem = out, sem

    def store(self):
        self.line.result(lambda src: pltpu.make_async_copy(src, self.out, self.sem).start())

    def drain(self):
        pltpu.make_async_copy(self.line.zo, self.out, self.sem).wait()
        self.scatter.drain()
        self.line.drain()


class Vectors:
    def __init__(self, pc, vec, tot, land, ssem, rsem, line):
        self.vec, self.tot, self.land, self.line = vec, tot, land, line
        self.steps = [
            rcopy(tot.at[k], land.at[k], ssem.at[k], rsem.at[k], peer)
            for k, peer in enumerate((pc.sib, pc.xn, pc.yn))
        ]
        self.up, self.mid, self.dn = line.up, line.middle, line.down

    def p0(self):
        self.tot[0] = jnp.sum(self.vec[...], axis=1)
        self.steps[0].start()

    def take(self, k):
        self.steps[k].wait_recv()
        self.tot[k + 1] = self.tot[k] + self.land[k]

    def p1(self):
        self.take(0)
        self.steps[1].start()

    def p2(self):
        self.take(1)
        self.steps[2].start()

    def p3(self):
        self.take(2)
        self.line.send()

    def drain(self):
        for c in self.steps:
            c.wait_send()
        self.line.drain()


def scatter_scratch(lead, width):
    half = width // 2
    return dict(
        l0=pltpu.VMEM((2, 2, *lead, width), bf16),
        la=pltpu.VMEM((2, *lead, half), bf16),
        lb=pltpu.VMEM((2, *lead, half), bf16),
        la2=pltpu.VMEM((*lead, half), bf16),
        lb2=pltpu.VMEM((*lead, half), bf16),
        ssem=pltpu.SemaphoreType.DMA((8,)),
        rsem=pltpu.SemaphoreType.DMA((8,)),
    )


def line_scratch(shape, kind):
    return dict(
        zo=pltpu.VMEM(shape, kind),
        zi=pltpu.VMEM(shape, kind),
        ssem=pltpu.SemaphoreType.DMA((3,)),
        rsem=pltpu.SemaphoreType.DMA((2,)),
    )


class Gather:
    def __init__(self, pc, kv, rows, ssem, rsem):
        def blk(t, cols=slice(None)):
            return kv.at[rows, pl.ds(pl.multiple_of(t * 32, 32), 32), cols]

        h = kv.shape[-1] // 2
        A, B = pl.ds(0, h), pl.ds(h, h)
        ds_ = 2 * pc.dc + pc.core

        def copy(k, ref, peer):
            return rcopy(ref, ref, ssem.at[k], rsem.at[k], peer)

        self.own = [copy(0, blk(pc.s), pc.sib), copy(1, blk(pc.s), pc.xn), copy(2, blk(pc.s), pc.yn)]
        self.from_x = [copy(3, blk(pc.xn[0], A), pc.yn), copy(4, blk(pc.xn[0]), pc.sib)]
        self.from_y = [copy(5, blk(pc.yn[0], B), pc.xn), copy(6, blk(pc.yn[0]), pc.sib)]
        self.from_d = [copy(7, blk(ds_, A), pc.sib), copy(8, blk(ds_, B), pc.sib)]

    def p0(self):
        for c in self.own[::-1]:
            c.start()

    def p1(self):
        self.own[1].wait_recv()
        for c in self.from_x:
            c.start()
        self.own[2].wait_recv()
        for c in self.from_y:
            c.start()

    def p2(self):
        self.from_x[0].wait_recv()
        self.from_d[0].start()
        self.from_y[0].wait_recv()
        self.from_d[1].start()

    def p3(self):
        for c in (self.own[0], self.from_x[1], self.from_y[1], *self.from_d):
            c.wait_recv()

    def drain(self):
        for c in self.own + self.from_x + self.from_y + self.from_d:
            c.wait_send()


def kernel(n_rows, names, *refs):
    R = types.SimpleNamespace(**dict(zip(names, refs, strict=True)))
    q_hbm, c_hbm, lat_hbm = R.queries, R.cotangent, R.latents
    line_of = lambda ref: ref[...].reshape(1, -1)
    q_ref, c_ref, lat_ref = R.q_v, R.c_v, R.lat_v
    wq, wk, wv, wo, wu, wd = R.wq_v, R.wk_v, R.wv_v, R.wo_v, R.wu_v, R.wd_v
    kv, qn_s, qp_s, p_s, mix_s, hn_s = R.kv, R.qn, R.qp, R.p, R.mix, R.hn
    act_s, dpre_s, dres_s, dm_s, dq_s = R.act, R.dpre, R.dres, R.dm, R.dq
    s_scr, ds_scr, inv_s = R.s_scr, R.ds_scr, R.inv
    lidT, ln_s, dkv_own, vec = R.lidT, R.ln, R.dkv_own, R.vec
    rows, positions, width = q_ref.shape
    lats, lwidth = lat_ref.shape[1:]
    pair = 2
    n_pairs = rows // pair
    tokens = rows * positions
    span = positions * pair

    loads = {}
    for k, (name, src, dst) in enumerate(
        [
            ("lat", lat_hbm, lat_ref),
            ("wk", R.key_weight, wk),
            ("wv", R.value_weight, wv),
            ("q", q_hbm, q_ref),
            ("wq", R.query_weight, wq),
            ("wo", R.out_weight, wo),
            ("wu", R.up_weight, wu),
            ("wd", R.down_weight, wd),
            ("c", c_hbm, c_ref),
        ]
    ):
        loads[name] = pltpu.make_async_copy(src, dst, R.load_sem.at[k])
        loads[name].start()

    pc = Place(n_rows)
    pc.greet()

    def loop(first, last, body):
        def step(i, carry):
            body(i)
            return carry

        lax.fori_loop(first, last, step, 0)

    lane1 = lax.broadcasted_iota(jnp.int32, (1, 128), 1)

    def head_mask(hh, kind):
        return ((lane1 >= QKDIM * hh) & (lane1 < QKDIM * (hh + 1))).astype(kind)

    own = pl.ds(pl.multiple_of(pc.s * lats, lats), lats)

    def l0(g):
        rs = pl.ds(g * pair, pair)
        hat, _ = norm(flat(lat_ref[rs]).astype(f32))
        ln = (hat * line_of(R.gain_latent) + line_of(R.shift_latent)).astype(bf16)
        ln_s[pl.ds(g * pair * lats, pair * lats), :] = ln
        k = dg(ln, wk[...], 1, 0).astype(bf16)
        v = dg(ln, wv[...], 1, 0).astype(bf16)
        kv[rs, own, 0:256] = k.reshape(pair, lats, -1)
        kv[rs, own, 256:1024] = v.reshape(pair, lats, -1)

    def at(i):
        return pl.ds(pl.multiple_of(i * span, span), span)

    def row(r):
        return pl.ds(pl.multiple_of(r * positions, positions), positions)

    def f1(i):
        hat, _ = norm(flat(q_ref[pl.ds(i * pair, pair)]).astype(f32))
        qn = (hat * line_of(R.gain_query) + line_of(R.shift_query)).astype(bf16)
        qn_s[at(i), :] = qn
        qp_s[at(i), :] = (dg(qn, wq[...], 1, 0) * SCALE).astype(bf16)

    def f1b(i):
        c = flat(c_ref[pl.ds(i * pair, pair)])
        vec[5, :, :width] += row_sum(c.astype(f32))
        dpre_s[at(i), :] = dg(c, wd[...], 1, 1).astype(bf16)

    def row8(r):
        return pl.ds(pl.multiple_of(r * HEADS * 256, HEADS * 256), HEADS * 256)

    def f2(r):
        k = kv[r, :, :256]
        vT = kv[r, :, 256:].T
        lane = lax.broadcasted_iota(jnp.int32, (256, 128), 1)
        col = jnp.sum(jnp.where(lane == r, lidT[...], 0.0), axis=1, keepdims=True)
        allowed = col == R.query_ids[pl.ds(r, 1), :].astype(f32)
        for g in range(2):
            kb = k[:, 128 * g : 128 * g + 128]
            km = jnp.concatenate([kb * head_mask(hh, bf16) for hh in range(4)], axis=0)
            sg = dg(km, qp_s[row(r), 128 * g : 128 * g + 128], 1, 1)
            for hh in range(4):
                s_scr[4 * g + hh] = sg[256 * hh : 256 * (hh + 1)]
        p_r = p_s.at[row8(r)]
        for h in range(HEADS):
            s = jnp.where(allowed, s_scr[h], -1e30)
            e = jnp.exp(s - jnp.max(s, axis=0, keepdims=True))
            p_r[256 * h : 256 * (h + 1), :] = e.astype(bf16)
            inv_s[r, h : h + 1, :] = 1.0 / jnp.sum(e, axis=0, keepdims=True)
        mix_r = mix_s.at[:, row(r)]
        for h in range(HEADS):
            hs = slice(HDIM * h, HDIM * (h + 1))
            got = dg(vT[hs], p_r[256 * h : 256 * (h + 1), :], 1, 0)
            mix_r[hs, :] = (got * inv_s[r, h : h + 1, :]).astype(bf16)

    def chunks(dst, sems, i, n):
        return [
            pltpu.make_async_copy(
                ds_scr.at[pl.ds(k * n, n)],
                dst.at[pl.ds(pl.multiple_of(i * n, n), n), pl.ds(256 * k, 256)],
                sems.at[k],
            )
            for k in range(width // 256)
        ]

    def stage(value, dst, sems, i, n):
        for k, c in enumerate(chunks(dst, sems, i, n)):
            ds_scr[n * k : n * (k + 1), :] = value[:, 256 * k : 256 * (k + 1)].astype(bf16)
            c.start()

    def staged(dst, sems, i, n):
        for c in chunks(dst, sems, i, n):
            c.wait()

    def f3(i, between):
        rs = pl.ds(i * pair, pair)
        resid = flat(q_ref[rs]).astype(f32) + dg(mix_s[:, at(i)], wo[...], 0, 0)
        hat, inv = norm(resid)
        hn = (hat * line_of(R.gain_hidden) + line_of(R.shift_hidden)).astype(bf16)
        hn_s[at(i), :] = hn
        pre = dg(hn, wu[...], 1, 0) + line_of(R.bias_up)
        phi = 0.5 * (1.0 + lax.erf(pre * (0.5**0.5)))
        act = (pre * phi).astype(bf16)
        act_s[at(i), :] = act
        slope = phi + pre * (jnp.exp(-0.5 * pre * pre) * 0.3989422804014327)
        dpre = (dpre_s[at(i), :].astype(f32) * slope).astype(bf16)
        dpre_s[at(i), :] = dpre

        between()
        out = resid + dg(act, wd[...], 1, 0) + line_of(R.bias_down)
        stage(out, R.block_out, R.bo_sem, i, span)
        vec[4, :, :width] += row_sum(dpre.astype(f32))
        dh = dg(dpre, wu[...], 1, 1)
        vec[2, :, :width] += row_sum(dh * hat)
        vec[3, :, :width] += row_sum(dh)
        cf = flat(c_ref[rs]).astype(f32)
        dlow = (norm_back(dh, line_of(R.gain_hidden), hat, inv) + cf).astype(bf16)
        dres_s[at(i), :] = dlow
        dm_s[:, at(i)] = dg(wo[...], dlow, 1, 1).astype(bf16)
        staged(R.block_out, R.bo_sem, i, span)

    def b2(r):
        k = kv[r, :, :256]
        kT = k.T
        v = kv[r, :, 256:]
        dvs, dqs, dks = [], [], []
        p_r, dm_r, qp_r = p_s.at[row8(r)], dm_s.at[:, row(r)], qp_s.at[row(r)]
        for h in range(HEADS):
            hs = slice(HDIM * h, HDIM * (h + 1))
            dm_r[hs, :] = (dm_r[hs, :].astype(f32) * inv_s[r, h : h + 1, :]).astype(bf16)
        for h in range(HEADS):
            hs = slice(HDIM * h, HDIM * (h + 1))
            s_scr[h] = dg(v[:, hs], dm_r[hs, :], 1, 0)
        for h in range(HEADS):
            hs = slice(HDIM * h, HDIM * (h + 1))
            dvs.append(dg(dm_r[hs, :], p_r[256 * h : 256 * (h + 1), :], 1, 1).astype(bf16))
        for h in range(HEADS):
            e = p_r[256 * h : 256 * (h + 1), :].astype(f32)
            ed = e * s_scr[h]
            ds = ed - e * (jnp.sum(ed, axis=0, keepdims=True) * inv_s[r, h : h + 1, :])
            ds_scr[256 * h : 256 * (h + 1), :] = ds.astype(bf16)
        for g in range(2):
            t = dg(ds_scr[1024 * g : 1024 * (g + 1), :], qp_r[:, 128 * g : 128 * g + 128], 1, 0)
            dks.append(sum(t[256 * hh : 256 * (hh + 1)] * head_mask(hh, f32) for hh in range(4)))
        for h in range(HEADS):
            kh = kT[QKDIM * h : QKDIM * (h + 1)]
            dqs.append(dg(kh, ds_scr[256 * h : 256 * (h + 1), :], 1, 0).astype(bf16))
        dq_s[row(r), :] = jnp.concatenate(dqs, axis=0).T
        kv[r, :, :128] = dks[0].astype(bf16)
        kv[r, :, 128:256] = dks[1].astype(bf16)
        kv[r, :, 256:] = jnp.concatenate(dvs, axis=0).T

    def b3(r):
        dqn = dg(dq_s[row(r), :], wq[...], 1, 1) * SCALE
        hat, inv = norm(q_ref[r].astype(f32))
        vec[0, :, :width] += row_sum(dqn * hat)
        vec[1, :, :width] += row_sum(dqn)

        got = norm_back(dqn, line_of(R.gain_query), hat, inv) + dres_s[row(r), :].astype(f32)

        if r >= 1:
            staged(R.grad_queries, R.gq_sem, r - 1, positions)

        stage(got, R.grad_queries, R.gq_sem, r, positions)

    def cols(j):
        return pl.ds(pl.multiple_of(j * 256, 256), 256)

    def cols_at(j):
        return pl.ds(256 * j, 256)

    def w_down(j):
        R.g_down[:, cols_at(j)] = dg(act_s[...], flat(c_ref[:, :, cols_at(j)]), 0, 0).astype(bf16)

    g_up, g_out = act_s.at[pl.ds(0, width)], hn_s.at[pl.ds(0, width)]

    def w_up(j):
        g_up[:, cols_at(j)] = dg(hn_s[...], dpre_s[:, cols_at(j)], 0, 0).astype(bf16)

    def w_out(j):
        g_out[:, cols_at(j)] = dg(mix_s[...], dres_s[:, cols_at(j)], 1, 0).astype(bf16)

    def w_q():
        R.g_q[...] = (dg(qn_s[...], dq_s[...], 0, 0) * SCALE).astype(bf16)

    def w_kv(j):
        got = dg(ln_s[:, cols(j)], dkv_own[...], 0, 0).astype(bf16)
        for k in range(4):
            to = pl.ds(pl.multiple_of(k * lwidth + j * 256, 256), 256)
            p_s[to, :] = got[:, 256 * k : 256 * (k + 1)]

    put_gl = [
        pltpu.make_async_copy(
            ds_scr.at[pl.ds(1024 + k * rows * lats, rows * lats)], R.grad_latents.at[:, pl.ds(256 * k, 256)], R.gl_sem.at[k]
        )
        for k in range(lwidth // 256)
    ]

    def l1():
        d = dg(dkv_own[:, :256], wk[...], 1, 1) + dg(dkv_own[:, 256:], wv[...], 1, 1)
        hat, inv = norm(flat(lat_ref[...]).astype(f32))
        vec[6] += row_sum(d * hat)
        vec[7] += row_sum(d)
        got = norm_back(d, line_of(R.gain_latent), hat, inv)
        for k, c in enumerate(put_gl):
            ds_scr[1024 + k * rows * lats : 1024 + (k + 1) * rows * lats, :] = got[:, 256 * k : 256 * (k + 1)].astype(bf16)
            c.start()

    G = [Gather(pc, kv, pl.ds(g * pair, pair), R.ag_s.at[g], R.ag_r.at[g]) for g in range(n_pairs)]

    def job(k, ref, lo, c0, height, out):
        block = height // 8

        def part(t):
            return ref.at[pl.ds(pl.multiple_of(lo + t * block, 32), block), pl.ds(c0, 256)]

        sc = R.sc[k]
        ln = Line(pc, sc["l0"].at[pc.yb, pc.xb], kind=bf16, **R.li[k])
        return Job(Scatter(pc, part, 256, **sc), ln, out, R.t_sem.at[k])

    D = [job(j, R.g_down, 0, 256 * j, width, R.t_down.at[:, cols_at(j)]) for j in range(3)]
    U = [job(3 + j, act_s, 0, 256 * j, width, R.t_up.at[:, cols_at(j)]) for j in range(3)]
    O = [job(6 + j, hn_s, 0, 256 * j, width, R.t_out.at[:, cols_at(j)]) for j in range(3)]
    Q = job(9, R.g_q, 0, 0, width, R.t_q)
    K = [job(10 + j, p_s, j * lwidth, 0, lwidth, R.t_kv.at[j]) for j in range(4)]

    def keys_values(g):
        def part(t):
            return kv.at[pl.ds(g * pair, pair), pl.ds(pl.multiple_of(t * lats, lats), lats), :]

        sc = R.scd[g]

        def keep():
            dkv_own[pl.ds(g * pair * lats, pair * lats), :] = flat(sc["l0"][pc.yb, pc.xb])

        return Scatter(pc, part, 1024, then=keep, **sc)

    DKV = [keys_values(g) for g in range(n_pairs)]
    lv = Line(pc, R.vtot.at[3], kind=f32, **R.ln_vec)
    V = Vectors(pc, vec, R.vtot, R.vland, R.vs, R.vr, lv)

    vec[...] = jnp.zeros_like(vec)
    lid = R.latent_ids[...].astype(f32)
    lidT[...] = jnp.concatenate([lid, jnp.zeros((128 - rows, lid.shape[1]), f32)], axis=0).T
    loads["lat"].wait()
    loads["wk"].wait()
    loads["wv"].wait()
    l0(0)
    pc.met()
    G[0].p0()
    loads["q"].wait()
    loads["wq"].wait()
    f1(0)
    l0(1)
    G[1].p0()
    f1(1)
    f1(2)
    l0(2)
    G[0].p1()
    G[2].p0()
    loads["c"].wait()
    loads["wd"].wait()
    f1b(0)
    f1b(1)
    f1b(2)
    G[1].p1()
    G[0].p2()
    G[0].p3()
    loads["wo"].wait()
    loads["wu"].wait()
    hooks = {
        0: {
            2: (DKV[0].p3,),
        },
        1: {
            0: (G[2].p1,),
            1: (DKV[0].p1,),
            2: (DKV[1].p1,),
        },
        2: {
            0: (G[1].p2,),
        },
        3: {
            0: (G[2].p2, G[1].p3, G[0].drain,),
            1: (DKV[0].p2, G[1].drain,),
            2: (DKV[1].p2, G[2].drain,),
        },
        4: {
            0: (G[2].p3,),
        },
        5: {
            0: (DKV[0].p0,),
            1: (DKV[1].p0,),
            2: (DKV[2].p0,),
        },
    }

    def hook(k, i):
        for p, fns in hooks.get(k, {}).items():

            @pl.when(i == p)
            def _():
                for fn in fns:
                    fn()

    def main(i):
        f2(pair * i)
        hook(0, i)
        f2(pair * i + 1)
        hook(1, i)
        f3(i, lambda: hook(2, i))
        hook(3, i)
        b2(pair * i)
        hook(4, i)
        b2(pair * i + 1)
        hook(5, i)

    loop(0, n_pairs, main)
    w_down(0)
    DKV[1].p3()
    D[0].p0()
    w_down(1)
    DKV[2].p1()
    D[0].p1()
    D[1].p0()
    w_down(2)
    D[2].p0()
    w_up(0)
    D[1].p1()
    U[0].p0()
    D[2].p1()
    w_up(1)
    U[0].p1()
    U[1].p0()
    w_up(2)
    DKV[2].p2()
    U[1].p1()
    U[2].p0()
    w_out(0)
    D[0].p2()
    O[0].p0()
    D[1].p2()
    U[2].p1()
    D[2].p2()
    O[0].p1()
    U[0].p2()
    DKV[2].p3()
    loop(0, 5, w_kv)
    U[1].p2()
    D[0].p3()
    K[0].p0()
    K[1].p0()
    K[2].p0()
    K[3].p0()
    D[1].p3()
    l1()
    U[2].p2()
    K[0].p1()
    D[2].p3()
    K[1].p1()
    b3(0)
    K[2].p1()
    O[0].p2()
    D[0].up()
    U[0].p3()
    K[3].p1()
    U[1].p3()
    b3(1)
    D[1].up()
    U[2].p3()
    b3(2)
    D[2].up()
    b3(3)
    K[0].p2()
    D[0].mid()
    U[0].up()
    b3(4)
    K[1].p2()
    U[1].up()
    D[1].mid()
    b3(5)
    U[2].up()
    D[2].mid()
    V.p0()
    w_q()
    K[2].p2()
    O[0].p3()
    D[0].dn()
    V.p1()
    U[0].mid()
    U[1].mid()
    D[1].dn()
    K[3].p2()
    Q.p0()
    w_out(1)
    U[2].mid()
    K[0].p3()
    D[2].dn()
    O[1].p0()
    Q.p1()
    K[1].p3()
    w_out(2)
    K[2].p3()
    O[1].p1()
    O[0].up()
    U[0].dn()
    O[2].p0()
    V.p2()
    U[1].dn()
    K[3].p3()
    O[2].p1()
    U[2].dn()
    K[0].up()
    Q.p2()
    O[1].p2()
    O[0].mid()
    K[1].up()
    V.p3()
    O[2].p2()
    K[2].up()
    Q.p3()
    O[1].p3()
    K[0].mid()
    O[0].dn()
    K[3].up()
    K[1].mid()
    O[2].p3()
    V.up()
    Q.up()
    K[2].mid()
    O[1].up()
    K[0].dn()
    K[3].mid()
    O[2].up()
    K[1].dn()
    V.mid()
    Q.mid()
    K[2].dn()
    O[1].mid()
    O[2].mid()
    K[3].dn()
    V.dn()
    Q.dn()
    O[1].dn()
    O[2].dn()
    jobs = [*D, *U, *O, Q, *K]
    for x in jobs:
        x.store()
    t_vec = pltpu.make_async_copy(lv.zo, R.t_vec, R.t_sem.at[len(jobs)])
    lv.result(lambda src: pltpu.make_async_copy(src, R.t_vec, R.t_sem.at[len(jobs)]).start())
    for x in (*jobs, *DKV, V):
        x.drain()
    t_vec.wait()
    staged(R.grad_queries, R.gq_sem, rows - 1, positions)
    for c in put_gl:
        c.wait()


def unpack(*refs):
    n = len(Outs._fields)
    ins, out = refs[:9], Outs(*refs[9 : 9 + n])
    stay, wide, narrow = refs[9 + n : 18 + n], refs[18 + n : -3], refs[-3]
    sem_in, sem_out = refs[-2], refs[-1]
    loads = [pltpu.make_async_copy(a, b, sem_in.at[k]) for k, (a, b) in enumerate(zip(ins, stay))]
    for c in loads:
        c.start()
    t_vec = stay[8]
    outs = (
        out.block_out,
        out.grad_queries,
        out.grad_latents,
        out.grad_down_weight,
        out.grad_up_weight,
        out.grad_out_weight,
        out.grad_query_weight,
        out.grad_key_weight,
        out.grad_value_weight,
    )
    stores = [pltpu.make_async_copy(stay[0], out.block_out, sem_out.at[0])]
    stores += [pltpu.make_async_copy(v, outs[k + 1], sem_out.at[k + 1]) for k, v in enumerate(wide)]
    loads[1].wait()
    half = wide[0].shape[0] // 2
    halves = []
    for j in range(2):
        rs = pl.ds(j * half, half)
        wide[0][rs] = stay[1][rs].astype(f32)
        halves.append(pltpu.make_async_copy(wide[0].at[rs], out.grad_queries.at[rs], narrow.at[j]))
        halves[-1].start()
    stores = stores[:1] + stores[2:]
    loads[0].wait()
    stores[0].start()
    for k in range(1, 6):
        loads[k + 1].wait()
        wide[k][...] = stay[k + 1][...].astype(f32)
        stores[k].start()
    loads[7].wait()
    wide[6][...] = stay[7][0].astype(f32)
    stores[6].start()
    for k in range(3):
        wide[7][:, 256 * k : 256 * (k + 1)] = stay[7][k + 1].astype(f32)
    stores[7].start()
    loads[8].wait()
    vectors = (
        out.grad_gain_query,
        out.grad_shift_query,
        out.grad_gain_hidden,
        out.grad_shift_hidden,
        out.grad_bias_up,
        out.grad_bias_down,
        out.grad_gain_latent,
        out.grad_shift_latent,
    )
    for t in range(8):

        @pl.when(lax.axis_index("seq") == t)
        def _():
            for k, ref in enumerate(vectors):
                m = ref.shape[0]
                ref[...] = t_vec[k, m * t : m * (t + 1)]

    for c in stores + halves:
        c.wait()


class Args(NamedTuple):
    queries: Any
    latents: Any
    query_ids: Any
    latent_ids: Any
    query_weight: Any
    key_weight: Any
    value_weight: Any
    out_weight: Any
    up_weight: Any
    down_weight: Any
    gain_query: Any
    shift_query: Any
    gain_latent: Any
    shift_latent: Any
    gain_hidden: Any
    shift_hidden: Any
    bias_up: Any
    bias_down: Any
    cotangent: Any


class Outs(NamedTuple):
    block_out: Any
    grad_queries: Any
    grad_latents: Any
    grad_query_weight: Any
    grad_key_weight: Any
    grad_value_weight: Any
    grad_out_weight: Any
    grad_up_weight: Any
    grad_down_weight: Any
    grad_gain_query: Any
    grad_shift_query: Any
    grad_gain_latent: Any
    grad_shift_latent: Any
    grad_gain_hidden: Any
    grad_shift_hidden: Any
    grad_bias_up: Any
    grad_bias_down: Any


def body(n_rows, n_seq, *args):
    A = Args(*args)
    rows, pos, width = A.queries.shape
    lats, lwidth = A.latents.shape[1:]
    nl = lats * n_seq
    F_ = lambda *s: jax.ShapeDtypeStruct(s, f32)
    wide, vec, lvec = F_(width // n_seq, width), F_(width // n_seq), F_(lwidth // n_seq)
    out = Outs(
        block_out=jax.ShapeDtypeStruct((rows, pos, width), bf16),
        grad_queries=F_(rows, pos, width),
        grad_latents=F_(rows, lats, lwidth),
        grad_query_weight=F_(width // n_seq, 256),
        grad_key_weight=F_(lwidth // n_seq, 256),
        grad_value_weight=F_(lwidth // n_seq, width),
        grad_out_weight=wide,
        grad_up_weight=wide,
        grad_down_weight=wide,
        grad_gain_query=vec,
        grad_shift_query=vec,
        grad_gain_latent=lvec,
        grad_shift_latent=lvec,
        grad_gain_hidden=vec,
        grad_shift_hidden=vec,
        grad_bias_up=vec,
        grad_bias_down=vec,
    )
    V = lambda *s: pltpu.VMEM(s, bf16)
    F = lambda *s: pltpu.VMEM(s, f32)
    dma = lambda *s: pltpu.SemaphoreType.DMA(s)
    tok = V(rows, pos, width)
    tok2 = V(rows * pos, width)
    tokT = V(width, rows * pos)
    scratch = dict(
        q_v=tok,
        c_v=tok,
        lat_v=V(rows, lats, lwidth),
        wq_v=V(width, 256),
        wk_v=V(lwidth, 256),
        wv_v=V(lwidth, width),
        wo_v=V(width, width),
        wu_v=V(width, width),
        wd_v=V(width, width),
        kv=V(rows, nl, 1024),
        qn=tok2,
        qp=V(rows * pos, 256),
        s_scr=F(HEADS, nl, pos),
        ds_scr=V(HEADS * nl, pos),
        inv=F(rows, HEADS, pos),
        p=V(rows * HEADS * nl, pos),
        mix=tokT,
        hn=tok2,
        act=tok2,
        dpre=tok2,
        dres=tok2,
        dm=tokT,
        dq=V(rows * pos, 256),
        lidT=F(nl, 128),
        ln=V(rows * lats, lwidth),
        dkv_own=V(rows * lats, 1024),
        vec=F(8, 8, lwidth),
        vtot=F(4, 8, lwidth),
        vland=F(3, 8, lwidth),
        vs=dma(3),
        vr=dma(3),
        bo_sem=dma(width // 256),
        gq_sem=dma(width // 256),
        gl_sem=dma(lwidth // 256),
        t_sem=dma(15),
        load_sem=dma(9),
        ag_s=dma(rows // 2, 9),
        ag_r=dma(rows // 2, 9),
        g_down=V(width, width),
        g_q=V(width, 256),
        ln_vec=line_scratch((8, lwidth), f32),
    )
    lead, llead = (width // n_seq,), (lwidth // n_seq,)
    shapes = [lead] * 10 + [llead] * 4
    scratch["sc"] = [scatter_scratch(x, 256) for x in shapes]
    scratch["li"] = [line_scratch((*x, 256), bf16) for x in shapes]
    scratch["scd"] = [scatter_scratch((2, lats), 1024) for _ in range(rows // 2)]
    any_ = pl.BlockSpec(memory_space=pl.ANY)
    vm = pl.BlockSpec(memory_space=pltpu.VMEM)
    far = (A.queries, A.cotangent, A.latents, *A[4:10])
    in_specs = [any_ if any(a is f for f in far) else vm for a in A]
    sds = jax.ShapeDtypeStruct
    mid = dict(
        block_out=sds((rows * pos, width), bf16),
        grad_queries=sds((rows * pos, width), bf16),
        grad_latents=sds((rows * lats, lwidth), bf16),
        t_down=sds(wide.shape, bf16),
        t_up=sds(wide.shape, bf16),
        t_out=sds(wide.shape, bf16),
        t_q=sds((width // n_seq, 256), bf16),
        t_kv=sds((4, lwidth // n_seq, 256), bf16),
        t_vec=sds((8, lwidth), f32),
    )
    names = (*Args._fields, *mid, *scratch)
    flops = 2 * rows * pos * width * width * 14
    got = pl.pallas_call(
        functools.partial(kernel, n_rows, names),
        out_shape=tuple(mid.values()),
        in_specs=in_specs,
        out_specs=(any_,) * len(mid),
        scratch_shapes=list(scratch.values()),
        compiler_params=pltpu.CompilerParams(
            collective_id=0, has_side_effects=True, vmem_limit_bytes=64 << 20
        ),
        cost_estimate=pl.CostEstimate(flops=flops, bytes_accessed=24 << 20, transcendentals=0),
    )(*A)
    three = lambda x: x.reshape(rows, -1, x.shape[-1])
    got = (three(got[0]), three(got[1]), three(got[2]), *got[3:])
    return pl.pallas_call(
        unpack,
        out_shape=tuple(out),
        in_specs=[any_] * 9,
        out_specs=(any_,) * 9 + (vm,) * 8,
        scratch_shapes=[pltpu.VMEM(x.shape, x.dtype) for x in got]
        + [
            pltpu.VMEM(o.shape, f32)
            for o in (
                out.grad_queries,
                out.grad_latents,
                wide,
                wide,
                wide,
                out.grad_query_weight,
                out.grad_key_weight,
                out.grad_value_weight,
            )
        ]
        + [dma(2), dma(9), dma(9)],
        compiler_params=pltpu.CompilerParams(vmem_limit_bytes=64 << 20),
        cost_estimate=pl.CostEstimate(flops=0, bytes_accessed=18 << 20, transcendentals=0),
    )(*got)


def solution(mesh):
    seq = P("rows", "seq", None)
    rep = P()
    in_specs = (seq, seq, P("rows", "seq"), P("rows", None)) + (rep,) * 14 + (seq,)
    out_specs = (seq,) * 3 + (P("seq", None),) * 6 + (P("seq"),) * 8
    return jax.shard_map(
        functools.partial(body, mesh.shape["rows"], mesh.shape["seq"]),
        mesh=mesh,
        in_specs=in_specs,
        out_specs=out_specs,
        check_vma=False,
    )
```

```python
import functools
import types
from typing import Any, NamedTuple

import jax
import jax.numpy as jnp
from jax import lax
from jax.experimental import pallas as pl
from jax.experimental.pallas import tpu as pltpu
from jax.sharding import PartitionSpec as P

HEADS = 8
HDIM = 96
QKDIM = 32
EPS = 1e-05
SCALE = QKDIM ** (-0.5)
MESH = pl.DeviceIdType.MESH
f32, bf16 = jnp.float32, jnp.bfloat16


def dg(a, b, ca, cb):
    return lax.dot_general(a, b, (((ca,), (cb,)), ((), ())), preferred_element_type=f32)


def norm(x):
    mean = jnp.mean(x, -1, keepdims=True)
    cen = x - mean
    inv = lax.rsqrt(jnp.mean(cen * cen, -1, keepdims=True) + EPS)
    return cen * inv, inv


def norm_back(grad, gain, hat, inv):
    g = grad * gain
    return inv * (
        g - jnp.mean(g, -1, keepdims=True) - hat * jnp.mean(g * hat, -1, keepdims=True)
    )


def row_sum(x):
    n, w = x.shape
    return jnp.sum(x.reshape(n // 8, 8, w), axis=0)


def flat(x):
    return x.reshape(-1, x.shape[-1])


def add(a, b):
    return (a.astype(f32) + b.astype(f32)).astype(bf16)


class Place:
    def __init__(self, n_rows):
        self.n = n_rows
        self.s = lax.axis_index("seq")
        self.r = lax.axis_index("rows")
        self.core = lax.rem(self.s, 2)
        self.chip = self.s // 2
        self.xc = self.chip + 1 - 2 * lax.rem(self.chip, 2)
        self.yc = lax.rem(self.chip + 2, 4)
        self.dc = lax.rem(self.xc + 2, 4)
        self.xb, self.yb = lax.rem(self.chip, 2), self.chip // 2
        self.sib = (self.s + 1 - 2 * self.core, self.r)
        self.xn = (2 * self.xc + self.core, self.r)
        self.yn = (2 * self.yc + self.core, self.r)
        half = n_rows // 2
        self.left = self.r < half
        self.mid = (self.r == half - 1) | (self.r == half)
        self.not_end = (self.r != 0) & (self.r != n_rows - 1)
        step = jnp.where(self.left, 1, -1)
        self.inner = (self.s, lax.rem(self.r + step + n_rows, n_rows))
        self.outer = (self.s, lax.rem(self.r - step + n_rows, n_rows))

        self.dn = (2 * self.dc + self.core, self.r)
        hops = range(1, n_rows) if n_rows <= 4 else (1, n_rows - 1)
        self.line = [(self.s, lax.rem(self.r + k, n_rows)) for k in hops]

    def greet(self):
        self.bar = pltpu.get_barrier_semaphore()
        self.peers = [self.sib, self.xn, self.yn, self.dn, *self.line]
        for peer in self.peers:
            pl.semaphore_signal(self.bar, inc=1, device_id=peer, device_id_type=MESH)

    def met(self):
        pl.semaphore_wait(self.bar, len(self.peers))


def rcopy(src, dst, ssem, rsem, peer):
    return pltpu.make_async_remote_copy(
        src_ref=src, dst_ref=dst, send_sem=ssem, recv_sem=rsem, device_id=peer, device_id_type=MESH
    )


class Line:
    def __init__(self, pc, src, zo, zi, ssem, rsem, kind):
        zt = zo
        self.pc, self.src, self.zo, self.zi, self.zt, self.kind = pc, src, zo, zi, zt, kind
        self.up_c = rcopy(src, zo, ssem.at[0], rsem.at[0], pc.inner)
        self.cross_c = rcopy(src, zi, ssem.at[1], rsem.at[1], pc.inner)
        self.down_mid = rcopy(zt, zi, ssem.at[2], rsem.at[1], pc.outer)
        self.down_far = rcopy(zi, zi, ssem.at[2], rsem.at[1], pc.outer)

    def plus(self, a, b):
        return (a.astype(f32) + b.astype(f32)).astype(self.kind)

    def send(self):
        pc = self.pc
        pl.when(jnp.logical_not(pc.not_end) & jnp.logical_not(pc.mid))(self.up_c.start)

    def up(self):
        pc = self.pc

        @pl.when(pc.not_end)
        def _():
            self.up_c.wait_recv()
            self.src[...] = self.plus(self.src[...], self.zo[...])

        pl.when(pc.mid)(self.cross_c.start)
        pl.when(jnp.logical_not(pc.mid) & pc.not_end)(self.up_c.start)

    def middle(self):
        pc = self.pc

        @pl.when(pc.mid)
        def _():
            self.cross_c.wait_recv()
            self.zt[...] = self.plus(self.src[...], self.zi[...])

        pl.when(pc.mid & pc.not_end)(self.down_mid.start)

    def down(self):
        pc = self.pc
        pl.when(jnp.logical_not(pc.mid))(self.cross_c.wait_recv)
        pl.when(jnp.logical_not(pc.mid) & pc.not_end)(self.down_far.start)

    def result(self, write):
        pc = self.pc
        pl.when(pc.mid)(lambda: write(self.zt))
        pl.when(jnp.logical_not(pc.mid))(lambda: write(self.zi))

    def drain(self):
        pc = self.pc
        pl.when(pc.mid)(self.cross_c.wait_send)
        pl.when(jnp.logical_not(pc.mid))(self.up_c.wait_send)
        pl.when(pc.mid & pc.not_end)(self.down_mid.wait_send)
        pl.when(jnp.logical_not(pc.mid) & pc.not_end)(self.down_far.wait_send)


class Scatter:
    def __init__(self, pc, part, width, l0, la, lb, la2, lb2, ssem, rsem, then=None):
        self.pc, self.part, self.l0, self.then = pc, part, l0, then
        self.la, self.lb, self.la2, self.lb2 = la, lb, la2, lb2
        h = width // 2
        A, B = self.A, self.B = pl.ds(0, h), pl.ds(h, h)
        lead = (slice(None),) * (len(l0.shape) - 3)
        xb, yb = pc.xb, pc.yb

        def blk(y, x, cols):
            return l0.at[(y, x, *lead, cols)]

        self.blk = blk
        other = 1 - pc.core
        self.pair = [
            rcopy(part(2 * q + other), l0.at[q // 2, q % 2], ssem.at[q], rsem.at[q], pc.sib)
            for q in range(4)
        ]
        every = slice(None)
        self.first = [
            rcopy(blk(every, 1 - xb, A), la, ssem.at[4], rsem.at[4], pc.xn),
            rcopy(blk(1 - yb, every, B), lb, ssem.at[5], rsem.at[5], pc.yn),
        ]
        self.second = [
            rcopy(blk(1 - yb, xb, A), la2, ssem.at[6], rsem.at[6], pc.yn),
            rcopy(blk(yb, 1 - xb, B), lb2, ssem.at[7], rsem.at[7], pc.xn),
        ]

    def p0(self):
        for c in self.pair:
            c.start()

    def p1(self):
        for q in range(4):
            self.pair[q].wait_recv()
            own = self.part(2 * q + self.pc.core)[...]
            self.l0[q // 2, q % 2] = add(self.l0[q // 2, q % 2], own)
        for c in self.first:
            c.start()

    def into(self, y, x, cols, got):
        v = self.blk(y, x, cols)
        v[...] = add(v[...], got[...])

    def p2(self):
        xb, yb = self.pc.xb, self.pc.yb
        self.first[0].wait_recv()
        self.into(1 - yb, xb, self.A, self.la.at[1 - yb])
        self.second[0].start()
        self.first[1].wait_recv()
        self.into(yb, 1 - xb, self.B, self.lb.at[1 - xb])
        self.second[1].start()
        self.into(yb, xb, self.A, self.la.at[yb])
        self.into(yb, xb, self.B, self.lb.at[xb])

    def p3(self):
        for c, cols, got in zip(self.second, (self.A, self.B), (self.la2, self.lb2)):
            c.wait_recv()
            self.into(self.pc.yb, self.pc.xb, cols, got)
        self.then()

    def drain(self):
        for c in self.pair + self.first + self.second:
            c.wait_send()


class Job:
    def __init__(self, scatter, line, out, sem):
        self.scatter, self.line = scatter, line
        scatter.then = line.send
        self.p0, self.p1, self.p2, self.p3 = scatter.p0, scatter.p1, scatter.p2, scatter.p3
        self.up, self.mid, self.dn = line.up, line.middle, line.down
        self.out, self.sem = out, sem

    def store(self):
        self.line.result(lambda src: pltpu.make_async_copy(src, self.out, self.sem).start())

    def drain(self):
        pltpu.make_async_copy(self.line.zo, self.out, self.sem).wait()
        self.scatter.drain()
        self.line.drain()


class Vectors:
    def __init__(self, pc, vec, pair, chips, rows, ssem, rsem, line):
        self.pc, self.vec, self.pair, self.chips, self.rows, self.line = pc, vec, pair, chips, rows, line
        self.swap = rcopy(pair.at[0], pair.at[1], ssem.at[0], rsem.at[0], pc.sib)
        mine = chips.at[pc.chip]
        self.around = [
            rcopy(mine, mine, ssem.at[k + 1], rsem.at[k + 1], peer)
            for k, peer in enumerate((pc.xn, pc.yn, pc.dn))
        ]
        self.along = []
        if line is None:
            mine = rows.at[pc.r]
            self.along = [
                rcopy(mine, mine, ssem.at[k + 4], rsem.at[k + 4], peer)
                for k, peer in enumerate(pc.line)
            ]

    def p0(self):
        self.pair[0] = jnp.sum(self.vec[...], axis=1)
        self.swap.start()

    def p1(self):
        self.swap.wait_recv()
        self.swap.wait_send()
        self.chips[self.pc.chip] = self.pair[0] + self.pair[1]
        for c in self.around:
            c.start()

    def p2(self):
        for c in self.around:
            c.wait_recv()
        at = self.pc.r if self.line is None else 0
        self.rows[at] = jnp.sum(self.chips[...], axis=0)
        for c in self.along:
            c.start()
        if self.line is not None:
            self.line.send()

    def p3(self):
        for c in self.along:
            c.wait_recv()
        if self.line is None:
            self.pair[0] = jnp.sum(self.rows[...], axis=0)
        else:
            self.line.up()
            self.line.middle()
            self.line.down()

    def store(self, out, sem):
        def write(src):
            pltpu.make_async_copy(src, out, sem).start()

        if self.line is None:
            write(self.pair.at[0])
        else:
            self.line.result(write)

    def drain(self):
        for c in (*self.around, *self.along):
            c.wait_send()
        if self.line is not None:
            self.line.drain()


def scatter_scratch(lead, width):
    half = width // 2
    return dict(
        l0=pltpu.VMEM((2, 2, *lead, width), bf16),
        la=pltpu.VMEM((2, *lead, half), bf16),
        lb=pltpu.VMEM((2, *lead, half), bf16),
        la2=pltpu.VMEM((*lead, half), bf16),
        lb2=pltpu.VMEM((*lead, half), bf16),
        ssem=pltpu.SemaphoreType.DMA((8,)),
        rsem=pltpu.SemaphoreType.DMA((8,)),
    )


def line_scratch(shape, kind):
    return dict(
        zo=pltpu.VMEM(shape, kind),
        zi=pltpu.VMEM(shape, kind),
        ssem=pltpu.SemaphoreType.DMA((3,)),
        rsem=pltpu.SemaphoreType.DMA((2,)),
    )


class Gather:
    def __init__(self, pc, kv, rows, ssem, rsem):
        def blk(t, cols=slice(None)):
            return kv.at[rows, pl.ds(pl.multiple_of(t * 32, 32), 32), cols]

        h = kv.shape[-1] // 2
        A, B = pl.ds(0, h), pl.ds(h, h)
        ds_ = 2 * pc.dc + pc.core

        def copy(k, ref, peer):
            return rcopy(ref, ref, ssem.at[k], rsem.at[k], peer)

        self.own = [copy(0, blk(pc.s), pc.sib), copy(1, blk(pc.s), pc.xn), copy(2, blk(pc.s), pc.yn)]
        self.from_x = [copy(3, blk(pc.xn[0], A), pc.yn), copy(4, blk(pc.xn[0]), pc.sib)]
        self.from_y = [copy(5, blk(pc.yn[0], B), pc.xn), copy(6, blk(pc.yn[0]), pc.sib)]
        self.from_d = [copy(7, blk(ds_, A), pc.sib), copy(8, blk(ds_, B), pc.sib)]

    def p0(self):
        for c in self.own[::-1]:
            c.start()

    def p1(self):
        self.own[1].wait_recv()
        for c in self.from_x:
            c.start()
        self.own[2].wait_recv()
        for c in self.from_y:
            c.start()

    def p2(self):
        self.from_x[0].wait_recv()
        self.from_d[0].start()
        self.from_y[0].wait_recv()
        self.from_d[1].start()

    def p3(self):
        for c in (self.own[0], self.from_x[1], self.from_y[1], *self.from_d):
            c.wait_recv()

    def drain(self):
        for c in self.own + self.from_x + self.from_y + self.from_d:
            c.wait_send()


def kernel(n_rows, names, *refs):
    R = types.SimpleNamespace(**dict(zip(names, refs, strict=True)))
    q_hbm, c_hbm, lat_hbm = R.queries, R.cotangent, R.latents
    line_of = lambda ref: ref[...].reshape(1, -1)
    q_ref, c_ref, lat_ref = R.q_v, R.c_v, R.lat_v
    wq, wk, wv, wo, wu, wd = R.wq_v, R.wk_v, R.wv_v, R.wo_v, R.wu_v, R.wd_v
    kv, qn_s, qp_s, p_s, mix_s, hn_s = R.kv, R.qn, R.qp, R.p, R.mix, R.hn
    act_s, dpre_s, dres_s, dm_s, dq_s = R.act, R.dpre, R.dres, R.dm, R.qp
    s_scr, ds_scr, inv_s = R.s_scr, R.ds_scr, R.inv
    lidT, ln_s, ln2, dkv_own, vec = R.lidT, R.ln, R.ln2, R.dkv_own, R.vec
    rows, positions, width = q_ref.shape
    lats, lwidth = lat_ref.shape[1:]
    pair = 2
    n_pairs = rows // pair
    tokens = rows * positions
    span = positions * pair

    loads = {}
    for k, (name, src, dst) in enumerate(
        [
            ("lat", lat_hbm, lat_ref),
            ("wk", R.key_weight, wk),
            ("wv", R.value_weight, wv),
            ("q", q_hbm, q_ref),
            ("wq", R.query_weight, wq),
            ("wo", R.out_weight, wo),
            ("wu", R.up_weight, wu),
            ("wd", R.down_weight, wd),
            ("c", c_hbm, c_ref),
        ]
    ):
        loads[name] = pltpu.make_async_copy(src, dst, R.load_sem.at[k])
        if k < 3:
            loads[name].start()

    pc = Place(n_rows)
    pc.greet()

    def loop(first, last, body):
        def step(i, carry):
            body(i)
            return carry

        lax.fori_loop(first, last, step, 0)

    lane1 = lax.broadcasted_iota(jnp.int32, (1, 128), 1)

    def head_mask(hh, kind):
        return ((lane1 >= QKDIM * hh) & (lane1 < QKDIM * (hh + 1))).astype(kind)

    own = pl.ds(pl.multiple_of(pc.s * lats, lats), lats)

    def l0():
        hat, _ = norm(flat(lat_ref[...]).astype(f32))
        ln = (hat * line_of(R.gain_latent) + line_of(R.shift_latent)).astype(bf16)
        ln_s[...] = ln
        ln2[:, own, :] = ln[(rows - pair) * lats :].reshape(pair, lats, lwidth)
        k = dg(ln, wk[...], 1, 0).astype(bf16)
        v = dg(ln, wv[...], 1, 0).astype(bf16)
        kv[:, own, 0:256] = k.reshape(rows, lats, -1)
        kv[:, own, 256:1024] = v.reshape(rows, lats, -1)

    def at(i):
        return pl.ds(pl.multiple_of(i * span, span), span)

    def row(r):
        return pl.ds(pl.multiple_of(r * positions, positions), positions)

    def f1(i):
        hat, _ = norm(flat(q_ref[pl.ds(i * pair, pair)]).astype(f32))
        qn = (hat * line_of(R.gain_query) + line_of(R.shift_query)).astype(bf16)
        qn_s[at(i), :] = qn
        qp_s[at(i), :] = (dg(qn, wq[...], 1, 0) * SCALE).astype(bf16)

    def f1b(i):
        c = flat(c_ref[pl.ds(i * pair, pair)])
        vec[5, :, :width] += row_sum(c.astype(f32))
        dpre_s[at(i), :] = dg(c, wd[...], 1, 1).astype(bf16)

    def row8(r):
        return pl.ds(pl.multiple_of(r * HEADS * 256, HEADS * 256), HEADS * 256)

    def f2(r):
        k = kv[r, :, :256]
        vT = kv[r, :, 256:].T
        lane = lax.broadcasted_iota(jnp.int32, (256, 128), 1)
        col = jnp.sum(jnp.where(lane == r, lidT[...], 0.0), axis=1, keepdims=True)
        allowed = col == R.query_ids[pl.ds(r, 1), :].astype(f32)
        for g in range(2):
            kb = k[:, 128 * g : 128 * g + 128]
            km = jnp.concatenate([kb * head_mask(hh, bf16) for hh in range(4)], axis=0)
            sg = dg(km, qp_s[row(r), 128 * g : 128 * g + 128], 1, 1)
            for hh in range(4):
                s_scr[4 * g + hh] = sg[256 * hh : 256 * (hh + 1)]
        p_r = p_s.at[row8(r)]
        for h in range(HEADS):
            s = jnp.where(allowed, s_scr[h], -1e30)
            e = jnp.exp(s - jnp.max(s, axis=0, keepdims=True))
            p_r[256 * h : 256 * (h + 1), :] = e.astype(bf16)
            inv_s[r, h : h + 1, :] = 1.0 / jnp.sum(e, axis=0, keepdims=True)
        mix_r = mix_s.at[:, row(r)]
        for h in range(HEADS):
            hs = slice(HDIM * h, HDIM * (h + 1))
            got = dg(vT[hs], p_r[256 * h : 256 * (h + 1), :], 1, 0)
            mix_r[hs, :] = (got * inv_s[r, h : h + 1, :]).astype(bf16)

    def by_rows(k, n):
        return ds_scr.at[pl.ds(k * n, n)]

    def by_columns(k, n):
        return dm_s.at[pl.ds(0, n), pl.ds(256 * k, 256)]

    def chunks(area, dst, sems, i, n):
        return [
            pltpu.make_async_copy(
                area(k, n),
                dst.at[pl.ds(pl.multiple_of(i * n, n), n), pl.ds(256 * k, 256)],
                sems.at[k],
            )
            for k in range(width // 256)
        ]

    def stage(value, area, dst, sems, i, n):
        for k, c in enumerate(chunks(area, dst, sems, i, n)):
            area(k, n)[...] = value[:, 256 * k : 256 * (k + 1)].astype(bf16)
            c.start()

    def staged(area, dst, sems, i, n):
        for c in chunks(area, dst, sems, i, n):
            c.wait()

    def f3(i):
        rs = pl.ds(i * pair, pair)
        resid = flat(q_ref[rs]).astype(f32) + dg(mix_s[:, at(i)], wo[...], 0, 0)
        hat, inv = norm(resid)
        hn = (hat * line_of(R.gain_hidden) + line_of(R.shift_hidden)).astype(bf16)
        hn_s[at(i), :] = hn
        pre = dg(hn, wu[...], 1, 0) + line_of(R.bias_up)
        phi = 0.5 * (1.0 + lax.erf(pre * (0.5**0.5)))
        act = (pre * phi).astype(bf16)
        act_s[at(i), :] = act
        slope = phi + pre * (jnp.exp(-0.5 * pre * pre) * 0.3989422804014327)
        dpre = (dpre_s[at(i), :].astype(f32) * slope).astype(bf16)
        dpre_s[at(i), :] = dpre

        vec[4, :, :width] += row_sum(dpre.astype(f32))
        dh = dg(dpre, wu[...], 1, 1)
        vec[2, :, :width] += row_sum(dh * hat)
        vec[3, :, :width] += row_sum(dh)
        cf = flat(c_ref[rs]).astype(f32)
        dlow = (norm_back(dh, line_of(R.gain_hidden), hat, inv) + cf).astype(bf16)
        dres_s[at(i), :] = dlow
        dm_s[:, at(i)] = dg(wo[...], dlow, 1, 1).astype(bf16)

    def bo(i):
        resid = flat(q_ref[pl.ds(i * pair, pair)]).astype(f32) + dg(mix_s[:, at(i)], wo[...], 0, 0)
        out = resid + dg(act_s[at(i), :], wd[...], 1, 0) + line_of(R.bias_down)
        if i >= 1:
            staged(by_columns, R.block_out, R.bo_sem, i - 1, span)
        stage(out, by_columns, R.block_out, R.bo_sem, i, span)

    def b2(r):
        k = kv[r, :, :256]
        kT = k.T
        v = kv[r, :, 256:]
        dvs, dqs, dks = [], [], []
        p_r, dm_r, qp_r = p_s.at[row8(r)], dm_s.at[:, row(r)], qp_s.at[row(r)]
        for h in range(HEADS):
            hs = slice(HDIM * h, HDIM * (h + 1))
            dm_r[hs, :] = (dm_r[hs, :].astype(f32) * inv_s[r, h : h + 1, :]).astype(bf16)
        for h in range(HEADS):
            hs = slice(HDIM * h, HDIM * (h + 1))
            s_scr[h] = dg(v[:, hs], dm_r[hs, :], 1, 0)
        for h in range(HEADS):
            hs = slice(HDIM * h, HDIM * (h + 1))
            dvs.append(dg(dm_r[hs, :], p_r[256 * h : 256 * (h + 1), :], 1, 1).astype(bf16))
        for h in range(HEADS):
            e = p_r[256 * h : 256 * (h + 1), :].astype(f32)
            ed = e * s_scr[h]
            ds = ed - e * (jnp.sum(ed, axis=0, keepdims=True) * inv_s[r, h : h + 1, :])
            ds_scr[256 * h : 256 * (h + 1), :] = ds.astype(bf16)
        for g in range(2):
            t = dg(ds_scr[1024 * g : 1024 * (g + 1), :], qp_r[:, 128 * g : 128 * g + 128], 1, 0)
            dks.append(sum(t[256 * hh : 256 * (hh + 1)] * head_mask(hh, f32) for hh in range(4)))
        for h in range(HEADS):
            kh = kT[QKDIM * h : QKDIM * (h + 1)]
            dqs.append(dg(kh, ds_scr[256 * h : 256 * (h + 1), :], 1, 0).astype(bf16))
        dq_s[row(r), :] = jnp.concatenate(dqs, axis=0).T
        kv[r, :, :128] = dks[0].astype(bf16)
        kv[r, :, 128:256] = dks[1].astype(bf16)
        kv[r, :, 256:] = jnp.concatenate(dvs, axis=0).T

    def b3(r):
        dqn = dg(dq_s[row(r), :], wq[...], 1, 1) * SCALE
        hat, inv = norm(q_ref[r].astype(f32))
        vec[0, :, :width] += row_sum(dqn * hat)
        vec[1, :, :width] += row_sum(dqn)

        got = norm_back(dqn, line_of(R.gain_query), hat, inv) + dres_s[row(r), :].astype(f32)

        if r >= 1:
            staged(by_rows, R.grad_queries, R.gq_sem, r - 1, positions)

        stage(got, by_rows, R.grad_queries, R.gq_sem, r, positions)

    def cols(j):
        return pl.ds(pl.multiple_of(j * 256, 256), 256)

    def cols_at(j):
        return pl.ds(256 * j, 256)

    def chunk(k):
        return p_s.at[pl.ds(width * k, width)]

    def w_down(j):
        chunk(j)[...] = dg(act_s[...], flat(c_ref[:, :, cols_at(j)]), 0, 0).astype(bf16)

    def w_up(j):
        chunk(3 + j)[...] = dg(hn_s[...], dpre_s[:, cols_at(j)], 0, 0).astype(bf16)

    def w_out(j):
        chunk(6 + j)[...] = dg(mix_s[...], dres_s[:, cols_at(j)], 1, 0).astype(bf16)

    def w_q():
        dm_s[:, 1024:1280] = (dg(qn_s[...], dq_s[...], 0, 0) * SCALE).astype(bf16)

    def w_kv(j):
        early = (rows - pair) * lats
        left = jnp.concatenate([flat(ln2[...]), ln_s[:early, :]], axis=0)
        late = flat(kv[rows - pair :, :, 256 * j : 256 * (j + 1)])
        right = jnp.concatenate([late, dkv_own[:early, cols_at(j)]], axis=0)
        p_s[pl.ds(9 * width + j * lwidth, lwidth), :] = dg(left, right, 0, 0).astype(bf16)

    put_gl = [
        pltpu.make_async_copy(
            ds_scr.at[pl.ds(1024 + k * rows * lats, rows * lats)], R.grad_latents.at[:, pl.ds(256 * k, 256)], R.gl_sem.at[k]
        )
        for k in range(lwidth // 256)
    ]

    def l1():
        d = dg(dkv_own[:, :256], wk[...], 1, 1) + dg(dkv_own[:, 256:], wv[...], 1, 1)
        hat, inv = norm(flat(lat_ref[...]).astype(f32))
        vec[6] += row_sum(d * hat)
        vec[7] += row_sum(d)
        got = norm_back(d, line_of(R.gain_latent), hat, inv)
        for k, c in enumerate(put_gl):
            ds_scr[1024 + k * rows * lats : 1024 + (k + 1) * rows * lats, :] = got[:, 256 * k : 256 * (k + 1)].astype(bf16)
            c.start()

    spans = ((0, 1), (1, 1), (2, 2), (4, 2))
    G = [
        Gather(pc, kv, pl.ds(r0, n), R.ag_s.at[g], R.ag_r.at[g])
        for g, (r0, n) in enumerate(spans)
    ]
    G.append(Gather(pc, ln2, pl.ds(0, pair), R.ag_s.at[4], R.ag_r.at[4]))

    def job(k, ref, lo, c0, height, out):
        block = height // 8

        def part(t):
            return ref.at[pl.ds(pl.multiple_of(lo + t * block, 32), block), pl.ds(c0, 256)]

        sc = R.sc[k]
        ln = Line(pc, sc["l0"].at[pc.yb, pc.xb], kind=bf16, **R.li[k])
        return Job(Scatter(pc, part, 256, **sc), ln, out, R.t_sem.at[k])

    D = [job(j, p_s, width * j, 0, width, R.t_down.at[:, cols_at(j)]) for j in range(3)]
    U = [job(3 + j, p_s, width * (3 + j), 0, width, R.t_up.at[:, cols_at(j)]) for j in range(3)]
    O = [job(6 + j, p_s, width * (6 + j), 0, width, R.t_out.at[:, cols_at(j)]) for j in range(3)]
    Q = job(9, dm_s, 0, 1024, width, R.t_q)
    K = [job(10 + j, p_s, width * 9 + lwidth * j, 0, lwidth, R.t_kv.at[j]) for j in range(4)]

    dspans = ((0, 2), (2, 2), (4, 2))

    def keys_values(r0, n, sc):
        def part(t):
            return kv.at[pl.ds(r0, n), pl.ds(pl.multiple_of(t * lats, lats), lats), :]

        def keep():
            dkv_own[pl.ds(r0 * lats, n * lats), :] = flat(sc["l0"][pc.yb, pc.xb])

        return Scatter(pc, part, 1024, then=keep, **sc)

    DKV = [keys_values(r0, n, sc) for (r0, n), sc in zip(dspans, R.scd, strict=True)]
    lv = None if n_rows <= 4 else Line(pc, R.v_rows.at[0], kind=f32, **R.ln_vec)
    V = Vectors(pc, vec, R.v_pair, R.v_chips, R.v_rows, R.vs, R.vr, lv)

    vec[...] = jnp.zeros_like(vec)
    lid = R.latent_ids[...].astype(f32)
    lidT[...] = jnp.concatenate([lid, jnp.zeros((128 - rows, lid.shape[1]), f32)], axis=0).T
    loads["lat"].wait()
    loads["wk"].wait()
    loads["wv"].wait()
    for k in ("q", "wq", "c", "wd", "wo", "wu"):
        loads[k].start()
    l0()
    pc.met()
    G[0].p0()
    G[1].p0()
    loads["q"].wait()
    loads["wq"].wait()
    f1(0)
    f1(1)
    f1(2)
    G[0].p1()
    G[1].p1()
    G[2].p0()
    loads["c"].wait()
    loads["wd"].wait()
    f1b(0)
    f1b(1)
    f1b(2)
    G[3].p0()
    G[0].p2()
    G[1].p2()
    G[0].p3()
    G[2].p1()
    loads["wo"].wait()
    loads["wu"].wait()
    hooks = {
        0: {
            0: (G[1].p3,),
        },
        3: {
            0: (G[2].p2, G[3].p1, G[0].drain, G[1].drain,),
            1: (G[3].p3, DKV[0].p1, G[4].p0, G[2].drain,),
            2: (DKV[0].p2, DKV[1].p1, G[4].p1, G[3].drain,),
        },
        5: {
            0: (G[2].p3, G[3].p2, DKV[0].p0,),
            1: (DKV[1].p0,),
        },
    }

    def hook(k, i):
        for p, fns in hooks.get(k, {}).items():

            @pl.when(i == p)
            def _():
                for fn in fns:
                    fn()

    def main(i):
        f2(pair * i)
        hook(0, i)
        f2(pair * i + 1)
        f3(i)
        hook(3, i)

        @pl.when(i < n_pairs - 1)
        def _():
            b2(pair * i)
            b2(pair * i + 1)

        hook(5, i)

    loop(0, n_pairs, main)
    w_out(2)
    O[2].p0()
    w_out(1)
    O[1].p0()
    b2(4)
    O[2].p1()
    DKV[0].p3()
    O[1].p1()
    w_up(0)
    U[0].p0()
    w_down(2)
    DKV[1].p2()
    D[2].p0()
    b2(5)
    U[0].p1()
    G[4].p2()
    DKV[2].p0()
    D[2].p1()
    O[2].p2()
    b3(0)
    O[1].p2()
    w_down(1)
    G[4].p3()
    D[1].p0()
    DKV[1].p3()
    DKV[2].p1()
    w_kv(1)
    U[0].p2()
    K[1].p0()
    w_kv(3)
    D[1].p1()
    D[2].p2()
    K[3].p0()
    O[2].p3()
    b3(1)
    O[1].p3()
    K[1].p1()
    w_out(0)
    K[3].p1()
    O[0].p0()
    b3(2)
    DKV[2].p2()
    O[2].up()
    U[0].p3()
    w_kv(2)
    O[0].p1()
    O[1].up()
    D[1].p2()
    K[2].p0()
    bo(0)
    D[2].p3()
    K[1].p2()
    K[2].p1()
    O[2].mid()
    U[0].up()
    w_down(0)
    O[1].mid()
    K[3].p2()
    D[0].p0()
    w_kv(0)
    K[0].p0()
    DKV[2].p3()
    w_q()
    D[2].up()
    O[0].p2()
    D[0].p1()
    O[2].dn()
    U[0].mid()
    D[1].p3()
    K[0].p1()
    K[1].p3()
    O[1].dn()
    Q.p0()
    w_up(2)
    K[2].p2()
    U[2].p0()
    w_up(1)
    K[3].p3()
    Q.p1()
    O[0].p3()
    D[2].mid()
    U[1].p0()
    U[0].dn()
    D[1].up()
    D[0].p2()
    U[2].p1()
    bo(1)
    K[1].up()
    K[0].p2()
    U[1].p1()
    K[2].p3()
    b3(3)
    D[2].dn()
    Q.p2()
    K[3].up()
    D[1].mid()
    D[0].p3()
    b3(4)
    O[0].up()
    U[2].p2()
    b3(5)
    K[0].p3()
    l1()
    K[1].mid()
    U[1].p2()
    K[2].up()
    Q.p3()
    D[1].dn()
    D[0].up()
    K[3].mid()
    U[2].p3()
    V.p0()
    bo(2)
    O[0].mid()
    V.p1()
    K[0].up()
    U[1].p3()
    Q.up()
    K[1].dn()
    K[2].mid()
    U[2].up()
    D[0].mid()
    K[3].dn()
    U[1].up()
    O[0].dn()
    V.p2()
    K[0].mid()
    Q.mid()
    K[2].dn()
    U[2].mid()
    D[0].dn()
    U[1].mid()
    K[0].dn()
    Q.dn()
    U[2].dn()
    V.p3()
    U[1].dn()
    jobs = [*D, *U, *O, Q, *K]
    for x in jobs:
        x.store()
    V.store(R.t_vec, R.t_sem.at[len(jobs)])
    for x in (G[4], *jobs, *DKV, V):
        x.drain()
    pltpu.make_async_copy(R.v_pair.at[0], R.t_vec, R.t_sem.at[len(jobs)]).wait()
    staged(by_rows, R.grad_queries, R.gq_sem, rows - 1, positions)
    staged(by_columns, R.block_out, R.bo_sem, n_pairs - 1, span)
    for c in put_gl:
        c.wait()


def unpack(*refs):
    n = len(Outs._fields)
    ins, out = refs[:9], Outs(*refs[9 : 9 + n])
    stay, wide, narrow = refs[9 + n : 18 + n], refs[18 + n : -3], refs[-3]
    sem_in, sem_out = refs[-2], refs[-1]
    loads = [pltpu.make_async_copy(a, b, sem_in.at[k]) for k, (a, b) in enumerate(zip(ins, stay))]
    for c in loads:
        c.start()
    t_vec = stay[8]
    outs = (
        out.block_out,
        out.grad_queries,
        out.grad_latents,
        out.grad_down_weight,
        out.grad_up_weight,
        out.grad_out_weight,
        out.grad_query_weight,
        out.grad_key_weight,
        out.grad_value_weight,
    )
    stores = [pltpu.make_async_copy(stay[0], out.block_out, sem_out.at[0])]
    stores += [pltpu.make_async_copy(v, outs[k + 1], sem_out.at[k + 1]) for k, v in enumerate(wide)]
    loads[1].wait()
    half = wide[0].shape[0] // 2
    halves = []
    for j in range(2):
        rs = pl.ds(j * half, half)
        wide[0][rs] = stay[1][rs].astype(f32)
        halves.append(pltpu.make_async_copy(wide[0].at[rs], out.grad_queries.at[rs], narrow.at[j]))
        halves[-1].start()
    stores = stores[:1] + stores[2:]
    loads[0].wait()
    stores[0].start()
    for k in range(1, 6):
        loads[k + 1].wait()
        wide[k][...] = stay[k + 1][...].astype(f32)
        stores[k].start()
    loads[7].wait()
    wide[6][...] = stay[7][0].astype(f32)
    stores[6].start()
    for k in range(3):
        wide[7][:, 256 * k : 256 * (k + 1)] = stay[7][k + 1].astype(f32)
    stores[7].start()
    loads[8].wait()
    vectors = (
        out.grad_gain_query,
        out.grad_shift_query,
        out.grad_gain_hidden,
        out.grad_shift_hidden,
        out.grad_bias_up,
        out.grad_bias_down,
        out.grad_gain_latent,
        out.grad_shift_latent,
    )
    for t in range(8):

        @pl.when(lax.axis_index("seq") == t)
        def _():
            for k, ref in enumerate(vectors):
                m = ref.shape[0]
                ref[...] = t_vec[k, m * t : m * (t + 1)]

    for c in stores + halves:
        c.wait()


class Args(NamedTuple):
    queries: Any
    latents: Any
    query_ids: Any
    latent_ids: Any
    query_weight: Any
    key_weight: Any
    value_weight: Any
    out_weight: Any
    up_weight: Any
    down_weight: Any
    gain_query: Any
    shift_query: Any
    gain_latent: Any
    shift_latent: Any
    gain_hidden: Any
    shift_hidden: Any
    bias_up: Any
    bias_down: Any
    cotangent: Any


class Outs(NamedTuple):
    block_out: Any
    grad_queries: Any
    grad_latents: Any
    grad_query_weight: Any
    grad_key_weight: Any
    grad_value_weight: Any
    grad_out_weight: Any
    grad_up_weight: Any
    grad_down_weight: Any
    grad_gain_query: Any
    grad_shift_query: Any
    grad_gain_latent: Any
    grad_shift_latent: Any
    grad_gain_hidden: Any
    grad_shift_hidden: Any
    grad_bias_up: Any
    grad_bias_down: Any


def body(n_rows, n_seq, *args):
    A = Args(*args)
    rows, pos, width = A.queries.shape
    lats, lwidth = A.latents.shape[1:]
    nl = lats * n_seq
    F_ = lambda *s: jax.ShapeDtypeStruct(s, f32)
    wide, vec, lvec = F_(width // n_seq, width), F_(width // n_seq), F_(lwidth // n_seq)
    out = Outs(
        block_out=jax.ShapeDtypeStruct((rows, pos, width), bf16),
        grad_queries=F_(rows, pos, width),
        grad_latents=F_(rows, lats, lwidth),
        grad_query_weight=F_(width // n_seq, 256),
        grad_key_weight=F_(lwidth // n_seq, 256),
        grad_value_weight=F_(lwidth // n_seq, width),
        grad_out_weight=wide,
        grad_up_weight=wide,
        grad_down_weight=wide,
        grad_gain_query=vec,
        grad_shift_query=vec,
        grad_gain_latent=lvec,
        grad_shift_latent=lvec,
        grad_gain_hidden=vec,
        grad_shift_hidden=vec,
        grad_bias_up=vec,
        grad_bias_down=vec,
    )
    V = lambda *s: pltpu.VMEM(s, bf16)
    F = lambda *s: pltpu.VMEM(s, f32)
    dma = lambda *s: pltpu.SemaphoreType.DMA(s)
    tok = V(rows, pos, width)
    tok2 = V(rows * pos, width)
    tokT = V(width, rows * pos)
    scratch = dict(
        q_v=tok,
        c_v=tok,
        lat_v=V(rows, lats, lwidth),
        wq_v=V(width, 256),
        wk_v=V(lwidth, 256),
        wv_v=V(lwidth, width),
        wo_v=V(width, width),
        wu_v=V(width, width),
        wd_v=V(width, width),
        kv=V(rows, nl, 1024),
        qn=tok2,
        qp=V(rows * pos, 256),
        s_scr=F(HEADS, nl, pos),
        ds_scr=V(HEADS * nl, pos),
        inv=F(rows, HEADS, pos),
        p=V(rows * HEADS * nl, pos),
        mix=tokT,
        hn=tok2,
        act=tok2,
        dpre=tok2,
        dres=tok2,
        dm=tokT,
        lidT=F(nl, 128),
        ln=V(rows * lats, lwidth),
        ln2=V(2, nl, lwidth),
        dkv_own=V(rows * lats, 1024),
        vec=F(8, 8, lwidth),
        v_pair=F(2, 8, lwidth),
        v_chips=F(4, 8, lwidth),
        v_rows=F(min(n_rows, 4), 8, lwidth),
        vs=dma(7),
        vr=dma(7),
        bo_sem=dma(width // 256),
        gq_sem=dma(width // 256),
        gl_sem=dma(lwidth // 256),
        t_sem=dma(15),
        load_sem=dma(9),
        ag_s=dma(5, 9),
        ag_r=dma(5, 9),
        ln_vec=line_scratch((8, lwidth), f32),
    )
    lead, llead = (width // n_seq,), (lwidth // n_seq,)
    shapes = [lead] * 10 + [llead] * 4
    scratch["sc"] = [scatter_scratch(x, 256) for x in shapes]
    scratch["li"] = [line_scratch((*x, 256), bf16) for x in shapes]
    scratch["scd"] = [scatter_scratch((n, lats), 1024) for n in (2, 2, 2)]
    any_ = pl.BlockSpec(memory_space=pl.ANY)
    vm = pl.BlockSpec(memory_space=pltpu.VMEM)
    far = (A.queries, A.cotangent, A.latents, *A[4:10])
    in_specs = [any_ if any(a is f for f in far) else vm for a in A]
    sds = jax.ShapeDtypeStruct
    mid = dict(
        block_out=sds((rows * pos, width), bf16),
        grad_queries=sds((rows * pos, width), bf16),
        grad_latents=sds((rows * lats, lwidth), bf16),
        t_down=sds(wide.shape, bf16),
        t_up=sds(wide.shape, bf16),
        t_out=sds(wide.shape, bf16),
        t_q=sds((width // n_seq, 256), bf16),
        t_kv=sds((4, lwidth // n_seq, 256), bf16),
        t_vec=sds((8, lwidth), f32),
    )
    names = (*Args._fields, *mid, *scratch)
    flops = 2 * rows * pos * width * width * 14
    got = pl.pallas_call(
        functools.partial(kernel, n_rows, names),
        out_shape=tuple(mid.values()),
        in_specs=in_specs,
        out_specs=(any_,) * len(mid),
        scratch_shapes=list(scratch.values()),
        compiler_params=pltpu.CompilerParams(
            collective_id=0, has_side_effects=True, vmem_limit_bytes=64 << 20
        ),
        cost_estimate=pl.CostEstimate(flops=flops, bytes_accessed=24 << 20, transcendentals=0),
    )(*A)
    three = lambda x: x.reshape(rows, -1, x.shape[-1])
    got = (three(got[0]), three(got[1]), three(got[2]), *got[3:])
    return pl.pallas_call(
        unpack,
        out_shape=tuple(out),
        in_specs=[any_] * 9,
        out_specs=(any_,) * 9 + (vm,) * 8,
        scratch_shapes=[pltpu.VMEM(x.shape, x.dtype) for x in got]
        + [
            pltpu.VMEM(o.shape, f32)
            for o in (
                out.grad_queries,
                out.grad_latents,
                wide,
                wide,
                wide,
                out.grad_query_weight,
                out.grad_key_weight,
                out.grad_value_weight,
            )
        ]
        + [dma(2), dma(9), dma(9)],
        compiler_params=pltpu.CompilerParams(vmem_limit_bytes=64 << 20),
        cost_estimate=pl.CostEstimate(flops=0, bytes_accessed=18 << 20, transcendentals=0),
    )(*got)


def solution(mesh):
    seq = P("rows", "seq", None)
    rep = P()
    in_specs = (seq, seq, P("rows", "seq"), P("rows", None)) + (rep,) * 14 + (seq,)
    out_specs = (seq,) * 3 + (P("seq", None),) * 6 + (P("seq"),) * 8
    return jax.shard_map(
        functools.partial(body, mesh.shape["rows"], mesh.shape["seq"]),
        mesh=mesh,
        in_specs=in_specs,
        out_specs=out_specs,
        check_vma=False,
    )
```

```python
import functools
import types
from typing import Any, NamedTuple

import jax
import jax.numpy as jnp
from jax import lax
from jax.experimental import pallas as pl
from jax.experimental.pallas import tpu as pltpu
from jax.sharding import PartitionSpec as P

HEADS = 8
HDIM = 96
QKDIM = 32
EPS = 1e-05
SCALE = QKDIM ** (-0.5)
MESH = pl.DeviceIdType.MESH
f32, bf16 = jnp.float32, jnp.bfloat16


def dg(a, b, ca, cb):
    return lax.dot_general(a, b, (((ca,), (cb,)), ((), ())), preferred_element_type=f32)


def norm(x):
    mean = jnp.mean(x, -1, keepdims=True)
    cen = x - mean
    inv = lax.rsqrt(jnp.mean(cen * cen, -1, keepdims=True) + EPS)
    return cen * inv, inv


def norm_back(grad, gain, hat, inv):
    g = grad * gain
    return inv * (
        g - jnp.mean(g, -1, keepdims=True) - hat * jnp.mean(g * hat, -1, keepdims=True)
    )


def row_sum(x):
    n, w = x.shape
    return jnp.sum(x.reshape(n // 8, 8, w), axis=0)


def flat(x):
    return x.reshape(-1, x.shape[-1])


def add(a, b):
    return (a.astype(f32) + b.astype(f32)).astype(bf16)


class Place:
    def __init__(self, n_rows):
        self.n = n_rows
        self.s = lax.axis_index("seq")
        self.r = lax.axis_index("rows")
        self.core = lax.rem(self.s, 2)
        self.chip = self.s // 2
        self.xc = self.chip + 1 - 2 * lax.rem(self.chip, 2)
        self.yc = lax.rem(self.chip + 2, 4)
        self.dc = lax.rem(self.xc + 2, 4)
        self.xb, self.yb = lax.rem(self.chip, 2), self.chip // 2
        self.sib = (self.s + 1 - 2 * self.core, self.r)
        self.xn = (2 * self.xc + self.core, self.r)
        self.yn = (2 * self.yc + self.core, self.r)
        half = n_rows // 2
        self.left = self.r < half
        self.mid = (self.r == half - 1) | (self.r == half)
        self.not_end = (self.r != 0) & (self.r != n_rows - 1)
        step = jnp.where(self.left, 1, -1)
        self.inner = (self.s, lax.rem(self.r + step + n_rows, n_rows))
        self.outer = (self.s, lax.rem(self.r - step + n_rows, n_rows))

    def greet(self):
        up = (self.s, lax.rem(self.r + 1, self.n))
        down = (self.s, lax.rem(self.r + self.n - 1, self.n))
        self.bar = pltpu.get_barrier_semaphore()
        for peer in (self.sib, self.xn, self.yn, up, down):
            pl.semaphore_signal(self.bar, inc=1, device_id=peer, device_id_type=MESH)

    def met(self):
        pl.semaphore_wait(self.bar, 5)


def rcopy(src, dst, ssem, rsem, peer):
    return pltpu.make_async_remote_copy(
        src_ref=src, dst_ref=dst, send_sem=ssem, recv_sem=rsem, device_id=peer, device_id_type=MESH
    )


class Line:
    def __init__(self, pc, src, zo, zi, ssem, rsem, kind):
        zt = zo
        self.pc, self.src, self.zo, self.zi, self.zt, self.kind = pc, src, zo, zi, zt, kind
        self.up_c = rcopy(src, zo, ssem.at[0], rsem.at[0], pc.inner)
        self.cross_c = rcopy(src, zi, ssem.at[1], rsem.at[1], pc.inner)
        self.down_mid = rcopy(zt, zi, ssem.at[2], rsem.at[1], pc.outer)
        self.down_far = rcopy(zi, zi, ssem.at[2], rsem.at[1], pc.outer)

    def plus(self, a, b):
        return (a.astype(f32) + b.astype(f32)).astype(self.kind)

    def send(self):
        pc = self.pc
        pl.when(jnp.logical_not(pc.not_end) & jnp.logical_not(pc.mid))(self.up_c.start)

    def up(self):
        pc = self.pc

        @pl.when(pc.not_end)
        def _():
            self.up_c.wait_recv()
            self.src[...] = self.plus(self.src[...], self.zo[...])

        pl.when(pc.mid)(self.cross_c.start)
        pl.when(jnp.logical_not(pc.mid) & pc.not_end)(self.up_c.start)

    def middle(self):
        pc = self.pc

        @pl.when(pc.mid)
        def _():
            self.cross_c.wait_recv()
            self.zt[...] = self.plus(self.src[...], self.zi[...])

        pl.when(pc.mid & pc.not_end)(self.down_mid.start)

    def down(self):
        pc = self.pc
        pl.when(jnp.logical_not(pc.mid))(self.cross_c.wait_recv)
        pl.when(jnp.logical_not(pc.mid) & pc.not_end)(self.down_far.start)

    def result(self, write):
        pc = self.pc
        pl.when(pc.mid)(lambda: write(self.zt))
        pl.when(jnp.logical_not(pc.mid))(lambda: write(self.zi))

    def drain(self):
        pc = self.pc
        pl.when(pc.mid)(self.cross_c.wait_send)
        pl.when(jnp.logical_not(pc.mid))(self.up_c.wait_send)
        pl.when(pc.mid & pc.not_end)(self.down_mid.wait_send)
        pl.when(jnp.logical_not(pc.mid) & pc.not_end)(self.down_far.wait_send)


class Scatter:
    def __init__(self, pc, part, width, l0, la, lb, la2, lb2, ssem, rsem, then=None):
        self.pc, self.part, self.l0, self.then = pc, part, l0, then
        self.la, self.lb, self.la2, self.lb2 = la, lb, la2, lb2
        h = width // 2
        A, B = self.A, self.B = pl.ds(0, h), pl.ds(h, h)
        lead = (slice(None),) * (len(l0.shape) - 3)
        xb, yb = pc.xb, pc.yb

        def blk(y, x, cols):
            return l0.at[(y, x, *lead, cols)]

        self.blk = blk
        other = 1 - pc.core
        self.pair = [
            rcopy(part(2 * q + other), l0.at[q // 2, q % 2], ssem.at[q], rsem.at[q], pc.sib)
            for q in range(4)
        ]
        every = slice(None)
        self.first = [
            rcopy(blk(every, 1 - xb, A), la, ssem.at[4], rsem.at[4], pc.xn),
            rcopy(blk(1 - yb, every, B), lb, ssem.at[5], rsem.at[5], pc.yn),
        ]
        self.second = [
            rcopy(blk(1 - yb, xb, A), la2, ssem.at[6], rsem.at[6], pc.yn),
            rcopy(blk(yb, 1 - xb, B), lb2, ssem.at[7], rsem.at[7], pc.xn),
        ]

    def p0(self):
        for c in self.pair:
            c.start()

    def p1(self):
        for q in range(4):
            self.pair[q].wait_recv()
            own = self.part(2 * q + self.pc.core)[...]
            self.l0[q // 2, q % 2] = add(self.l0[q // 2, q % 2], own)
        for c in self.first:
            c.start()

    def into(self, y, x, cols, got):
        v = self.blk(y, x, cols)
        v[...] = add(v[...], got[...])

    def p2(self):
        xb, yb = self.pc.xb, self.pc.yb
        self.first[0].wait_recv()
        self.into(1 - yb, xb, self.A, self.la.at[1 - yb])
        self.second[0].start()
        self.first[1].wait_recv()
        self.into(yb, 1 - xb, self.B, self.lb.at[1 - xb])
        self.second[1].start()
        self.into(yb, xb, self.A, self.la.at[yb])
        self.into(yb, xb, self.B, self.lb.at[xb])

    def p3(self):
        for c, cols, got in zip(self.second, (self.A, self.B), (self.la2, self.lb2)):
            c.wait_recv()
            self.into(self.pc.yb, self.pc.xb, cols, got)
        self.then()

    def drain(self):
        for c in self.pair + self.first + self.second:
            c.wait_send()


class Job:
    def __init__(self, scatter, line, out, sem):
        self.scatter, self.line = scatter, line
        scatter.then = line.send
        self.p0, self.p1, self.p2, self.p3 = scatter.p0, scatter.p1, scatter.p2, scatter.p3
        self.up, self.mid, self.dn = line.up, line.middle, line.down
        self.out, self.sem = out, sem

    def store(self):
        self.line.result(lambda src: pltpu.make_async_copy(src, self.out, self.sem).start())

    def drain(self):
        pltpu.make_async_copy(self.line.zo, self.out, self.sem).wait()
        self.scatter.drain()
        self.line.drain()


class Vectors:
    def __init__(self, pc, vec, tot, land, ssem, rsem, line):
        self.vec, self.tot, self.land, self.line = vec, tot, land, line
        self.steps = [
            rcopy(tot.at[k], land.at[k], ssem.at[k], rsem.at[k], peer)
            for k, peer in enumerate((pc.sib, pc.xn, pc.yn))
        ]
        self.up, self.mid, self.dn = line.up, line.middle, line.down

    def p0(self):
        self.tot[0] = jnp.sum(self.vec[...], axis=1)
        self.steps[0].start()

    def take(self, k):
        self.steps[k].wait_recv()
        self.tot[k + 1] = self.tot[k] + self.land[k]

    def p1(self):
        self.take(0)
        self.steps[1].start()

    def p2(self):
        self.take(1)
        self.steps[2].start()

    def p3(self):
        self.take(2)
        self.line.send()

    def drain(self):
        for c in self.steps:
            c.wait_send()
        self.line.drain()


def scatter_scratch(lead, width):
    half = width // 2
    return dict(
        l0=pltpu.VMEM((2, 2, *lead, width), bf16),
        la=pltpu.VMEM((2, *lead, half), bf16),
        lb=pltpu.VMEM((2, *lead, half), bf16),
        la2=pltpu.VMEM((*lead, half), bf16),
        lb2=pltpu.VMEM((*lead, half), bf16),
        ssem=pltpu.SemaphoreType.DMA((8,)),
        rsem=pltpu.SemaphoreType.DMA((8,)),
    )


def line_scratch(shape, kind):
    return dict(
        zo=pltpu.VMEM(shape, kind),
        zi=pltpu.VMEM(shape, kind),
        ssem=pltpu.SemaphoreType.DMA((3,)),
        rsem=pltpu.SemaphoreType.DMA((2,)),
    )


class Gather:
    def __init__(self, pc, kv, rows, ssem, rsem):
        def blk(t, cols=slice(None)):
            return kv.at[rows, pl.ds(pl.multiple_of(t * 32, 32), 32), cols]

        h = kv.shape[-1] // 2
        A, B = pl.ds(0, h), pl.ds(h, h)
        ds_ = 2 * pc.dc + pc.core

        def copy(k, ref, peer):
            return rcopy(ref, ref, ssem.at[k], rsem.at[k], peer)

        self.own = [copy(0, blk(pc.s), pc.sib), copy(1, blk(pc.s), pc.xn), copy(2, blk(pc.s), pc.yn)]
        self.from_x = [copy(3, blk(pc.xn[0], A), pc.yn), copy(4, blk(pc.xn[0]), pc.sib)]
        self.from_y = [copy(5, blk(pc.yn[0], B), pc.xn), copy(6, blk(pc.yn[0]), pc.sib)]
        self.from_d = [copy(7, blk(ds_, A), pc.sib), copy(8, blk(ds_, B), pc.sib)]

    def p0(self):
        for c in self.own[::-1]:
            c.start()

    def p1(self):
        self.own[1].wait_recv()
        for c in self.from_x:
            c.start()
        self.own[2].wait_recv()
        for c in self.from_y:
            c.start()

    def p2(self):
        self.from_x[0].wait_recv()
        self.from_d[0].start()
        self.from_y[0].wait_recv()
        self.from_d[1].start()

    def p3(self):
        for c in (self.own[0], self.from_x[1], self.from_y[1], *self.from_d):
            c.wait_recv()

    def drain(self):
        for c in self.own + self.from_x + self.from_y + self.from_d:
            c.wait_send()


def kernel(n_rows, names, *refs):
    R = types.SimpleNamespace(**dict(zip(names, refs, strict=True)))
    q_hbm, c_hbm, lat_hbm = R.queries, R.cotangent, R.latents
    line_of = lambda ref: ref[...].reshape(1, -1)
    q_ref, c_ref, lat_ref = R.q_v, R.c_v, R.lat_v
    wq, wk, wv, wo, wu, wd = R.wq_v, R.wk_v, R.wv_v, R.wo_v, R.wu_v, R.wd_v
    kv, qn_s, qp_s, p_s, mix_s, hn_s = R.kv, R.qn, R.qp, R.p, R.mix, R.hn
    act_s, dpre_s, dres_s, dm_s, dq_s = R.act, R.dpre, R.dres, R.dm, R.dq
    s_scr, ds_scr, inv_s = R.s_scr, R.ds_scr, R.inv
    lidT, ln_s, dkv_own, vec = R.lidT, R.ln, R.dkv_own, R.vec
    rows, positions, width = q_ref.shape
    lats, lwidth = lat_ref.shape[1:]
    pair = 2
    n_pairs = rows // pair
    tokens = rows * positions
    span = positions * pair

    loads = {}
    for k, (name, src, dst) in enumerate(
        [
            ("lat", lat_hbm, lat_ref),
            ("wk", R.key_weight, wk),
            ("wv", R.value_weight, wv),
            ("q", q_hbm, q_ref),
            ("wq", R.query_weight, wq),
            ("wo", R.out_weight, wo),
            ("wu", R.up_weight, wu),
            ("wd", R.down_weight, wd),
            ("c", c_hbm, c_ref),
        ]
    ):
        loads[name] = pltpu.make_async_copy(src, dst, R.load_sem.at[k])
        loads[name].start()

    pc = Place(n_rows)
    pc.greet()

    def loop(first, last, body):
        def step(i, carry):
            body(i)
            return carry

        lax.fori_loop(first, last, step, 0)

    lane1 = lax.broadcasted_iota(jnp.int32, (1, 128), 1)

    def head_mask(hh, kind):
        return ((lane1 >= QKDIM * hh) & (lane1 < QKDIM * (hh + 1))).astype(kind)

    own = pl.ds(pl.multiple_of(pc.s * lats, lats), lats)

    def l0(g):
        rs = pl.ds(g * pair, pair)
        hat, _ = norm(flat(lat_ref[rs]).astype(f32))
        ln = (hat * line_of(R.gain_latent) + line_of(R.shift_latent)).astype(bf16)
        ln_s[pl.ds(g * pair * lats, pair * lats), :] = ln
        k = dg(ln, wk[...], 1, 0).astype(bf16)
        v = dg(ln, wv[...], 1, 0).astype(bf16)
        kv[rs, own, 0:256] = k.reshape(pair, lats, -1)
        kv[rs, own, 256:1024] = v.reshape(pair, lats, -1)

    def at(i):
        return pl.ds(pl.multiple_of(i * span, span), span)

    def row(r):
        return pl.ds(pl.multiple_of(r * positions, positions), positions)

    def f1(i):
        hat, _ = norm(flat(q_ref[pl.ds(i * pair, pair)]).astype(f32))
        qn = (hat * line_of(R.gain_query) + line_of(R.shift_query)).astype(bf16)
        qn_s[at(i), :] = qn
        qp_s[at(i), :] = (dg(qn, wq[...], 1, 0) * SCALE).astype(bf16)

    def f1b(i):
        c = flat(c_ref[pl.ds(i * pair, pair)])
        vec[5, :, :width] += row_sum(c.astype(f32))
        dpre_s[at(i), :] = dg(c, wd[...], 1, 1).astype(bf16)

    def row8(r):
        return pl.ds(pl.multiple_of(r * HEADS * 256, HEADS * 256), HEADS * 256)

    def f2(r):
        k = kv[r, :, :256]
        vT = kv[r, :, 256:].T
        lane = lax.broadcasted_iota(jnp.int32, (256, 128), 1)
        col = jnp.sum(jnp.where(lane == r, lidT[...], 0.0), axis=1, keepdims=True)
        allowed = col == R.query_ids[pl.ds(r, 1), :].astype(f32)
        for g in range(2):
            kb = k[:, 128 * g : 128 * g + 128]
            km = jnp.concatenate([kb * head_mask(hh, bf16) for hh in range(4)], axis=0)
            sg = dg(km, qp_s[row(r), 128 * g : 128 * g + 128], 1, 1)
            for hh in range(4):
                s_scr[4 * g + hh] = sg[256 * hh : 256 * (hh + 1)]
        p_r = p_s.at[row8(r)]
        for h in range(HEADS):
            s = jnp.where(allowed, s_scr[h], -1e30)
            e = jnp.exp(s - jnp.max(s, axis=0, keepdims=True))
            p_r[256 * h : 256 * (h + 1), :] = e.astype(bf16)
            inv_s[r, h : h + 1, :] = 1.0 / jnp.sum(e, axis=0, keepdims=True)
        mix_r = mix_s.at[:, row(r)]
        for h in range(HEADS):
            hs = slice(HDIM * h, HDIM * (h + 1))
            got = dg(vT[hs], p_r[256 * h : 256 * (h + 1), :], 1, 0)
            mix_r[hs, :] = (got * inv_s[r, h : h + 1, :]).astype(bf16)

    def chunks(dst, sems, i, n):
        return [
            pltpu.make_async_copy(
                ds_scr.at[pl.ds(k * n, n)],
                dst.at[pl.ds(pl.multiple_of(i * n, n), n), pl.ds(256 * k, 256)],
                sems.at[k],
            )
            for k in range(width // 256)
        ]

    def stage(value, dst, sems, i, n):
        for k, c in enumerate(chunks(dst, sems, i, n)):
            ds_scr[n * k : n * (k + 1), :] = value[:, 256 * k : 256 * (k + 1)].astype(bf16)
            c.start()

    def staged(dst, sems, i, n):
        for c in chunks(dst, sems, i, n):
            c.wait()

    def f3(i):
        rs = pl.ds(i * pair, pair)
        resid = flat(q_ref[rs]).astype(f32) + dg(mix_s[:, at(i)], wo[...], 0, 0)
        hat, inv = norm(resid)
        hn = (hat * line_of(R.gain_hidden) + line_of(R.shift_hidden)).astype(bf16)
        hn_s[at(i), :] = hn
        pre = dg(hn, wu[...], 1, 0) + line_of(R.bias_up)
        phi = 0.5 * (1.0 + lax.erf(pre * (0.5**0.5)))
        act = (pre * phi).astype(bf16)
        act_s[at(i), :] = act
        slope = phi + pre * (jnp.exp(-0.5 * pre * pre) * 0.3989422804014327)
        dpre = (dpre_s[at(i), :].astype(f32) * slope).astype(bf16)
        dpre_s[at(i), :] = dpre

        out = resid + dg(act, wd[...], 1, 0) + line_of(R.bias_down)
        stage(out, R.block_out, R.bo_sem, i, span)
        vec[4, :, :width] += row_sum(dpre.astype(f32))
        dh = dg(dpre, wu[...], 1, 1)
        vec[2, :, :width] += row_sum(dh * hat)
        vec[3, :, :width] += row_sum(dh)
        cf = flat(c_ref[rs]).astype(f32)
        dlow = (norm_back(dh, line_of(R.gain_hidden), hat, inv) + cf).astype(bf16)
        dres_s[at(i), :] = dlow
        dm_s[:, at(i)] = dg(wo[...], dlow, 1, 1).astype(bf16)
        staged(R.block_out, R.bo_sem, i, span)

    def b2(r):
        k = kv[r, :, :256]
        kT = k.T
        v = kv[r, :, 256:]
        dvs, dqs, dks = [], [], []
        p_r, dm_r, qp_r = p_s.at[row8(r)], dm_s.at[:, row(r)], qp_s.at[row(r)]
        for h in range(HEADS):
            hs = slice(HDIM * h, HDIM * (h + 1))
            dm_r[hs, :] = (dm_r[hs, :].astype(f32) * inv_s[r, h : h + 1, :]).astype(bf16)
        for h in range(HEADS):
            hs = slice(HDIM * h, HDIM * (h + 1))
            s_scr[h] = dg(v[:, hs], dm_r[hs, :], 1, 0)
        for h in range(HEADS):
            hs = slice(HDIM * h, HDIM * (h + 1))
            dvs.append(dg(dm_r[hs, :], p_r[256 * h : 256 * (h + 1), :], 1, 1).astype(bf16))
        for h in range(HEADS):
            e = p_r[256 * h : 256 * (h + 1), :].astype(f32)
            ed = e * s_scr[h]
            ds = ed - e * (jnp.sum(ed, axis=0, keepdims=True) * inv_s[r, h : h + 1, :])
            ds_scr[256 * h : 256 * (h + 1), :] = ds.astype(bf16)
        for g in range(2):
            t = dg(ds_scr[1024 * g : 1024 * (g + 1), :], qp_r[:, 128 * g : 128 * g + 128], 1, 0)
            dks.append(sum(t[256 * hh : 256 * (hh + 1)] * head_mask(hh, f32) for hh in range(4)))
        for h in range(HEADS):
            kh = kT[QKDIM * h : QKDIM * (h + 1)]
            dqs.append(dg(kh, ds_scr[256 * h : 256 * (h + 1), :], 1, 0).astype(bf16))
        dq_s[row(r), :] = jnp.concatenate(dqs, axis=0).T
        kv[r, :, :128] = dks[0].astype(bf16)
        kv[r, :, 128:256] = dks[1].astype(bf16)
        kv[r, :, 256:] = jnp.concatenate(dvs, axis=0).T

    def b3(r):
        dqn = dg(dq_s[row(r), :], wq[...], 1, 1) * SCALE
        hat, inv = norm(q_ref[r].astype(f32))
        vec[0, :, :width] += row_sum(dqn * hat)
        vec[1, :, :width] += row_sum(dqn)

        got = norm_back(dqn, line_of(R.gain_query), hat, inv) + dres_s[row(r), :].astype(f32)

        if r >= 1:
            staged(R.grad_queries, R.gq_sem, r - 1, positions)

        stage(got, R.grad_queries, R.gq_sem, r, positions)

    def cols(j):
        return pl.ds(pl.multiple_of(j * 256, 256), 256)

    def cols_at(j):
        return pl.ds(256 * j, 256)

    def w_down(j):
        R.g_down[:, cols_at(j)] = dg(act_s[...], flat(c_ref[:, :, cols_at(j)]), 0, 0).astype(bf16)

    g_up, g_out = act_s.at[pl.ds(0, width)], hn_s.at[pl.ds(0, width)]

    def w_up(j):
        g_up[:, cols_at(j)] = dg(hn_s[...], dpre_s[:, cols_at(j)], 0, 0).astype(bf16)

    def w_out(j):
        g_out[:, cols_at(j)] = dg(mix_s[...], dres_s[:, cols_at(j)], 1, 0).astype(bf16)

    def w_q():
        R.g_q[...] = (dg(qn_s[...], dq_s[...], 0, 0) * SCALE).astype(bf16)

    def w_kv(j):
        got = dg(ln_s[:, cols(j)], dkv_own[...], 0, 0).astype(bf16)
        for k in range(4):
            to = pl.ds(pl.multiple_of(k * lwidth + j * 256, 256), 256)
            p_s[to, :] = got[:, 256 * k : 256 * (k + 1)]

    put_gl = [
        pltpu.make_async_copy(
            ds_scr.at[pl.ds(1024 + k * rows * lats, rows * lats)], R.grad_latents.at[:, pl.ds(256 * k, 256)], R.gl_sem.at[k]
        )
        for k in range(lwidth // 256)
    ]

    def l1():
        d = dg(dkv_own[:, :256], wk[...], 1, 1) + dg(dkv_own[:, 256:], wv[...], 1, 1)
        hat, inv = norm(flat(lat_ref[...]).astype(f32))
        vec[6] += row_sum(d * hat)
        vec[7] += row_sum(d)
        got = norm_back(d, line_of(R.gain_latent), hat, inv)
        for k, c in enumerate(put_gl):
            ds_scr[1024 + k * rows * lats : 1024 + (k + 1) * rows * lats, :] = got[:, 256 * k : 256 * (k + 1)].astype(bf16)
            c.start()

    G = [Gather(pc, kv, pl.ds(g * pair, pair), R.ag_s.at[g], R.ag_r.at[g]) for g in range(n_pairs)]

    def job(k, ref, lo, c0, height, out):
        block = height // 8

        def part(t):
            return ref.at[pl.ds(pl.multiple_of(lo + t * block, 32), block), pl.ds(c0, 256)]

        sc = R.sc[k]
        ln = Line(pc, sc["l0"].at[pc.yb, pc.xb], kind=bf16, **R.li[k])
        return Job(Scatter(pc, part, 256, **sc), ln, out, R.t_sem.at[k])

    D = [job(j, R.g_down, 0, 256 * j, width, R.t_down.at[:, cols_at(j)]) for j in range(3)]
    U = [job(3 + j, act_s, 0, 256 * j, width, R.t_up.at[:, cols_at(j)]) for j in range(3)]
    O = [job(6 + j, hn_s, 0, 256 * j, width, R.t_out.at[:, cols_at(j)]) for j in range(3)]
    Q = job(9, R.g_q, 0, 0, width, R.t_q)
    K = [job(10 + j, p_s, j * lwidth, 0, lwidth, R.t_kv.at[j]) for j in range(4)]

    def keys_values(g):
        def part(t):
            return kv.at[pl.ds(g * pair, pair), pl.ds(pl.multiple_of(t * lats, lats), lats), :]

        sc = R.scd[g]

        def keep():
            dkv_own[pl.ds(g * pair * lats, pair * lats), :] = flat(sc["l0"][pc.yb, pc.xb])

        return Scatter(pc, part, 1024, then=keep, **sc)

    DKV = [keys_values(g) for g in range(n_pairs)]
    lv = Line(pc, R.vtot.at[3], kind=f32, **R.ln_vec)
    V = Vectors(pc, vec, R.vtot, R.vland, R.vs, R.vr, lv)

    vec[...] = jnp.zeros_like(vec)
    lid = R.latent_ids[...].astype(f32)
    lidT[...] = jnp.concatenate([lid, jnp.zeros((128 - rows, lid.shape[1]), f32)], axis=0).T
    loads["lat"].wait()
    loads["wk"].wait()
    loads["wv"].wait()
    l0(0)
    pc.met()
    G[0].p0()
    loads["q"].wait()
    loads["wq"].wait()
    f1(0)
    l0(1)
    G[1].p0()
    f1(1)
    f1(2)
    l0(2)
    G[0].p1()
    G[2].p0()
    loads["c"].wait()
    loads["wd"].wait()
    f1b(0)
    f1b(1)
    f1b(2)
    G[1].p1()
    G[0].p2()
    G[0].p3()
    loads["wo"].wait()
    loads["wu"].wait()
    hooks = {
        1: {
            0: (
                G[2].p1,
                G[1].p2,
            ),
            1: (DKV[0].p1,),
            2: (
                DKV[0].p3,
                DKV[1].p1,
            ),
        },
        3: {
            0: (
                G[2].p2,
                G[1].p3,
                G[0].drain,
            ),
            1: (
                DKV[0].p2,
                G[1].drain,
            ),
            2: (
                DKV[1].p2,
                G[2].drain,
            ),
        },
        5: {
            0: (
                G[2].p3,
                DKV[0].p0,
            ),
            1: (DKV[1].p0,),
            2: (DKV[2].p0,),
        },
    }

    def hook(k, i):
        for p, fns in hooks.get(k, {}).items():

            @pl.when(i == p)
            def _():
                for fn in fns:
                    fn()

    def main(i):
        f2(pair * i)
        f2(pair * i + 1)
        hook(1, i)
        f3(i)
        hook(3, i)
        b2(pair * i)
        b2(pair * i + 1)
        hook(5, i)

    loop(0, n_pairs, main)
    w_down(0)
    DKV[1].p3()
    D[0].p0()
    w_down(1)
    DKV[2].p1()
    D[0].p1()
    D[1].p0()
    w_down(2)
    D[2].p0()
    w_up(0)
    D[1].p1()
    U[0].p0()
    D[2].p1()
    w_up(1)
    U[0].p1()
    U[1].p0()
    w_up(2)
    DKV[2].p2()
    U[1].p1()
    U[2].p0()
    w_out(0)
    D[0].p2()
    O[0].p0()
    D[1].p2()
    U[2].p1()
    D[2].p2()
    O[0].p1()
    U[0].p2()
    DKV[2].p3()
    loop(0, 5, w_kv)
    U[1].p2()
    D[0].p3()
    K[0].p0()
    K[1].p0()
    K[2].p0()
    K[3].p0()
    D[1].p3()
    l1()
    U[2].p2()
    K[0].p1()
    D[2].p3()
    K[1].p1()
    b3(0)
    K[2].p1()
    O[0].p2()
    D[0].up()
    U[0].p3()
    K[3].p1()
    U[1].p3()
    b3(1)
    D[1].up()
    U[2].p3()
    b3(2)
    D[2].up()
    b3(3)
    K[0].p2()
    D[0].mid()
    U[0].up()
    b3(4)
    K[1].p2()
    U[1].up()
    D[1].mid()
    b3(5)
    U[2].up()
    D[2].mid()
    V.p0()
    w_q()
    K[2].p2()
    O[0].p3()
    D[0].dn()
    V.p1()
    U[0].mid()
    U[1].mid()
    D[1].dn()
    K[3].p2()
    Q.p0()
    w_out(1)
    U[2].mid()
    K[0].p3()
    D[2].dn()
    O[1].p0()
    Q.p1()
    K[1].p3()
    w_out(2)
    K[2].p3()
    O[1].p1()
    O[0].up()
    U[0].dn()
    O[2].p0()
    V.p2()
    U[1].dn()
    K[3].p3()
    O[2].p1()
    U[2].dn()
    K[0].up()
    Q.p2()
    O[1].p2()
    O[0].mid()
    K[1].up()
    V.p3()
    O[2].p2()
    K[2].up()
    Q.p3()
    O[1].p3()
    K[0].mid()
    O[0].dn()
    K[3].up()
    K[1].mid()
    O[2].p3()
    V.up()
    Q.up()
    K[2].mid()
    O[1].up()
    K[0].dn()
    K[3].mid()
    O[2].up()
    K[1].dn()
    V.mid()
    Q.mid()
    K[2].dn()
    O[1].mid()
    O[2].mid()
    K[3].dn()
    V.dn()
    Q.dn()
    O[1].dn()
    O[2].dn()
    jobs = [*D, *U, *O, Q, *K]
    for x in jobs:
        x.store()
    t_vec = pltpu.make_async_copy(lv.zo, R.t_vec, R.t_sem.at[len(jobs)])
    lv.result(lambda src: pltpu.make_async_copy(src, R.t_vec, R.t_sem.at[len(jobs)]).start())
    for x in (*jobs, *DKV, V):
        x.drain()
    t_vec.wait()
    staged(R.grad_queries, R.gq_sem, rows - 1, positions)
    for c in put_gl:
        c.wait()


def unpack(*refs):
    n = len(Outs._fields)
    ins, out = refs[:9], Outs(*refs[9 : 9 + n])
    stay, wide, narrow = refs[9 + n : 18 + n], refs[18 + n : -3], refs[-3]
    sem_in, sem_out = refs[-2], refs[-1]
    loads = [pltpu.make_async_copy(a, b, sem_in.at[k]) for k, (a, b) in enumerate(zip(ins, stay))]
    for c in loads:
        c.start()
    t_vec = stay[8]
    outs = (
        out.block_out,
        out.grad_queries,
        out.grad_latents,
        out.grad_down_weight,
        out.grad_up_weight,
        out.grad_out_weight,
        out.grad_query_weight,
        out.grad_key_weight,
        out.grad_value_weight,
    )
    stores = [pltpu.make_async_copy(stay[0], out.block_out, sem_out.at[0])]
    stores += [pltpu.make_async_copy(v, outs[k + 1], sem_out.at[k + 1]) for k, v in enumerate(wide)]
    loads[1].wait()
    half = wide[0].shape[0] // 2
    halves = []
    for j in range(2):
        rs = pl.ds(j * half, half)
        wide[0][rs] = stay[1][rs].astype(f32)
        halves.append(pltpu.make_async_copy(wide[0].at[rs], out.grad_queries.at[rs], narrow.at[j]))
        halves[-1].start()
    stores = stores[:1] + stores[2:]
    loads[0].wait()
    stores[0].start()
    for k in range(1, 6):
        loads[k + 1].wait()
        wide[k][...] = stay[k + 1][...].astype(f32)
        stores[k].start()
    loads[7].wait()
    wide[6][...] = stay[7][0].astype(f32)
    stores[6].start()
    for k in range(3):
        wide[7][:, 256 * k : 256 * (k + 1)] = stay[7][k + 1].astype(f32)
    stores[7].start()
    loads[8].wait()
    vectors = (
        out.grad_gain_query,
        out.grad_shift_query,
        out.grad_gain_hidden,
        out.grad_shift_hidden,
        out.grad_bias_up,
        out.grad_bias_down,
        out.grad_gain_latent,
        out.grad_shift_latent,
    )
    for t in range(8):

        @pl.when(lax.axis_index("seq") == t)
        def _():
            for k, ref in enumerate(vectors):
                m = ref.shape[0]
                ref[...] = t_vec[k, m * t : m * (t + 1)]

    for c in stores + halves:
        c.wait()


class Args(NamedTuple):
    queries: Any
    latents: Any
    query_ids: Any
    latent_ids: Any
    query_weight: Any
    key_weight: Any
    value_weight: Any
    out_weight: Any
    up_weight: Any
    down_weight: Any
    gain_query: Any
    shift_query: Any
    gain_latent: Any
    shift_latent: Any
    gain_hidden: Any
    shift_hidden: Any
    bias_up: Any
    bias_down: Any
    cotangent: Any


class Outs(NamedTuple):
    block_out: Any
    grad_queries: Any
    grad_latents: Any
    grad_query_weight: Any
    grad_key_weight: Any
    grad_value_weight: Any
    grad_out_weight: Any
    grad_up_weight: Any
    grad_down_weight: Any
    grad_gain_query: Any
    grad_shift_query: Any
    grad_gain_latent: Any
    grad_shift_latent: Any
    grad_gain_hidden: Any
    grad_shift_hidden: Any
    grad_bias_up: Any
    grad_bias_down: Any


def body(n_rows, n_seq, *args):
    A = Args(*args)
    rows, pos, width = A.queries.shape
    lats, lwidth = A.latents.shape[1:]
    nl = lats * n_seq
    F_ = lambda *s: jax.ShapeDtypeStruct(s, f32)
    wide, vec, lvec = F_(width // n_seq, width), F_(width // n_seq), F_(lwidth // n_seq)
    out = Outs(
        block_out=jax.ShapeDtypeStruct((rows, pos, width), bf16),
        grad_queries=F_(rows, pos, width),
        grad_latents=F_(rows, lats, lwidth),
        grad_query_weight=F_(width // n_seq, 256),
        grad_key_weight=F_(lwidth // n_seq, 256),
        grad_value_weight=F_(lwidth // n_seq, width),
        grad_out_weight=wide,
        grad_up_weight=wide,
        grad_down_weight=wide,
        grad_gain_query=vec,
        grad_shift_query=vec,
        grad_gain_latent=lvec,
        grad_shift_latent=lvec,
        grad_gain_hidden=vec,
        grad_shift_hidden=vec,
        grad_bias_up=vec,
        grad_bias_down=vec,
    )
    V = lambda *s: pltpu.VMEM(s, bf16)
    F = lambda *s: pltpu.VMEM(s, f32)
    dma = lambda *s: pltpu.SemaphoreType.DMA(s)
    tok = V(rows, pos, width)
    tok2 = V(rows * pos, width)
    tokT = V(width, rows * pos)
    scratch = dict(
        q_v=tok,
        c_v=tok,
        lat_v=V(rows, lats, lwidth),
        wq_v=V(width, 256),
        wk_v=V(lwidth, 256),
        wv_v=V(lwidth, width),
        wo_v=V(width, width),
        wu_v=V(width, width),
        wd_v=V(width, width),
        kv=V(rows, nl, 1024),
        qn=tok2,
        qp=V(rows * pos, 256),
        s_scr=F(HEADS, nl, pos),
        ds_scr=V(HEADS * nl, pos),
        inv=F(rows, HEADS, pos),
        p=V(rows * HEADS * nl, pos),
        mix=tokT,
        hn=tok2,
        act=tok2,
        dpre=tok2,
        dres=tok2,
        dm=tokT,
        dq=V(rows * pos, 256),
        lidT=F(nl, 128),
        ln=V(rows * lats, lwidth),
        dkv_own=V(rows * lats, 1024),
        vec=F(8, 8, lwidth),
        vtot=F(4, 8, lwidth),
        vland=F(3, 8, lwidth),
        vs=dma(3),
        vr=dma(3),
        bo_sem=dma(width // 256),
        gq_sem=dma(width // 256),
        gl_sem=dma(lwidth // 256),
        t_sem=dma(15),
        load_sem=dma(9),
        ag_s=dma(rows // 2, 9),
        ag_r=dma(rows // 2, 9),
        g_down=V(width, width),
        g_q=V(width, 256),
        ln_vec=line_scratch((8, lwidth), f32),
    )
    lead, llead = (width // n_seq,), (lwidth // n_seq,)
    shapes = [lead] * 10 + [llead] * 4
    scratch["sc"] = [scatter_scratch(x, 256) for x in shapes]
    scratch["li"] = [line_scratch((*x, 256), bf16) for x in shapes]
    scratch["scd"] = [scatter_scratch((2, lats), 1024) for _ in range(rows // 2)]
    any_ = pl.BlockSpec(memory_space=pl.ANY)
    vm = pl.BlockSpec(memory_space=pltpu.VMEM)
    far = (A.queries, A.cotangent, A.latents, *A[4:10])
    in_specs = [any_ if any(a is f for f in far) else vm for a in A]
    sds = jax.ShapeDtypeStruct
    mid = dict(
        block_out=sds((rows * pos, width), bf16),
        grad_queries=sds((rows * pos, width), bf16),
        grad_latents=sds((rows * lats, lwidth), bf16),
        t_down=sds(wide.shape, bf16),
        t_up=sds(wide.shape, bf16),
        t_out=sds(wide.shape, bf16),
        t_q=sds((width // n_seq, 256), bf16),
        t_kv=sds((4, lwidth // n_seq, 256), bf16),
        t_vec=sds((8, lwidth), f32),
    )
    names = (*Args._fields, *mid, *scratch)
    flops = 2 * rows * pos * width * width * 14
    got = pl.pallas_call(
        functools.partial(kernel, n_rows, names),
        out_shape=tuple(mid.values()),
        in_specs=in_specs,
        out_specs=(any_,) * len(mid),
        scratch_shapes=list(scratch.values()),
        compiler_params=pltpu.CompilerParams(
            collective_id=0, has_side_effects=True, vmem_limit_bytes=64 << 20
        ),
        cost_estimate=pl.CostEstimate(flops=flops, bytes_accessed=24 << 20, transcendentals=0),
    )(*A)
    three = lambda x: x.reshape(rows, -1, x.shape[-1])
    got = (three(got[0]), three(got[1]), three(got[2]), *got[3:])
    return pl.pallas_call(
        unpack,
        out_shape=tuple(out),
        in_specs=[any_] * 9,
        out_specs=(any_,) * 9 + (vm,) * 8,
        scratch_shapes=[pltpu.VMEM(x.shape, x.dtype) for x in got]
        + [
            pltpu.VMEM(o.shape, f32)
            for o in (
                out.grad_queries,
                out.grad_latents,
                wide,
                wide,
                wide,
                out.grad_query_weight,
                out.grad_key_weight,
                out.grad_value_weight,
            )
        ]
        + [dma(2), dma(9), dma(9)],
        compiler_params=pltpu.CompilerParams(vmem_limit_bytes=64 << 20),
        cost_estimate=pl.CostEstimate(flops=0, bytes_accessed=18 << 20, transcendentals=0),
    )(*got)


def solution(mesh):
    seq = P("rows", "seq", None)
    rep = P()
    in_specs = (seq, seq, P("rows", "seq"), P("rows", None)) + (rep,) * 14 + (seq,)
    out_specs = (seq,) * 3 + (P("seq", None),) * 6 + (P("seq"),) * 8
    return jax.shard_map(
        functools.partial(body, mesh.shape["rows"], mesh.shape["seq"]),
        mesh=mesh,
        in_specs=in_specs,
        out_specs=out_specs,
        check_vma=False,
    )
```

```python
import functools
import types
from typing import Any, NamedTuple

import jax
import jax.numpy as jnp
from jax import lax
from jax.experimental import pallas as pl
from jax.experimental.pallas import tpu as pltpu
from jax.sharding import PartitionSpec as P

HEADS = 8
HDIM = 96
QKDIM = 32
EPS = 1e-05
SCALE = QKDIM ** (-0.5)
MESH = pl.DeviceIdType.MESH
f32, bf16 = jnp.float32, jnp.bfloat16


def dg(a, b, ca, cb):
    return lax.dot_general(a, b, (((ca,), (cb,)), ((), ())), preferred_element_type=f32)


def norm(x):
    mean = jnp.mean(x, -1, keepdims=True)
    cen = x - mean
    inv = lax.rsqrt(jnp.mean(cen * cen, -1, keepdims=True) + EPS)
    return cen * inv, inv


def norm_back(grad, gain, hat, inv):
    g = grad * gain
    return inv * (
        g - jnp.mean(g, -1, keepdims=True) - hat * jnp.mean(g * hat, -1, keepdims=True)
    )


def row_sum(x):
    n, w = x.shape
    return jnp.sum(x.reshape(n // 8, 8, w), axis=0)


def flat(x):
    return x.reshape(-1, x.shape[-1])


def add(a, b):
    return (a.astype(f32) + b.astype(f32)).astype(bf16)


class Place:
    def __init__(self, n_rows):
        self.n = n_rows
        self.s = lax.axis_index("seq")
        self.r = lax.axis_index("rows")
        self.core = lax.rem(self.s, 2)
        self.chip = self.s // 2
        self.xc = self.chip + 1 - 2 * lax.rem(self.chip, 2)
        self.yc = lax.rem(self.chip + 2, 4)
        self.dc = lax.rem(self.xc + 2, 4)
        self.xb, self.yb = lax.rem(self.chip, 2), self.chip // 2
        self.sib = (self.s + 1 - 2 * self.core, self.r)
        self.xn = (2 * self.xc + self.core, self.r)
        self.yn = (2 * self.yc + self.core, self.r)
        half = n_rows // 2
        self.left = self.r < half
        self.mid = (self.r == half - 1) | (self.r == half)
        self.not_end = (self.r != 0) & (self.r != n_rows - 1)
        step = jnp.where(self.left, 1, -1)
        self.inner = (self.s, lax.rem(self.r + step + n_rows, n_rows))
        self.outer = (self.s, lax.rem(self.r - step + n_rows, n_rows))

    def greet(self):
        up = (self.s, lax.rem(self.r + 1, self.n))
        down = (self.s, lax.rem(self.r + self.n - 1, self.n))
        self.bar = pltpu.get_barrier_semaphore()
        for peer in (self.sib, self.xn, self.yn, up, down):
            pl.semaphore_signal(self.bar, inc=1, device_id=peer, device_id_type=MESH)

    def met(self):
        pl.semaphore_wait(self.bar, 5)


def rcopy(src, dst, ssem, rsem, peer):
    return pltpu.make_async_remote_copy(
        src_ref=src, dst_ref=dst, send_sem=ssem, recv_sem=rsem, device_id=peer, device_id_type=MESH
    )


class Line:
    def __init__(self, pc, src, zo, zi, ssem, rsem, kind):
        zt = zo
        self.pc, self.src, self.zo, self.zi, self.zt, self.kind = pc, src, zo, zi, zt, kind
        self.up_c = rcopy(src, zo, ssem.at[0], rsem.at[0], pc.inner)
        self.cross_c = rcopy(src, zi, ssem.at[1], rsem.at[1], pc.inner)
        self.down_mid = rcopy(zt, zi, ssem.at[2], rsem.at[1], pc.outer)
        self.down_far = rcopy(zi, zi, ssem.at[2], rsem.at[1], pc.outer)

    def plus(self, a, b):
        return (a.astype(f32) + b.astype(f32)).astype(self.kind)

    def send(self):
        pc = self.pc
        pl.when(jnp.logical_not(pc.not_end) & jnp.logical_not(pc.mid))(self.up_c.start)

    def up(self):
        pc = self.pc

        @pl.when(pc.not_end)
        def _():
            self.up_c.wait_recv()
            self.src[...] = self.plus(self.src[...], self.zo[...])

        pl.when(pc.mid)(self.cross_c.start)
        pl.when(jnp.logical_not(pc.mid) & pc.not_end)(self.up_c.start)

    def middle(self):
        pc = self.pc

        @pl.when(pc.mid)
        def _():
            self.cross_c.wait_recv()
            self.zt[...] = self.plus(self.src[...], self.zi[...])

        pl.when(pc.mid & pc.not_end)(self.down_mid.start)

    def down(self):
        pc = self.pc
        pl.when(jnp.logical_not(pc.mid))(self.cross_c.wait_recv)
        pl.when(jnp.logical_not(pc.mid) & pc.not_end)(self.down_far.start)

    def result(self, write):
        pc = self.pc
        pl.when(pc.mid)(lambda: write(self.zt))
        pl.when(jnp.logical_not(pc.mid))(lambda: write(self.zi))

    def drain(self):
        pc = self.pc
        pl.when(pc.mid)(self.cross_c.wait_send)
        pl.when(jnp.logical_not(pc.mid))(self.up_c.wait_send)
        pl.when(pc.mid & pc.not_end)(self.down_mid.wait_send)
        pl.when(jnp.logical_not(pc.mid) & pc.not_end)(self.down_far.wait_send)


class Scatter:
    def __init__(self, pc, part, width, l0, la, lb, la2, lb2, ssem, rsem, then=None):
        self.pc, self.part, self.l0, self.then = pc, part, l0, then
        self.la, self.lb, self.la2, self.lb2 = la, lb, la2, lb2
        h = width // 2
        A, B = self.A, self.B = pl.ds(0, h), pl.ds(h, h)
        lead = (slice(None),) * (len(l0.shape) - 3)
        xb, yb = pc.xb, pc.yb

        def blk(y, x, cols):
            return l0.at[(y, x, *lead, cols)]

        self.blk = blk
        other = 1 - pc.core
        self.pair = [
            rcopy(part(2 * q + other), l0.at[q // 2, q % 2], ssem.at[q], rsem.at[q], pc.sib)
            for q in range(4)
        ]
        every = slice(None)
        self.first = [
            rcopy(blk(every, 1 - xb, A), la, ssem.at[4], rsem.at[4], pc.xn),
            rcopy(blk(1 - yb, every, B), lb, ssem.at[5], rsem.at[5], pc.yn),
        ]
        self.second = [
            rcopy(blk(1 - yb, xb, A), la2, ssem.at[6], rsem.at[6], pc.yn),
            rcopy(blk(yb, 1 - xb, B), lb2, ssem.at[7], rsem.at[7], pc.xn),
        ]

    def p0(self):
        for c in self.pair:
            c.start()

    def p1(self):
        for q in range(4):
            self.pair[q].wait_recv()
            own = self.part(2 * q + self.pc.core)[...]
            self.l0[q // 2, q % 2] = add(self.l0[q // 2, q % 2], own)
        for c in self.first:
            c.start()

    def into(self, y, x, cols, got):
        v = self.blk(y, x, cols)
        v[...] = add(v[...], got[...])

    def p2(self):
        xb, yb = self.pc.xb, self.pc.yb
        self.first[0].wait_recv()
        self.into(1 - yb, xb, self.A, self.la.at[1 - yb])
        self.second[0].start()
        self.first[1].wait_recv()
        self.into(yb, 1 - xb, self.B, self.lb.at[1 - xb])
        self.second[1].start()
        self.into(yb, xb, self.A, self.la.at[yb])
        self.into(yb, xb, self.B, self.lb.at[xb])

    def p3(self):
        for c, cols, got in zip(self.second, (self.A, self.B), (self.la2, self.lb2)):
            c.wait_recv()
            self.into(self.pc.yb, self.pc.xb, cols, got)
        self.then()

    def drain(self):
        for c in self.pair + self.first + self.second:
            c.wait_send()


class Job:
    def __init__(self, scatter, line, out, sem):
        self.scatter, self.line = scatter, line
        scatter.then = line.send
        self.p0, self.p1, self.p2, self.p3 = scatter.p0, scatter.p1, scatter.p2, scatter.p3
        self.up, self.mid, self.dn = line.up, line.middle, line.down
        self.out, self.sem = out, sem

    def store(self):
        self.line.result(lambda src: pltpu.make_async_copy(src, self.out, self.sem).start())

    def drain(self):
        pltpu.make_async_copy(self.line.zo, self.out, self.sem).wait()
        self.scatter.drain()
        self.line.drain()


class Vectors:
    def __init__(self, pc, vec, tot, land, ssem, rsem, line):
        self.vec, self.tot, self.land, self.line = vec, tot, land, line
        self.steps = [
            rcopy(tot.at[k], land.at[k], ssem.at[k], rsem.at[k], peer)
            for k, peer in enumerate((pc.sib, pc.xn, pc.yn))
        ]
        self.up, self.mid, self.dn = line.up, line.middle, line.down

    def p0(self):
        self.tot[0] = jnp.sum(self.vec[...], axis=1)
        self.steps[0].start()

    def take(self, k):
        self.steps[k].wait_recv()
        self.tot[k + 1] = self.tot[k] + self.land[k]

    def p1(self):
        self.take(0)
        self.steps[1].start()

    def p2(self):
        self.take(1)
        self.steps[2].start()

    def p3(self):
        self.take(2)
        self.line.send()

    def drain(self):
        for c in self.steps:
            c.wait_send()
        self.line.drain()


def scatter_scratch(lead, width):
    half = width // 2
    return dict(
        l0=pltpu.VMEM((2, 2, *lead, width), bf16),
        la=pltpu.VMEM((2, *lead, half), bf16),
        lb=pltpu.VMEM((2, *lead, half), bf16),
        la2=pltpu.VMEM((*lead, half), bf16),
        lb2=pltpu.VMEM((*lead, half), bf16),
        ssem=pltpu.SemaphoreType.DMA((8,)),
        rsem=pltpu.SemaphoreType.DMA((8,)),
    )


def line_scratch(shape, kind):
    return dict(
        zo=pltpu.VMEM(shape, kind),
        zi=pltpu.VMEM(shape, kind),
        ssem=pltpu.SemaphoreType.DMA((3,)),
        rsem=pltpu.SemaphoreType.DMA((2,)),
    )


class Gather:
    def __init__(self, pc, kv, rows, ssem, rsem):
        def blk(t, cols=slice(None)):
            return kv.at[rows, pl.ds(pl.multiple_of(t * 32, 32), 32), cols]

        h = kv.shape[-1] // 2
        A, B = pl.ds(0, h), pl.ds(h, h)
        ds_ = 2 * pc.dc + pc.core

        def copy(k, ref, peer):
            return rcopy(ref, ref, ssem.at[k], rsem.at[k], peer)

        self.own = [copy(0, blk(pc.s), pc.sib), copy(1, blk(pc.s), pc.xn), copy(2, blk(pc.s), pc.yn)]
        self.from_x = [copy(3, blk(pc.xn[0], A), pc.yn), copy(4, blk(pc.xn[0]), pc.sib)]
        self.from_y = [copy(5, blk(pc.yn[0], B), pc.xn), copy(6, blk(pc.yn[0]), pc.sib)]
        self.from_d = [copy(7, blk(ds_, A), pc.sib), copy(8, blk(ds_, B), pc.sib)]

    def p0(self):
        for c in self.own[::-1]:
            c.start()

    def p1(self):
        self.own[1].wait_recv()
        for c in self.from_x:
            c.start()
        self.own[2].wait_recv()
        for c in self.from_y:
            c.start()

    def p2(self):
        self.from_x[0].wait_recv()
        self.from_d[0].start()
        self.from_y[0].wait_recv()
        self.from_d[1].start()

    def p3(self):
        for c in (self.own[0], self.from_x[1], self.from_y[1], *self.from_d):
            c.wait_recv()

    def drain(self):
        for c in self.own + self.from_x + self.from_y + self.from_d:
            c.wait_send()


def kernel(n_rows, names, *refs):
    R = types.SimpleNamespace(**dict(zip(names, refs, strict=True)))
    q_hbm, c_hbm, lat_hbm = R.queries, R.cotangent, R.latents
    line_of = lambda ref: ref[...].reshape(1, -1)
    q_ref, c_ref, lat_ref = R.q_v, R.c_v, R.lat_v
    wq, wk, wv, wo, wu, wd = R.wq_v, R.wk_v, R.wv_v, R.wo_v, R.wu_v, R.wd_v
    kv, qn_s, qp_s, p_s, mix_s, hn_s = R.kv, R.qn, R.qp, R.p, R.mix, R.hn
    act_s, dpre_s, dres_s, dm_s, dq_s = R.act, R.dpre, R.dres, R.dm, R.dq
    s_scr, ds_scr, inv_s = R.s_scr, R.ds_scr, R.inv
    lidT, ln_s, dkv_own, vec = R.lidT, R.ln, R.dkv_own, R.vec
    rows, positions, width = q_ref.shape
    lats, lwidth = lat_ref.shape[1:]
    pair = 2
    n_pairs = rows // pair
    tokens = rows * positions
    span = positions * pair

    loads = {}
    for k, (name, src, dst) in enumerate(
        [
            ("lat", lat_hbm, lat_ref),
            ("wk", R.key_weight, wk),
            ("wv", R.value_weight, wv),
            ("q", q_hbm, q_ref),
            ("wq", R.query_weight, wq),
            ("wo", R.out_weight, wo),
            ("wu", R.up_weight, wu),
            ("wd", R.down_weight, wd),
            ("c", c_hbm, c_ref),
        ]
    ):
        loads[name] = pltpu.make_async_copy(src, dst, R.load_sem.at[k])
        loads[name].start()

    pc = Place(n_rows)
    pc.greet()

    def loop(first, last, body):
        def step(i, carry):
            body(i)
            return carry

        lax.fori_loop(first, last, step, 0)

    lane1 = lax.broadcasted_iota(jnp.int32, (1, 128), 1)

    def head_mask(hh, kind):
        return ((lane1 >= QKDIM * hh) & (lane1 < QKDIM * (hh + 1))).astype(kind)

    own = pl.ds(pl.multiple_of(pc.s * lats, lats), lats)

    def l0(g):
        rs = pl.ds(g * pair, pair)
        hat, _ = norm(flat(lat_ref[rs]).astype(f32))
        ln = (hat * line_of(R.gain_latent) + line_of(R.shift_latent)).astype(bf16)
        ln_s[pl.ds(g * pair * lats, pair * lats), :] = ln
        k = dg(ln, wk[...], 1, 0).astype(bf16)
        v = dg(ln, wv[...], 1, 0).astype(bf16)
        kv[rs, own, 0:256] = k.reshape(pair, lats, -1)
        kv[rs, own, 256:1024] = v.reshape(pair, lats, -1)

    def at(i):
        return pl.ds(pl.multiple_of(i * span, span), span)

    def row(r):
        return pl.ds(pl.multiple_of(r * positions, positions), positions)

    def f1(i):
        hat, _ = norm(flat(q_ref[pl.ds(i * pair, pair)]).astype(f32))
        qn = (hat * line_of(R.gain_query) + line_of(R.shift_query)).astype(bf16)
        qn_s[at(i), :] = qn
        qp_s[at(i), :] = (dg(qn, wq[...], 1, 0) * SCALE).astype(bf16)

    def f1b(i):
        c = flat(c_ref[pl.ds(i * pair, pair)])
        vec[5, :, :width] += row_sum(c.astype(f32))
        dpre_s[at(i), :] = dg(c, wd[...], 1, 1).astype(bf16)

    def row8(r):
        return pl.ds(pl.multiple_of(r * HEADS * 256, HEADS * 256), HEADS * 256)

    def f2(r):
        k = kv[r, :, :256]
        vT = kv[r, :, 256:].T
        lane = lax.broadcasted_iota(jnp.int32, (256, 128), 1)
        col = jnp.sum(jnp.where(lane == r, lidT[...], 0.0), axis=1, keepdims=True)
        allowed = col == R.query_ids[pl.ds(r, 1), :].astype(f32)
        for g in range(2):
            kb = k[:, 128 * g : 128 * g + 128]
            km = jnp.concatenate([kb * head_mask(hh, bf16) for hh in range(4)], axis=0)
            sg = dg(km, qp_s[row(r), 128 * g : 128 * g + 128], 1, 1)
            for hh in range(4):
                s_scr[4 * g + hh] = sg[256 * hh : 256 * (hh + 1)]
        p_r = p_s.at[row8(r)]
        for h in range(HEADS):
            s = jnp.where(allowed, s_scr[h], -1e30)
            e = jnp.exp(s - jnp.max(s, axis=0, keepdims=True))
            p_r[256 * h : 256 * (h + 1), :] = e.astype(bf16)
            inv_s[r, h : h + 1, :] = 1.0 / jnp.sum(e, axis=0, keepdims=True)
        mix_r = mix_s.at[:, row(r)]
        for h in range(HEADS):
            hs = slice(HDIM * h, HDIM * (h + 1))
            got = dg(vT[hs], p_r[256 * h : 256 * (h + 1), :], 1, 0)
            mix_r[hs, :] = (got * inv_s[r, h : h + 1, :]).astype(bf16)

    def chunks(dst, sems, i, n):
        return [
            pltpu.make_async_copy(
                ds_scr.at[pl.ds(k * n, n)],
                dst.at[pl.ds(pl.multiple_of(i * n, n), n), pl.ds(256 * k, 256)],
                sems.at[k],
            )
            for k in range(width // 256)
        ]

    def stage(value, dst, sems, i, n):
        for k, c in enumerate(chunks(dst, sems, i, n)):
            ds_scr[n * k : n * (k + 1), :] = value[:, 256 * k : 256 * (k + 1)].astype(bf16)
            c.start()

    def staged(dst, sems, i, n):
        for c in chunks(dst, sems, i, n):
            c.wait()

    def f3(i):
        rs = pl.ds(i * pair, pair)
        resid = flat(q_ref[rs]).astype(f32) + dg(mix_s[:, at(i)], wo[...], 0, 0)
        hat, inv = norm(resid)
        hn = (hat * line_of(R.gain_hidden) + line_of(R.shift_hidden)).astype(bf16)
        hn_s[at(i), :] = hn
        pre = dg(hn, wu[...], 1, 0) + line_of(R.bias_up)
        phi = 0.5 * (1.0 + lax.erf(pre * (0.5**0.5)))
        act = (pre * phi).astype(bf16)
        act_s[at(i), :] = act
        slope = phi + pre * (jnp.exp(-0.5 * pre * pre) * 0.3989422804014327)
        dpre = (dpre_s[at(i), :].astype(f32) * slope).astype(bf16)
        dpre_s[at(i), :] = dpre

        out = resid + dg(act, wd[...], 1, 0) + line_of(R.bias_down)
        stage(out, R.block_out, R.bo_sem, i, span)
        vec[4, :, :width] += row_sum(dpre.astype(f32))
        dh = dg(dpre, wu[...], 1, 1)
        vec[2, :, :width] += row_sum(dh * hat)
        vec[3, :, :width] += row_sum(dh)
        cf = flat(c_ref[rs]).astype(f32)
        dlow = (norm_back(dh, line_of(R.gain_hidden), hat, inv) + cf).astype(bf16)
        dres_s[at(i), :] = dlow
        dm_s[:, at(i)] = dg(wo[...], dlow, 1, 1).astype(bf16)
        staged(R.block_out, R.bo_sem, i, span)

    def b2(r):
        k = kv[r, :, :256]
        kT = k.T
        v = kv[r, :, 256:]
        dvs, dqs, dks = [], [], []
        p_r, dm_r, qp_r = p_s.at[row8(r)], dm_s.at[:, row(r)], qp_s.at[row(r)]
        for h in range(HEADS):
            hs = slice(HDIM * h, HDIM * (h + 1))
            dm_r[hs, :] = (dm_r[hs, :].astype(f32) * inv_s[r, h : h + 1, :]).astype(bf16)
        for h in range(HEADS):
            hs = slice(HDIM * h, HDIM * (h + 1))
            s_scr[h] = dg(v[:, hs], dm_r[hs, :], 1, 0)
        for h in range(HEADS):
            hs = slice(HDIM * h, HDIM * (h + 1))
            dvs.append(dg(dm_r[hs, :], p_r[256 * h : 256 * (h + 1), :], 1, 1).astype(bf16))
        for h in range(HEADS):
            e = p_r[256 * h : 256 * (h + 1), :].astype(f32)
            ed = e * s_scr[h]
            ds = ed - e * (jnp.sum(ed, axis=0, keepdims=True) * inv_s[r, h : h + 1, :])
            ds_scr[256 * h : 256 * (h + 1), :] = ds.astype(bf16)
        for g in range(2):
            t = dg(ds_scr[1024 * g : 1024 * (g + 1), :], qp_r[:, 128 * g : 128 * g + 128], 1, 0)
            dks.append(sum(t[256 * hh : 256 * (hh + 1)] * head_mask(hh, f32) for hh in range(4)))
        for h in range(HEADS):
            kh = kT[QKDIM * h : QKDIM * (h + 1)]
            dqs.append(dg(kh, ds_scr[256 * h : 256 * (h + 1), :], 1, 0).astype(bf16))
        dq_s[row(r), :] = jnp.concatenate(dqs, axis=0).T
        kv[r, :, :128] = dks[0].astype(bf16)
        kv[r, :, 128:256] = dks[1].astype(bf16)
        kv[r, :, 256:] = jnp.concatenate(dvs, axis=0).T

    def b3(r):
        dqn = dg(dq_s[row(r), :], wq[...], 1, 1) * SCALE
        hat, inv = norm(q_ref[r].astype(f32))
        vec[0, :, :width] += row_sum(dqn * hat)
        vec[1, :, :width] += row_sum(dqn)

        got = norm_back(dqn, line_of(R.gain_query), hat, inv) + dres_s[row(r), :].astype(f32)

        if r >= 1:
            staged(R.grad_queries, R.gq_sem, r - 1, positions)

        stage(got, R.grad_queries, R.gq_sem, r, positions)

    def cols(j):
        return pl.ds(pl.multiple_of(j * 256, 256), 256)

    def cols_at(j):
        return pl.ds(256 * j, 256)

    def w_down(j):
        R.g_down[:, cols_at(j)] = dg(act_s[...], flat(c_ref[:, :, cols_at(j)]), 0, 0).astype(bf16)

    g_up, g_out = act_s.at[pl.ds(0, width)], hn_s.at[pl.ds(0, width)]

    def w_up(j):
        g_up[:, cols_at(j)] = dg(hn_s[...], dpre_s[:, cols_at(j)], 0, 0).astype(bf16)

    def w_out(j):
        g_out[:, cols_at(j)] = dg(mix_s[...], dres_s[:, cols_at(j)], 1, 0).astype(bf16)

    def w_q():
        R.g_q[...] = (dg(qn_s[...], dq_s[...], 0, 0) * SCALE).astype(bf16)

    def w_kv(j):
        got = dg(ln_s[:, cols(j)], dkv_own[...], 0, 0).astype(bf16)
        for k in range(4):
            to = pl.ds(pl.multiple_of(k * lwidth + j * 256, 256), 256)
            p_s[to, :] = got[:, 256 * k : 256 * (k + 1)]

    put_gl = [
        pltpu.make_async_copy(
            ds_scr.at[pl.ds(1024 + k * rows * lats, rows * lats)], R.grad_latents.at[:, pl.ds(256 * k, 256)], R.gl_sem.at[k]
        )
        for k in range(lwidth // 256)
    ]

    def l1():
        d = dg(dkv_own[:, :256], wk[...], 1, 1) + dg(dkv_own[:, 256:], wv[...], 1, 1)
        hat, inv = norm(flat(lat_ref[...]).astype(f32))
        vec[6] += row_sum(d * hat)
        vec[7] += row_sum(d)
        got = norm_back(d, line_of(R.gain_latent), hat, inv)
        for k, c in enumerate(put_gl):
            ds_scr[1024 + k * rows * lats : 1024 + (k + 1) * rows * lats, :] = got[:, 256 * k : 256 * (k + 1)].astype(bf16)
            c.start()

    G = [Gather(pc, kv, pl.ds(g * pair, pair), R.ag_s.at[g], R.ag_r.at[g]) for g in range(n_pairs)]

    def job(k, ref, lo, c0, height, out):
        block = height // 8

        def part(t):
            return ref.at[pl.ds(pl.multiple_of(lo + t * block, 32), block), pl.ds(c0, 256)]

        sc = R.sc[k]
        ln = Line(pc, sc["l0"].at[pc.yb, pc.xb], kind=bf16, **R.li[k])
        return Job(Scatter(pc, part, 256, **sc), ln, out, R.t_sem.at[k])

    D = [job(j, R.g_down, 0, 256 * j, width, R.t_down.at[:, cols_at(j)]) for j in range(3)]
    U = [job(3 + j, act_s, 0, 256 * j, width, R.t_up.at[:, cols_at(j)]) for j in range(3)]
    O = [job(6 + j, hn_s, 0, 256 * j, width, R.t_out.at[:, cols_at(j)]) for j in range(3)]
    Q = job(9, R.g_q, 0, 0, width, R.t_q)
    K = [job(10 + j, p_s, j * lwidth, 0, lwidth, R.t_kv.at[j]) for j in range(4)]

    def keys_values(g):
        def part(t):
            return kv.at[pl.ds(g * pair, pair), pl.ds(pl.multiple_of(t * lats, lats), lats), :]

        sc = R.scd[g]

        def keep():
            dkv_own[pl.ds(g * pair * lats, pair * lats), :] = flat(sc["l0"][pc.yb, pc.xb])

        return Scatter(pc, part, 1024, then=keep, **sc)

    DKV = [keys_values(g) for g in range(n_pairs)]
    lv = Line(pc, R.vtot.at[3], kind=f32, **R.ln_vec)
    V = Vectors(pc, vec, R.vtot, R.vland, R.vs, R.vr, lv)

    vec[...] = jnp.zeros_like(vec)
    lid = R.latent_ids[...].astype(f32)
    lidT[...] = jnp.concatenate([lid, jnp.zeros((128 - rows, lid.shape[1]), f32)], axis=0).T
    loads["lat"].wait()
    loads["wk"].wait()
    loads["wv"].wait()
    l0(0)
    pc.met()
    G[0].p0()
    loads["q"].wait()
    loads["wq"].wait()
    f1(0)
    l0(1)
    G[1].p0()
    f1(1)
    f1(2)
    l0(2)
    G[0].p1()
    G[2].p0()
    loads["c"].wait()
    loads["wd"].wait()
    f1b(0)
    f1b(1)
    f1b(2)
    G[1].p1()
    G[0].p2()
    G[0].p3()
    loads["wo"].wait()
    loads["wu"].wait()
    hooks = {
        1: {
            0: (
                G[2].p1,
                G[1].p2,
            ),
            1: (DKV[0].p1,),
            2: (
                DKV[0].p3,
                DKV[1].p1,
            ),
        },
        3: {
            0: (
                G[2].p2,
                G[1].p3,
                G[0].drain,
            ),
            1: (
                DKV[0].p2,
                G[1].drain,
            ),
            2: (
                DKV[1].p2,
                G[2].drain,
            ),
        },
        5: {
            0: (
                G[2].p3,
                DKV[0].p0,
            ),
            1: (DKV[1].p0,),
            2: (DKV[2].p0,),
        },
    }

    def hook(k, i):
        for p, fns in hooks.get(k, {}).items():

            @pl.when(i == p)
            def _():
                for fn in fns:
                    fn()

    def main(i):
        f2(pair * i)
        f2(pair * i + 1)
        hook(1, i)
        f3(i)
        hook(3, i)
        b2(pair * i)
        b2(pair * i + 1)
        hook(5, i)

    loop(0, n_pairs, main)
    w_down(0)
    DKV[1].p3()
    D[0].p0()
    w_down(1)
    DKV[2].p1()
    D[0].p1()
    D[1].p0()
    w_down(2)
    D[2].p0()
    w_up(0)
    D[1].p1()
    U[0].p0()
    D[2].p1()
    w_up(1)
    U[0].p1()
    U[1].p0()
    w_up(2)
    DKV[2].p2()
    U[1].p1()
    U[2].p0()
    w_out(0)
    D[0].p2()
    O[0].p0()
    D[1].p2()
    U[2].p1()
    D[2].p2()
    O[0].p1()
    U[0].p2()
    w_out(1)
    O[1].p0()
    w_out(2)
    O[2].p0()
    DKV[2].p3()
    loop(0, 5, w_kv)
    U[1].p2()
    D[0].p3()
    K[0].p0()
    K[1].p0()
    K[2].p0()
    K[3].p0()
    D[1].p3()
    l1()
    U[2].p2()
    K[0].p1()
    D[2].p3()
    K[1].p1()
    w_q()
    Q.p0()
    b3(0)
    K[2].p1()
    O[0].p2()
    D[0].up()
    U[0].p3()
    K[3].p1()
    O[1].p1()
    O[2].p1()
    Q.p1()
    U[1].p3()
    b3(1)
    D[1].up()
    U[2].p3()
    b3(2)
    D[2].up()
    b3(3)
    K[0].p2()
    D[0].mid()
    U[0].up()
    b3(4)
    K[1].p2()
    U[1].up()
    D[1].mid()
    b3(5)
    U[2].up()
    D[2].mid()
    V.p0()
    K[2].p2()
    O[0].p3()
    D[0].dn()
    V.p1()
    U[0].mid()
    U[1].mid()
    D[1].dn()
    K[3].p2()
    O[1].p2()
    O[2].p2()
    Q.p2()
    U[2].mid()
    K[0].p3()
    D[2].dn()
    K[1].p3()
    K[2].p3()
    O[0].up()
    U[0].dn()
    V.p2()
    U[1].dn()
    K[3].p3()
    U[2].dn()
    K[0].up()
    O[0].mid()
    K[1].up()
    V.p3()
    K[2].up()
    Q.p3()
    O[1].p3()
    K[0].mid()
    O[0].dn()
    K[3].up()
    K[1].mid()
    O[2].p3()
    V.up()
    Q.up()
    K[2].mid()
    O[1].up()
    K[0].dn()
    K[3].mid()
    O[2].up()
    K[1].dn()
    V.mid()
    Q.mid()
    K[2].dn()
    O[1].mid()
    O[2].mid()
    K[3].dn()
    V.dn()
    Q.dn()
    O[1].dn()
    O[2].dn()
    jobs = [*D, *U, *O, Q, *K]
    for x in jobs:
        x.store()
    t_vec = pltpu.make_async_copy(lv.zo, R.t_vec, R.t_sem.at[len(jobs)])
    lv.result(lambda src: pltpu.make_async_copy(src, R.t_vec, R.t_sem.at[len(jobs)]).start())
    for x in (*jobs, *DKV, V):
        x.drain()
    t_vec.wait()
    staged(R.grad_queries, R.gq_sem, rows - 1, positions)
    for c in put_gl:
        c.wait()


def unpack(*refs):
    n = len(Outs._fields)
    ins, out = refs[:9], Outs(*refs[9 : 9 + n])
    stay, wide, narrow = refs[9 + n : 18 + n], refs[18 + n : -3], refs[-3]
    sem_in, sem_out = refs[-2], refs[-1]
    loads = [pltpu.make_async_copy(a, b, sem_in.at[k]) for k, (a, b) in enumerate(zip(ins, stay))]
    for c in loads:
        c.start()
    t_vec = stay[8]
    outs = (
        out.block_out,
        out.grad_queries,
        out.grad_latents,
        out.grad_down_weight,
        out.grad_up_weight,
        out.grad_out_weight,
        out.grad_query_weight,
        out.grad_key_weight,
        out.grad_value_weight,
    )
    stores = [pltpu.make_async_copy(stay[0], out.block_out, sem_out.at[0])]
    stores += [pltpu.make_async_copy(v, outs[k + 1], sem_out.at[k + 1]) for k, v in enumerate(wide)]
    loads[1].wait()
    half = wide[0].shape[0] // 2
    halves = []
    for j in range(2):
        rs = pl.ds(j * half, half)
        wide[0][rs] = stay[1][rs].astype(f32)
        halves.append(pltpu.make_async_copy(wide[0].at[rs], out.grad_queries.at[rs], narrow.at[j]))
        halves[-1].start()
    stores = stores[:1] + stores[2:]
    loads[0].wait()
    stores[0].start()
    for k in range(1, 6):
        loads[k + 1].wait()
        wide[k][...] = stay[k + 1][...].astype(f32)
        stores[k].start()
    loads[7].wait()
    wide[6][...] = stay[7][0].astype(f32)
    stores[6].start()
    for k in range(3):
        wide[7][:, 256 * k : 256 * (k + 1)] = stay[7][k + 1].astype(f32)
    stores[7].start()
    loads[8].wait()
    vectors = (
        out.grad_gain_query,
        out.grad_shift_query,
        out.grad_gain_hidden,
        out.grad_shift_hidden,
        out.grad_bias_up,
        out.grad_bias_down,
        out.grad_gain_latent,
        out.grad_shift_latent,
    )
    for t in range(8):

        @pl.when(lax.axis_index("seq") == t)
        def _():
            for k, ref in enumerate(vectors):
                m = ref.shape[0]
                ref[...] = t_vec[k, m * t : m * (t + 1)]

    for c in stores + halves:
        c.wait()


class Args(NamedTuple):
    queries: Any
    latents: Any
    query_ids: Any
    latent_ids: Any
    query_weight: Any
    key_weight: Any
    value_weight: Any
    out_weight: Any
    up_weight: Any
    down_weight: Any
    gain_query: Any
    shift_query: Any
    gain_latent: Any
    shift_latent: Any
    gain_hidden: Any
    shift_hidden: Any
    bias_up: Any
    bias_down: Any
    cotangent: Any


class Outs(NamedTuple):
    block_out: Any
    grad_queries: Any
    grad_latents: Any
    grad_query_weight: Any
    grad_key_weight: Any
    grad_value_weight: Any
    grad_out_weight: Any
    grad_up_weight: Any
    grad_down_weight: Any
    grad_gain_query: Any
    grad_shift_query: Any
    grad_gain_latent: Any
    grad_shift_latent: Any
    grad_gain_hidden: Any
    grad_shift_hidden: Any
    grad_bias_up: Any
    grad_bias_down: Any


def body(n_rows, n_seq, *args):
    A = Args(*args)
    rows, pos, width = A.queries.shape
    lats, lwidth = A.latents.shape[1:]
    nl = lats * n_seq
    F_ = lambda *s: jax.ShapeDtypeStruct(s, f32)
    wide, vec, lvec = F_(width // n_seq, width), F_(width // n_seq), F_(lwidth // n_seq)
    out = Outs(
        block_out=jax.ShapeDtypeStruct((rows, pos, width), bf16),
        grad_queries=F_(rows, pos, width),
        grad_latents=F_(rows, lats, lwidth),
        grad_query_weight=F_(width // n_seq, 256),
        grad_key_weight=F_(lwidth // n_seq, 256),
        grad_value_weight=F_(lwidth // n_seq, width),
        grad_out_weight=wide,
        grad_up_weight=wide,
        grad_down_weight=wide,
        grad_gain_query=vec,
        grad_shift_query=vec,
        grad_gain_latent=lvec,
        grad_shift_latent=lvec,
        grad_gain_hidden=vec,
        grad_shift_hidden=vec,
        grad_bias_up=vec,
        grad_bias_down=vec,
    )
    V = lambda *s: pltpu.VMEM(s, bf16)
    F = lambda *s: pltpu.VMEM(s, f32)
    dma = lambda *s: pltpu.SemaphoreType.DMA(s)
    tok = V(rows, pos, width)
    tok2 = V(rows * pos, width)
    tokT = V(width, rows * pos)
    scratch = dict(
        q_v=tok,
        c_v=tok,
        lat_v=V(rows, lats, lwidth),
        wq_v=V(width, 256),
        wk_v=V(lwidth, 256),
        wv_v=V(lwidth, width),
        wo_v=V(width, width),
        wu_v=V(width, width),
        wd_v=V(width, width),
        kv=V(rows, nl, 1024),
        qn=tok2,
        qp=V(rows * pos, 256),
        s_scr=F(HEADS, nl, pos),
        ds_scr=V(HEADS * nl, pos),
        inv=F(rows, HEADS, pos),
        p=V(rows * HEADS * nl, pos),
        mix=tokT,
        hn=tok2,
        act=tok2,
        dpre=tok2,
        dres=tok2,
        dm=tokT,
        dq=V(rows * pos, 256),
        lidT=F(nl, 128),
        ln=V(rows * lats, lwidth),
        dkv_own=V(rows * lats, 1024),
        vec=F(8, 8, lwidth),
        vtot=F(4, 8, lwidth),
        vland=F(3, 8, lwidth),
        vs=dma(3),
        vr=dma(3),
        bo_sem=dma(width // 256),
        gq_sem=dma(width // 256),
        gl_sem=dma(lwidth // 256),
        t_sem=dma(15),
        load_sem=dma(9),
        ag_s=dma(rows // 2, 9),
        ag_r=dma(rows // 2, 9),
        g_down=V(width, width),
        g_q=V(width, 256),
        ln_vec=line_scratch((8, lwidth), f32),
    )
    lead, llead = (width // n_seq,), (lwidth // n_seq,)
    shapes = [lead] * 10 + [llead] * 4
    scratch["sc"] = [scatter_scratch(x, 256) for x in shapes]
    scratch["li"] = [line_scratch((*x, 256), bf16) for x in shapes]
    scratch["scd"] = [scatter_scratch((2, lats), 1024) for _ in range(rows // 2)]
    any_ = pl.BlockSpec(memory_space=pl.ANY)
    vm = pl.BlockSpec(memory_space=pltpu.VMEM)
    far = (A.queries, A.cotangent, A.latents, *A[4:10])
    in_specs = [any_ if any(a is f for f in far) else vm for a in A]
    sds = jax.ShapeDtypeStruct
    mid = dict(
        block_out=sds((rows * pos, width), bf16),
        grad_queries=sds((rows * pos, width), bf16),
        grad_latents=sds((rows * lats, lwidth), bf16),
        t_down=sds(wide.shape, bf16),
        t_up=sds(wide.shape, bf16),
        t_out=sds(wide.shape, bf16),
        t_q=sds((width // n_seq, 256), bf16),
        t_kv=sds((4, lwidth // n_seq, 256), bf16),
        t_vec=sds((8, lwidth), f32),
    )
    names = (*Args._fields, *mid, *scratch)
    flops = 2 * rows * pos * width * width * 14
    got = pl.pallas_call(
        functools.partial(kernel, n_rows, names),
        out_shape=tuple(mid.values()),
        in_specs=in_specs,
        out_specs=(any_,) * len(mid),
        scratch_shapes=list(scratch.values()),
        compiler_params=pltpu.CompilerParams(
            collective_id=0, has_side_effects=True, vmem_limit_bytes=64 << 20
        ),
        cost_estimate=pl.CostEstimate(flops=flops, bytes_accessed=24 << 20, transcendentals=0),
    )(*A)
    three = lambda x: x.reshape(rows, -1, x.shape[-1])
    got = (three(got[0]), three(got[1]), three(got[2]), *got[3:])
    return pl.pallas_call(
        unpack,
        out_shape=tuple(out),
        in_specs=[any_] * 9,
        out_specs=(any_,) * 9 + (vm,) * 8,
        scratch_shapes=[pltpu.VMEM(x.shape, x.dtype) for x in got]
        + [
            pltpu.VMEM(o.shape, f32)
            for o in (
                out.grad_queries,
                out.grad_latents,
                wide,
                wide,
                wide,
                out.grad_query_weight,
                out.grad_key_weight,
                out.grad_value_weight,
            )
        ]
        + [dma(2), dma(9), dma(9)],
        compiler_params=pltpu.CompilerParams(vmem_limit_bytes=64 << 20),
        cost_estimate=pl.CostEstimate(flops=0, bytes_accessed=18 << 20, transcendentals=0),
    )(*got)


def solution(mesh):
    seq = P("rows", "seq", None)
    rep = P()
    in_specs = (seq, seq, P("rows", "seq"), P("rows", None)) + (rep,) * 14 + (seq,)
    out_specs = (seq,) * 3 + (P("seq", None),) * 6 + (P("seq"),) * 8
    return jax.shard_map(
        functools.partial(body, mesh.shape["rows"], mesh.shape["seq"]),
        mesh=mesh,
        in_specs=in_specs,
        out_specs=out_specs,
        check_vma=False,
    )
```
